512 devices in a mesh: cells: 32 (over y, z_hi), bands: 16 (over x, z_lo, core).
Axes of the slice: x: 4, y: 8, z: 8 (z_hi: 4, z_lo: 2; z = z_hi * 2 + z_lo), core: 2. Of those that a mesh axis runs over, the one named last changes fastest.
Arguments:
- cur_block: bfloat16 [32, 1048576], P(None, ('cells', 'bands')), may hold values from -6 to 6
- stored_blocks: bfloat16 [64, 1048576], P('bands', 'cells'), may hold values from -6 to 6
- cell_potential: float32 [125, 16384], P(None, ('cells', 'bands')), may hold values from 0.1 to 2
- connectivity: int32 [125, 16384], P(None, ('cells', 'bands')), may hold values from 0 to 2311, as said below
Outputs:
- filtered_block: bfloat16 [32, 1048576], P(None, ('cells', 'bands'))
- correlation: float32 [64, 32], P('bands', 'cells')
The draws below stay inside these ranges and needn't reach their ends.
Inputs may be any that keep to these rules, and one draw needn't show every extreme that they name: `connectivity`: column e of device d (columns d * 32 to (d + 1) * 32 - 1) lists one of the device's 32 cells, each cell once, in an order drawn from the seed; for the cell at cell position (i, j, l), 0 <= i < 2, 0 <= j < 4, 0 <= l < 4, row k = 25 a + 5 b + c holds (((4 i + a) mod 8) (17) + 4 j + b) (17) + 4 l + c.
All inputs are finite; a program needn't handle non-finite values.
Results may differ from the reference program's by a relative error of at most 0.012.
The reference program's roundings to bfloat16 on the way (of `kinetic` and `block`) count: a program that leaves them out, or rounds other values in their place, can miss the bound.
Values may be sent and summed in bfloat16 or wider, within the bound.
No kernel may reach another device: no remote copies, remote signals or barrier semaphores. Data moves between devices by JAX's collectives and lax.ppermute only.
A program may use at most 64 MiB of HBM per device.

```python
import math
import jax
import jax.numpy as jnp
import numpy as np
from jax import lax

NWF = 32
CELL_NODES = 125
CYE = 4
CZE = 4
DEGREE = 4
STEPS = 2
STORED = 64
NXL = 8
NYL = 16
NZL = 16
CELLS_DEV = 32
NE = 2312
CELLS = 16384
NODES = 1048576
N_CELLS = 32
N_BANDS = 16


def draw_cur_block(key, part):
    nodes = jnp.arange(NODES, dtype=jnp.int32)
    node_z = nodes % NZL
    node_y = nodes // NZL % NYL
    node_x = nodes // (NZL * NYL) % NXL
    parity = (node_x + node_y + node_z) % 2
    pattern = (1 - 2 * parity).astype(jnp.float32)
    amplitude = 0.3 + jnp.abs(jax.random.normal(jax.random.fold_in(key, 13), (NWF, NODES), jnp.float32))
    values = jnp.clip(amplitude, 0.0, 6.0) * pattern[None, :]
    return values.astype(jnp.bfloat16)


def draw_connectivity(key, part):
    device_count = CELLS // CELLS_DEV
    streams = jax.random.split(key, device_count)
    orders = jax.vmap(lambda stream: jax.random.permutation(stream, CELLS_DEV))(streams)
    along_x = orders // (CYE * CZE)
    along_y = orders // CZE % CYE
    along_z = orders % CZE
    in_cell = jnp.arange(125)
    off_a = (in_cell // 25)[:, None, None]
    off_b = (in_cell // 5 % 5)[:, None, None]
    off_c = (in_cell % 5)[:, None, None]
    index_x = (4 * along_x[None] + off_a) % NXL
    index_y = 4 * along_y[None] + off_b
    index_z = 4 * along_z[None] + off_c
    linked = (index_x * (NYL + 1) + index_y) * (NZL + 1) + index_z
    return linked.reshape(125, CELLS).astype(jnp.int32)


def levels(own_key, shape, cuts, least, top_value):
    loudness, own = 1.0, jax.random.fold_in(own_key, 6)
    for position, parts in cuts:
        heights = jnp.exp(jax.random.uniform(jax.random.fold_in(own, position), (parts,), jnp.float32, least / len(cuts), top_value / len(cuts)))
        loudness = loudness * jnp.repeat(heights, shape[position] // parts).reshape([-1 if axis == position else 1 for axis in range(len(shape))])
    return loudness


def gaussian(key, dims, width, most, cuts=(), held_as=jnp.bfloat16):
    gain = levels(key, dims, cuts, -0.22, 0.18) if cuts else 1.0
    values = jax.random.normal(key, dims, jnp.float32) * width * gain
    return jnp.minimum(jnp.maximum(values, -most), most).astype(held_as)


def setup_inputs(seed: int = 0) -> dict:
    keys = jax.random.split(jax.random.key(seed), 5)
    cur_block = draw_cur_block(jax.random.fold_in(keys[4], 71), 0)
    stored_blocks = gaussian(keys[1], (STORED, NODES), 1.0, 6.0, ((0, 16), (1, 32)))
    cell_potential = jnp.clip(jnp.exp(math.log(2.0) - 2.9957323 * jax.random.uniform(keys[2], (CELL_NODES, CELLS), jnp.float32) ** levels(keys[2], (CELL_NODES, CELLS), ((1, 512),), -0.2, 0.2)), 0.1, 2.0)
    connectivity = draw_connectivity(jax.random.fold_in(keys[4], 71), 0)
    return dict(cur_block=cur_block, stored_blocks=stored_blocks, cell_potential=cell_potential, connectivity=connectivity)


def kinetic_table():
    points = [-1.0, -math.sqrt(3.0 / 7.0), 0.0, math.sqrt(3.0 / 7.0), 1.0]
    weights = [0.1, 49.0 / 90.0, 32.0 / 45.0, 49.0 / 90.0, 0.1]
    scales = []
    for row in range(5):
        prod_val = 1.0
        for other in range(5):
            if other != row:
                prod_val = prod_val * (points[row] - points[other])
        scales.append(prod_val)
    deriv = [[0.0] * 5 for row in range(5)]
    for row in range(5):
        for col in range(5):
            if row != col:
                deriv[row][col] = scales[row] / scales[col] / (points[row] - points[col])
            else:
                total = 0.0
                for other in range(5):
                    if other != row:
                        total = total + 1.0 / (points[row] - points[other])
                deriv[row][col] = total
    stiff_one = [[sum((deriv[i][a] * weights[i] * deriv[i][b] for i in range(5))) for b in range(5)] for a in range(5)]
    mass_one = [[weights[a] if a == b else 0.0 for b in range(5)] for a in range(5)]
    table = [[0.0] * 125 for row in range(125)]
    for k in range(125):
        ka, kb, kc = (k // 25, k // 5 % 5, k % 5)
        for j in range(125):
            ja, jb, jc = (j // 25, j // 5 % 5, j % 5)
            table[k][j] = 0.5 * (stiff_one[ka][ja] * mass_one[kb][jb] * mass_one[kc][jc] + mass_one[ka][ja] * stiff_one[kb][jb] * mass_one[kc][jc] + mass_one[ka][ja] * mass_one[kb][jb] * stiff_one[kc][jc])
    assembled = [dict() for row in range(512)]
    for cell_x in range(2):
        for cell_y in range(2):
            for cell_z in range(2):
                global_ids = []
                for k in range(125):
                    node_x = (4 * cell_x + k // 25) % 8
                    node_y = (4 * cell_y + k // 5 % 5) % 8
                    node_z = (4 * cell_z + k % 5) % 8
                    global_ids.append((node_x * 8 + node_y) * 8 + node_z)
                for k in range(125):
                    row_map = assembled[global_ids[k]]
                    for j in range(125):
                        target = global_ids[j]
                        row_map[target] = row_map.get(target, 0.0) + table[k][j]
    largest = 0.0
    for row_map in assembled:
        total = sum((abs(value) for value in row_map.values()))
        largest = max(largest, total)
    bound = largest + 8.0 * 2.0
    return (np.array(table), float(0.55 * bound), float(0.45 * bound))

def reference(cur_block, stored_blocks, cell_potential, connectivity):
    table, centre, half = kinetic_table()
    kinetic = jnp.asarray(table, jnp.float32).astype(jnp.bfloat16).astype(jnp.float32)
    links = connectivity.reshape(125, N_CELLS, N_BANDS, CELLS_DEV).transpose(1, 2, 0, 3)
    potential = cell_potential.reshape(125, N_CELLS, N_BANDS, CELLS_DEV).transpose(1, 2, 0, 3)

    def per_device(ext_one, index_one, pot_one):
        flat_idx = index_one.reshape(-1)
        cell_vals = jnp.take(ext_one, flat_idx, axis=1).reshape(NWF, 125, CELLS_DEV).astype(jnp.float32)
        product = jnp.einsum('kj,wjc->wkc', kinetic, cell_vals, precision=lax.Precision.HIGHEST)
        product = product + pot_one[None] * cell_vals
        return jnp.zeros((NWF, NE), jnp.float32).at[:, flat_idx].add(product.reshape(NWF, -1))

    def per_partition(packed):
        ext_part, index_part, pot_part = packed
        return jax.vmap(per_device)(ext_part, index_part, pot_part)

    def apply_op(values):
        upper_z = jnp.roll(values[..., 0], -1, axis=1)
        extended = jnp.concatenate([values, upper_z[..., None]], axis=-1)
        upper_y = jnp.roll(extended[..., 0, :], -1, axis=2)
        extended = jnp.concatenate([extended, upper_y[..., None, :]], axis=-2)
        extended = extended.reshape(NWF, N_CELLS, N_BANDS, NE).transpose(1, 2, 0, 3)
        summed = lax.map(per_partition, (extended, links, potential))
        summed = summed.reshape(N_CELLS, N_BANDS, NWF, NXL, NYL + 1, NZL + 1)
        back_y = jnp.roll(summed[..., NYL, :], 1, axis=1)
        summed = summed[..., :NYL, :].at[..., 0, :].add(back_y)
        back_z = jnp.roll(summed[..., NZL], 1, axis=0)
        summed = summed[..., :NZL].at[..., 0].add(back_z)
        return summed.transpose(2, 0, 1, 3, 4, 5)
    block = cur_block.reshape(NWF, N_CELLS, N_BANDS, NXL, NYL, NZL)
    for pass_idx in range(STEPS):
        previous = block
        applied = apply_op(previous)
        current = ((applied - centre * previous.astype(jnp.float32)) / half).astype(jnp.bfloat16)
        for order_idx in range(1, DEGREE):
            applied = apply_op(current)
            following = 2.0 * ((applied - centre * current.astype(jnp.float32)) / half) - previous.astype(jnp.float32)
            previous, current = (current, following.astype(jnp.bfloat16))
        block = current
    filtered_block = block.reshape(NWF, NODES)
    factor = 1.0 / math.sqrt(NODES)
    correlation = jnp.dot(stored_blocks, filtered_block.T, preferred_element_type=jnp.float32) * factor
    return (filtered_block, correlation)
```

```python
import functools
import math

import jax
import jax.numpy as jnp
import ml_dtypes
import numpy as np
from jax import lax
from jax.experimental import pallas as pl
from jax.experimental.pallas import tpu as pltpu
from jax.sharding import PartitionSpec as P

NWF = 32
DEGREE = 4
STEPS = 2
NXL = 8
NODES_DEV = 2048
PLANE = 256
GHOST = 128
V_AT = NODES_DEV
G_AT = 2 * NODES_DEV
S_AT = G_AT + NXL * GHOST
PAYLOAD = S_AT + 2 * NODES_DEV
LANES_V = PLANE + GHOST
X_ORDER = (0, 4, 1, 3, 5, 7, 2, 6)
CLASS_ROWS = ((0, 2), (2, 6), (6, 8))
VMEM = 48 * 1024 * 1024


def kinetic_table():
    points = [-1.0, -math.sqrt(3.0 / 7.0), 0.0, math.sqrt(3.0 / 7.0), 1.0]
    weights = [0.1, 49.0 / 90.0, 32.0 / 45.0, 49.0 / 90.0, 0.1]
    scales = []
    for row in range(5):
        prod_val = 1.0
        for other in range(5):
            if other != row:
                prod_val = prod_val * (points[row] - points[other])
        scales.append(prod_val)
    deriv = [[0.0] * 5 for row in range(5)]
    for row in range(5):
        for col in range(5):
            if row != col:
                deriv[row][col] = scales[row] / scales[col] / (points[row] - points[col])
            else:
                total = 0.0
                for other in range(5):
                    if other != row:
                        total = total + 1.0 / (points[row] - points[other])
                deriv[row][col] = total
    stiff_one = [
        [sum((deriv[i][a] * weights[i] * deriv[i][b] for i in range(5))) for b in range(5)]
        for a in range(5)
    ]
    mass_one = [[weights[a] if a == b else 0.0 for b in range(5)] for a in range(5)]
    table = [[0.0] * 125 for row in range(125)]
    for k in range(125):
        ka, kb, kc = (k // 25, k // 5 % 5, k % 5)
        for j in range(125):
            ja, jb, jc = (j // 25, j // 5 % 5, j % 5)
            table[k][j] = 0.5 * (
                stiff_one[ka][ja] * mass_one[kb][jb] * mass_one[kc][jc]
                + mass_one[ka][ja] * stiff_one[kb][jb] * mass_one[kc][jc]
                + mass_one[ka][ja] * mass_one[kb][jb] * stiff_one[kc][jc]
            )
    assembled = [dict() for row in range(512)]
    for cell_x in range(2):
        for cell_y in range(2):
            for cell_z in range(2):
                global_ids = []
                for k in range(125):
                    node_x = (4 * cell_x + k // 25) % 8
                    node_y = (4 * cell_y + k // 5 % 5) % 8
                    node_z = (4 * cell_z + k % 5) % 8
                    global_ids.append((node_x * 8 + node_y) * 8 + node_z)
                for k in range(125):
                    row_map = assembled[global_ids[k]]
                    for j in range(125):
                        target = global_ids[j]
                        row_map[target] = row_map.get(target, 0.0) + table[k][j]
    largest = 0.0
    for row_map in assembled:
        total = sum((abs(value) for value in row_map.values()))
        largest = max(largest, total)
    bound = largest + 8.0 * 2.0
    return (np.array(table), float(0.55 * bound), float(0.45 * bound))


@functools.lru_cache(maxsize=None)
def tables():
    table, centre, half = kinetic_table()
    kin = table.astype(np.float32).astype(ml_dtypes.bfloat16).astype(np.float64)
    kin = kin.reshape(5, 5, 5, 5, 5, 5)
    planes = np.zeros((3, 3, PLANE, PLANE))
    lines = np.zeros((5, 5, PLANE))
    for j in range(-1, 5):
        for l in range(-1, 5):
            for b in range(5):
                for c in range(5):
                    y, z = 4 * j + b, 4 * l + c
                    if not (0 <= y < 16 and 0 <= z < 16):
                        continue
                    at = 16 * y + z
                    for a in range(5):
                        for other in range(5):
                            if other != a:
                                lines[a, other, at] += kin[a, b, c, other, b, c]
                    for b2 in range(5):
                        for c2 in range(5):
                            y2, z2 = 4 * j + b2, 4 * l + c2
                            far_y, far_z = y2 // 16, z2 // 16
                            source = 16 * (y2 % 16) + z2 % 16
                            for kind, locals_a in enumerate(((0, 4), (1,), (2,))):
                                value = sum(kin[a, b, c, a, b2, c2] for a in locals_a)
                                if value == 0.0:
                                    continue
                                assert far_y == 0 or far_z == 0
                                part = 1 if far_y else 2 if far_z else 0
                                planes[kind, part, source, at] += value
    line_rows = np.stack(
        [lines[0, 1], lines[0, 2], lines[0, 3], 2.0 * lines[0, 4], lines[1, 2], lines[1, 3]]
    )
    codes = np.full((LANES_V, 8), -7, np.int32)
    mask = np.zeros((128, LANES_V), np.float32)
    kinds = np.zeros((128, 8), np.float32)
    to_x = np.zeros((2, 8, 128), np.float32)
    spread = np.zeros((3, GHOST, PLANE), np.float32)
    for lane in range(LANES_V):
        ghost = lane - PLANE
        if ghost < 0:
            y, z = lane // 16, lane % 16
        elif ghost < 16:
            y, z = 16, ghost
            spread[0, ghost, z] = 1.0
        elif ghost < 32:
            y, z = ghost - 16, 16
            spread[1, ghost, 16 * y] = 1.0
        elif ghost == 32:
            y, z = 16, 16
            spread[2, ghost, 0] = 1.0
        else:
            continue
        for i in range(2):
            for kind in range(4):
                j, l = y // 4 - kind // 2, z // 4 - kind % 2
                if 0 <= j < 4 and 0 <= l < 4:
                    codes[lane, 4 * i + kind] = (4 * i * 17 + 4 * j) * 17 + 4 * l
        for k in range(125):
            b, c = k // 5 % 5, k % 5
            mask[k, lane] = float(y % 4 == b % 4 and z % 4 == c % 4)
    for k in range(125):
        a, b, c = k // 25, k // 5 % 5, k % 5
        kinds[k, 2 * (b == 4) + (c == 4)] = 1.0
        for i in range(2):
            to_x[i, (4 * i + a) % 8, k] = 1.0
    pairs = np.zeros((32, 4, 32), np.float32)
    for row in range(32):
        for other in range(32):
            if row // 2 == other // 2:
                pairs[row, 0::2, other] = 1.0
            if (row // 2 - 1) % 16 == other // 2:
                pairs[row, 1::2, other] = 1.0
    bf = ml_dtypes.bfloat16
    weights = planes.reshape(3, 3 * PLANE, PLANE)
    return dict(
        centre=centre,
        half=half,
        weights=weights.astype(np.float32).astype(bf),
        lines=line_rows.astype(np.float32),
        codes=codes,
        mask=mask,
        kinds=kinds,
        to_x=to_x,
        spread=spread.astype(bf),
        pairs=pairs.reshape(32, 128).astype(bf),
    )


def pack_kernel(v_ref, st_ref, pot_ref, conn_ref, codes_ref, mask_ref, kinds_ref, to_x_ref, out_ref, pot, conn):
    out_ref[:, :V_AT] = v_ref[...]
    out_ref[:, S_AT:] = st_ref[...]
    pot[...] = jnp.zeros_like(pot)
    pot[:125, :32] = pot_ref[...]
    conn[...] = jnp.full_like(conn, -1)
    conn[0:1, :32] = conn_ref[0:1, :]
    first = conn[0:1, :]
    exact = lax.Precision.HIGHEST
    total = jnp.zeros((8, LANES_V), jnp.float32)
    for i in range(2):
        spread = jnp.zeros((128, LANES_V), jnp.float32)
        for kind in range(4):
            column = 4 * i + kind
            placed = jnp.where(codes_ref[:, column : column + 1] == first, 1.0, 0.0)
            spread += lax.dot_general(
                pot[...] * kinds_ref[:, kind : kind + 1],
                placed,
                (((1,), (1,)), ((), ())),
                precision=exact,
                preferred_element_type=jnp.float32,
            )
        total += jnp.dot(
            to_x_ref[i], spread * mask_ref[...], precision=exact, preferred_element_type=jnp.float32
        )
    high = total.astype(jnp.bfloat16).astype(jnp.float32)
    low = total - high
    even = lax.broadcasted_iota(jnp.int32, (32, PLANE), 0) % 2 == 0
    for x in range(NXL):
        main = jnp.where(even, high[x : x + 1, :PLANE], low[x : x + 1, :PLANE])
        out_ref[:, V_AT + PLANE * x : V_AT + PLANE * (x + 1)] = main.astype(jnp.bfloat16)
        ghost = jnp.where(even[:, :GHOST], high[x : x + 1, PLANE:], low[x : x + 1, PLANE:])
        out_ref[:, G_AT + GHOST * x : G_AT + GHOST * (x + 1)] = ghost.astype(jnp.bfloat16)


def diagonal(slabs, pairs_ref, spread_ref, g_ref, centre):
    for x in range(NXL):
        ghosts = []
        for slab in slabs:
            raw = slab[:, G_AT + GHOST * x : G_AT + GHOST * (x + 1)]
            ghosts.append(
                [
                    jnp.dot(raw, spread_ref[part], preferred_element_type=jnp.float32).astype(jnp.bfloat16)
                    for part in range(3)
                ]
            )
        for s, slab in enumerate(slabs):
            own = slab[:, V_AT + PLANE * x : V_AT + PLANE * (x + 1)]
            if s == 0:
                stack = jnp.concatenate([own, ghosts[0][0]], axis=0)
                pairs = pairs_ref[:, :64]
            else:
                stack = jnp.concatenate([own, ghosts[s][0], ghosts[s - 1][1], ghosts[s - 1][2]], axis=0)
                pairs = pairs_ref[...]
            g_ref[x, s] = jnp.dot(pairs, stack, preferred_element_type=jnp.float32) - centre


def filter_step(slabs, w_ref, lines_ref, g_ref, out_ref, cur, prev, acc, half):
    place = {x: at for at, x in enumerate(X_ORDER)}
    right_lanes = lax.broadcasted_iota(jnp.int32, (32, PLANE), 1) % 16 < 8
    for s, slab in enumerate(slabs):
        for x in range(NXL):
            block = slab[:, PLANE * x : PLANE * (x + 1)]
            cur[place[x], s, :, :PLANE] = block
            turn(cur, place[x], s, 0, block[:, :128].astype(jnp.float32))
            turn(cur, place[x], s, 1, block[:, 128:].astype(jnp.float32))
    prev[...] = jnp.zeros_like(prev)

    def sides():
        for at in range(NXL):
            left, middle, right = (cur[at, s, :, :PLANE].astype(jnp.float32) for s in range(3))
            zero = jnp.zeros_like(left)
            cur[at, 0, :, 2 * PLANE :] = jnp.where(right_lanes, middle, zero).astype(jnp.bfloat16)
            cur[at, 1, :, 2 * PLANE :] = jnp.where(right_lanes, right, left).astype(jnp.bfloat16)
            cur[at, 2, :, 2 * PLANE :] = jnp.where(right_lanes, zero, middle).astype(jnp.bfloat16)

    def apply(which, alpha, beta, store):
        first, last = which[0], which[-1] + 1
        for kind, (low, high) in enumerate(CLASS_ROWS):
            rows = cur[low:high, first:last]
            count = (high - low) * (last - first) * 32
            result = jnp.dot(
                rows.reshape(count, 3 * PLANE), w_ref[kind], preferred_element_type=jnp.float32
            )
            acc[low:high, first:last] = result.reshape(high - low, last - first, 32, PLANE)
        for s in which:
            for part in range(2):
                lanes = slice(128 * part, 128 * (part + 1))
                v = [cur[place[x], s, :, lanes].astype(jnp.float32) for x in range(NXL)]
                c01, c02, c03, c04, c12, c13 = (lines_ref[row : row + 1, lanes] for row in range(6))
                s17, s26, s35 = v[1] + v[7], v[2] + v[6], v[3] + v[5]
                s04 = c02 * (v[0] + v[4])
                extra = {
                    0: c01 * s17 + c02 * s26 + c03 * s35 + c04 * v[4],
                    4: c01 * s35 + c02 * s26 + c03 * s17 + c04 * v[0],
                    1: c01 * v[0] + c12 * v[2] + c13 * v[3] + c03 * v[4],
                    3: c01 * v[4] + c12 * v[2] + c13 * v[1] + c03 * v[0],
                    5: c01 * v[4] + c12 * v[6] + c13 * v[7] + c03 * v[0],
                    7: c01 * v[0] + c12 * v[6] + c13 * v[5] + c03 * v[4],
                    2: s04 + c12 * (v[1] + v[3]),
                    6: s04 + c12 * (v[5] + v[7]),
                }
                for x in range(NXL):
                    at = place[x]
                    applied = acc[at, s, :, lanes] + extra[x] + g_ref[x, s, :, lanes] * v[x]
                    store(x, at, s, part, alpha * applied - beta * prev[at, s, :, lanes].astype(jnp.float32))

    def keep(x, at, s, part, new):
        lanes = slice(128 * part, 128 * (part + 1))
        prev[at, s, :, lanes] = cur[at, s, :, lanes]
        new = new.astype(jnp.bfloat16)
        cur[at, s, :, lanes] = new
        turn(cur, at, s, part, new.astype(jnp.float32))

    def emit(x, at, s, part, new):
        out_ref[:, PLANE * x + 128 * part : PLANE * x + 128 * (part + 1)] = new.astype(jnp.bfloat16)

    def order(k, carry):
        sides()
        alpha = jnp.where(k == 0, jnp.float32(1.0 / half), jnp.float32(2.0 / half))
        beta = jnp.where(k == 0, jnp.float32(0.0), jnp.float32(1.0))
        apply((0, 1, 2), alpha, beta, keep)
        return carry

    lax.fori_loop(0, DEGREE - 1, order, 0)
    sides()
    apply((1,), jnp.float32(2.0 / half), jnp.float32(1.0), emit)


def turn(cur, at, s, part, value):
    shift = 30 if part == 0 else 2
    lanes = slice(PLANE + 128 * part, PLANE + 128 * (part + 1))
    cur[at, s, :, lanes] = pltpu.roll(value, shift, 0).astype(jnp.bfloat16)


def first_kernel(centre, half, c_ref, l_ref, r_ref, w_ref, lines_ref, pairs_ref, spread_ref, out_ref, g_ref, cur, prev, acc):
    slabs = (l_ref, c_ref, r_ref)
    diagonal(slabs, pairs_ref, spread_ref, g_ref, centre)
    filter_step(slabs, w_ref, lines_ref, g_ref, out_ref, cur, prev, acc, half)


def later_kernel(half, c_ref, l_ref, r_ref, w_ref, lines_ref, g_ref, out_ref, cur, prev, acc):
    filter_step((l_ref, c_ref, r_ref), w_ref, lines_ref, g_ref, out_ref, cur, prev, acc, half)


def corr_kernel(factor, st_ref, f_ref, out_ref):
    for part in range(2):
        out_ref[part] = factor * lax.dot_general(
            st_ref[:, NODES_DEV * part : NODES_DEV * (part + 1)],
            f_ref[...],
            (((1,), (1,)), ((), ())),
            preferred_element_type=jnp.float32,
        )


def full(shape):
    return pl.BlockSpec(shape, lambda *_: (0,) * len(shape))


def call(kernel, args, specs, outs, scratch=()):
    return pl.pallas_call(
        kernel,
        grid=(1,),
        in_specs=specs,
        out_specs=[full(o.shape) for o in outs],
        out_shape=list(outs),
        scratch_shapes=list(scratch),
        compiler_params=pltpu.CompilerParams(vmem_limit_bytes=VMEM),
    )(*args)


def passed_along(block, axis, distance):
    devices = range(lax.axis_size(axis))
    route = [((i - distance) % len(devices), i) for i in devices]
    return lax.ppermute(block, axis, route)


def shards(cur_block, stored_blocks, cell_potential, connectivity):
    t = tables()
    bf, f32 = jnp.bfloat16, jnp.float32
    n_cells, n_bands = lax.axis_size("cells"), lax.axis_size("bands")
    const = {k: jnp.asarray(v) for k, v in t.items() if isinstance(v, np.ndarray)}
    stored = stored_blocks.reshape(2, 2, n_bands, NODES_DEV).transpose(2, 1, 0, 3).reshape(NWF, 2 * NODES_DEV)
    pack_args = (cur_block, stored, cell_potential, connectivity) + tuple(
        const[k] for k in ("codes", "mask", "kinds", "to_x")
    )
    (payload,) = call(
        pack_kernel,
        pack_args,
        [full(a.shape) for a in pack_args],
        [jax.ShapeDtypeStruct((NWF, PAYLOAD), bf)],
        [pltpu.VMEM((128, 128), f32), pltpu.VMEM((8, 128), jnp.int32)],
    )
    got = lax.all_to_all(payload, "bands", 0, 0, tiled=True)
    near = got[:, :S_AT]
    left = passed_along(near, "cells", 1)
    right = passed_along(near, "cells", -1)
    scratch = [
        pltpu.VMEM((NXL, 3, NWF, 3 * PLANE), bf),
        pltpu.VMEM((NXL, 3, NWF, PLANE), bf),
        pltpu.VMEM((NXL, 3, NWF, PLANE), f32),
    ]
    args = (near, left, right) + tuple(const[k] for k in ("weights", "lines", "pairs", "spread"))
    block, diag = call(
        functools.partial(first_kernel, t["centre"], t["half"]),
        args,
        [full(a.shape) for a in args],
        [
            jax.ShapeDtypeStruct((NWF, NODES_DEV), bf),
            jax.ShapeDtypeStruct((NXL, 3, NWF, PLANE), f32),
        ],
        scratch,
    )
    for step in range(1, STEPS):
        left = passed_along(block, "cells", 1)
        right = passed_along(block, "cells", -1)
        args = (block, left, right, const["weights"], const["lines"], diag)
        (block,) = call(
            functools.partial(later_kernel, t["half"]),
            args,
            [full(a.shape) for a in args],
            [jax.ShapeDtypeStruct((NWF, NODES_DEV), bf)],
            scratch,
        )
    filtered = lax.all_to_all(block, "bands", 0, 0, tiled=True)
    factor = 1.0 / math.sqrt(NODES_DEV * n_cells * n_bands)
    args = (got[:, S_AT:], filtered)
    (partial,) = call(
        functools.partial(corr_kernel, factor),
        args,
        [full(a.shape) for a in args],
        [jax.ShapeDtypeStruct((2, NWF, NWF), f32)],
    )
    partial = partial.reshape(2, n_bands, 2, NWF).transpose(1, 3, 0, 2).reshape(n_bands, NWF, 4)
    partial = lax.all_to_all(partial, "bands", 0, 0, tiled=True).sum(axis=0)
    per_cell = NWF // n_cells
    partial = partial.reshape(n_cells, per_cell, 4)
    total = lax.all_to_all(partial, "cells", 0, 0, tiled=True).sum(axis=0)
    return (filtered, total.T)


def solution(mesh):
    in_specs = (
        P(None, ("cells", "bands")),
        P("bands", "cells"),
        P(None, ("cells", "bands")),
        P(None, ("cells", "bands")),
    )
    out_specs = (P(None, ("cells", "bands")), P("bands", "cells"))
    return jax.shard_map(shards, mesh=mesh, in_specs=in_specs, out_specs=out_specs, check_vma=False)
```

```python
import functools
import math

import jax
import jax.numpy as jnp
import ml_dtypes
import numpy as np
from jax import lax
from jax.experimental import pallas as pl
from jax.experimental.pallas import tpu as pltpu
from jax.sharding import PartitionSpec as P

NWF = 32
DEGREE = 4
STEPS = 2
NXL = 8
NODES_DEV = 2048
PLANE = 256
LANES_V = 384
MESSAGE = NODES_DEV + 256
V_AT = 3 * NODES_DEV
G_AT = 6 * NODES_DEV
PAYLOAD = G_AT + 3 * 128
X_ORDER = (0, 4, 1, 3, 5, 7, 2, 6)
CLASS_ROWS = ((0, 2), (2, 6), (6, 8))
VMEM = 48 * 1024 * 1024


def kinetic_table():
    points = [-1.0, -math.sqrt(3.0 / 7.0), 0.0, math.sqrt(3.0 / 7.0), 1.0]
    weights = [0.1, 49.0 / 90.0, 32.0 / 45.0, 49.0 / 90.0, 0.1]
    scales = []
    for row in range(5):
        prod_val = 1.0
        for other in range(5):
            if other != row:
                prod_val = prod_val * (points[row] - points[other])
        scales.append(prod_val)
    deriv = [[0.0] * 5 for row in range(5)]
    for row in range(5):
        for col in range(5):
            if row != col:
                deriv[row][col] = scales[row] / scales[col] / (points[row] - points[col])
            else:
                total = 0.0
                for other in range(5):
                    if other != row:
                        total = total + 1.0 / (points[row] - points[other])
                deriv[row][col] = total
    stiff_one = [
        [sum((deriv[i][a] * weights[i] * deriv[i][b] for i in range(5))) for b in range(5)]
        for a in range(5)
    ]
    mass_one = [[weights[a] if a == b else 0.0 for b in range(5)] for a in range(5)]
    table = [[0.0] * 125 for row in range(125)]
    for k in range(125):
        ka, kb, kc = (k // 25, k // 5 % 5, k % 5)
        for j in range(125):
            ja, jb, jc = (j // 25, j // 5 % 5, j % 5)
            table[k][j] = 0.5 * (
                stiff_one[ka][ja] * mass_one[kb][jb] * mass_one[kc][jc]
                + mass_one[ka][ja] * stiff_one[kb][jb] * mass_one[kc][jc]
                + mass_one[ka][ja] * mass_one[kb][jb] * stiff_one[kc][jc]
            )
    assembled = [dict() for row in range(512)]
    for cell_x in range(2):
        for cell_y in range(2):
            for cell_z in range(2):
                global_ids = []
                for k in range(125):
                    node_x = (4 * cell_x + k // 25) % 8
                    node_y = (4 * cell_y + k // 5 % 5) % 8
                    node_z = (4 * cell_z + k % 5) % 8
                    global_ids.append((node_x * 8 + node_y) * 8 + node_z)
                for k in range(125):
                    row_map = assembled[global_ids[k]]
                    for j in range(125):
                        target = global_ids[j]
                        row_map[target] = row_map.get(target, 0.0) + table[k][j]
    largest = 0.0
    for row_map in assembled:
        total = sum((abs(value) for value in row_map.values()))
        largest = max(largest, total)
    bound = largest + 8.0 * 2.0
    return (np.array(table), float(0.55 * bound), float(0.45 * bound))


@functools.lru_cache(maxsize=None)
def tables():
    table, centre, half = kinetic_table()
    kin = table.astype(np.float32).astype(ml_dtypes.bfloat16).astype(np.float64)
    kin = kin.reshape(5, 5, 5, 5, 5, 5)
    planes = np.zeros((3, 3, PLANE, PLANE))
    lines = np.zeros((5, 5, PLANE))
    for j in range(-1, 5):
        for l in range(-1, 5):
            for b in range(5):
                for c in range(5):
                    y, z = 4 * j + b, 4 * l + c
                    if not (0 <= y < 16 and 0 <= z < 16):
                        continue
                    at = 16 * y + z
                    for a in range(5):
                        for other in range(5):
                            if other != a:
                                lines[a, other, at] += kin[a, b, c, other, b, c]
                    for b2 in range(5):
                        for c2 in range(5):
                            y2, z2 = 4 * j + b2, 4 * l + c2
                            far_y, far_z = y2 // 16, z2 // 16
                            source = 16 * (y2 % 16) + z2 % 16
                            for kind, locals_a in enumerate(((0, 4), (1,), (2,))):
                                value = sum(kin[a, b, c, a, b2, c2] for a in locals_a)
                                if value == 0.0:
                                    continue
                                assert far_y == 0 or far_z == 0
                                part = 1 if far_y else 2 if far_z else 0
                                planes[kind, part, source, at] += value
    line_rows = np.stack(
        [lines[0, 1], lines[0, 2], lines[0, 3], 2.0 * lines[0, 4], lines[1, 2], lines[1, 3]]
    )
    cell_codes = np.full((1, 128), -1, np.int32)
    for cell in range(32):
        i, j, l = cell // 16, cell // 4 % 4, cell % 4
        cell_codes[0, cell] = (4 * i * 17 + 4 * j) * 17 + 4 * l
    places = np.full((2, 6, LANES_V), -1.0, np.float32)
    mask = np.zeros((128, LANES_V), np.float32)
    kinds = np.zeros((6, 128), np.float32)
    to_x = np.zeros((2, 8, 128), np.float32)
    spread = np.zeros((128, NXL, 128), np.float32)
    for lane in range(PLANE + 16):
        y, z = (lane // 16, lane % 16) if lane < PLANE else (16, lane - PLANE)
        for i in range(2):
            for kind in range(4):
                j, l = y // 4 - kind // 2, z // 4 - kind % 2
                if 0 <= j < 4 and 0 <= l < 4:
                    places[i, kind, lane] = 16 * i + 4 * j + l
            for kind in range(2):
                j = y // 4 - kind
                if 0 <= j < 4 and z == 0:
                    places[i, 4 + kind, lane] = 16 * i + 4 * j + 3
        for k in range(125):
            b, c = k // 5 % 5, k % 5
            mask[k, lane] = float(y % 4 == b % 4 and z % 4 == c % 4)
    for k in range(125):
        a, b, c = k // 25, k // 5 % 5, k % 5
        kinds[2 * (b == 4) + (c == 4), k] = 1.0
        if c == 4:
            kinds[4 + (b == 4), k] = 1.0
        for i in range(2):
            to_x[i, (4 * i + a) % 8, k] = 1.0
    for x in range(NXL):
        for z in range(16):
            spread[16 * x + z, x, z] = 1.0
    pairs = np.zeros((32, 2, 32), np.float32)
    for row in range(32):
        for other in range(32):
            if row // 2 == other // 2:
                pairs[row, 0, other] = 1.0
            if (row // 2 - 1) % 16 == other // 2:
                pairs[row, 1, other] = 1.0
    bf = ml_dtypes.bfloat16
    weights = planes.reshape(3, 3 * PLANE, PLANE)
    return dict(
        centre=centre,
        half=half,
        weights=weights.astype(np.float32).astype(bf),
        lines=line_rows.astype(np.float32),
        cell_codes=cell_codes,
        places=places,
        mask=mask,
        kinds=kinds,
        to_x=to_x.astype(bf),
        spread=spread.reshape(128, NXL * 128).astype(bf),
        pairs=pairs.reshape(32, 64).astype(bf),
    )


def message_kernel(v_ref, pot_ref, conn_ref, codes_ref, out_ref, pot):
    out_ref[:, :NODES_DEV] = v_ref[...]
    pot[...] = jnp.zeros_like(pot)
    pot[:, :125] = pot_ref[...]
    lane = lax.broadcasted_iota(jnp.int32, (32, 128), 1)
    here = jnp.where(conn_ref[:, 0:1] == codes_ref[...], lane.astype(jnp.float32), 0.0)
    cell = jnp.sum(here, axis=1, keepdims=True)
    high = pot[...].astype(jnp.bfloat16).astype(jnp.float32)
    low = pot[...] - high
    out_ref[:, NODES_DEV : NODES_DEV + 128] = jnp.where(lane == 127, cell, high).astype(jnp.bfloat16)
    out_ref[:, NODES_DEV + 128 :] = low.astype(jnp.bfloat16)


def nodal(own, left, places_ref, kinds_ref, mask_ref, to_x_ref):
    sides = [(own, range(4))] + ([(left, range(4, 6))] if left is not None else [])
    rows, ones = [], ([], [])
    for message, kind_range in sides:
        high = message[:, NODES_DEV : NODES_DEV + 128].astype(jnp.float32)
        low = message[:, NODES_DEV + 128 :].astype(jnp.float32)
        cell = high[:, 127:128]
        for kind in kind_range:
            pick = kinds_ref[kind : kind + 1, :]
            rows += [high * pick, low * pick]
            for i in range(2):
                one = jnp.where(cell == places_ref[i, kind : kind + 1, :], 1.0, 0.0)
                ones[i].extend([one, one])
    stack = jnp.concatenate(rows, axis=0).astype(jnp.bfloat16)
    total = jnp.zeros((8, LANES_V), jnp.float32)
    for i in range(2):
        placed = jnp.concatenate(ones[i], axis=0).astype(jnp.bfloat16)
        values = lax.dot_general(
            stack, placed, (((0,), (0,)), ((), ())), preferred_element_type=jnp.float32
        )
        values = values * mask_ref[...]
        high = values.astype(jnp.bfloat16)
        low = (values - high.astype(jnp.float32)).astype(jnp.bfloat16)
        total += jnp.dot(to_x_ref[i], high, preferred_element_type=jnp.float32)
        total += jnp.dot(to_x_ref[i], low, preferred_element_type=jnp.float32)
    return total


def pack_kernel(c_ref, l_ref, r_ref, places_ref, kinds_ref, mask_ref, to_x_ref, out_ref, ghost):
    messages = (l_ref, c_ref, r_ref)
    even = lax.broadcasted_iota(jnp.int32, (32, PLANE), 0) % 2 == 0
    for s, message in enumerate(messages):
        out_ref[:, NODES_DEV * s : NODES_DEV * (s + 1)] = message[:, :NODES_DEV]
        left = messages[s - 1] if s else None
        total = nodal(message, left, places_ref, kinds_ref, mask_ref, to_x_ref)
        high = total.astype(jnp.bfloat16).astype(jnp.float32)
        low = total - high
        for x in range(NXL):
            main = jnp.where(even, high[x : x + 1, :PLANE], low[x : x + 1, :PLANE])
            at = V_AT + NODES_DEV * s + PLANE * x
            out_ref[:, at : at + PLANE] = main.astype(jnp.bfloat16)
            edge = jnp.where(even[:, :128], high[x : x + 1, PLANE:], low[x : x + 1, PLANE:])
            ghost[:, 16 * x : 16 * (x + 1)] = edge[:, :16]
        at = G_AT + 128 * s
        out_ref[:, at : at + 128] = ghost[...].astype(jnp.bfloat16)


def diagonal(got, pairs_ref, spread_ref, g_ref, centre):
    for s in range(3):
        at = G_AT + 128 * s
        edge = jnp.dot(got[:, at : at + 128], spread_ref[...], preferred_element_type=jnp.float32)
        edge = edge.astype(jnp.bfloat16)
        for x in range(NXL):
            at = V_AT + NODES_DEV * s + PLANE * x
            stack = jnp.concatenate([got[:, at : at + 128], edge[:, 128 * x : 128 * (x + 1)]], axis=0)
            g_ref[x, s, :, :128] = jnp.dot(pairs_ref[...], stack, preferred_element_type=jnp.float32) - centre
            g_ref[x, s, :, 128:] = (
                jnp.dot(pairs_ref[:, :32], got[:, at + 128 : at + PLANE], preferred_element_type=jnp.float32)
                - centre
            )


def filter_step(slabs, w_ref, lines_ref, g_ref, out_ref, cur, prev, acc, half):
    place = {x: at for at, x in enumerate(X_ORDER)}
    right_lanes = lax.broadcasted_iota(jnp.int32, (32, PLANE), 1) % 16 < 8
    for s, slab in enumerate(slabs):
        for x in range(NXL):
            block = slab[:, PLANE * x : PLANE * (x + 1)]
            cur[place[x], s, :, :PLANE] = block
            turn(cur, place[x], s, 0, block[:, :128].astype(jnp.float32))
            turn(cur, place[x], s, 1, block[:, 128:].astype(jnp.float32))
    prev[...] = jnp.zeros_like(prev)

    def sides():
        for at in range(NXL):
            left, middle, right = (cur[at, s, :, :PLANE].astype(jnp.float32) for s in range(3))
            zero = jnp.zeros_like(left)
            cur[at, 0, :, 2 * PLANE :] = jnp.where(right_lanes, middle, zero).astype(jnp.bfloat16)
            cur[at, 1, :, 2 * PLANE :] = jnp.where(right_lanes, right, left).astype(jnp.bfloat16)
            cur[at, 2, :, 2 * PLANE :] = jnp.where(right_lanes, zero, middle).astype(jnp.bfloat16)

    def apply(which, alpha, beta, store):
        first, last = which[0], which[-1] + 1
        for kind, (low, high) in enumerate(CLASS_ROWS):
            rows = cur[low:high, first:last]
            count = (high - low) * (last - first) * 32
            result = jnp.dot(
                rows.reshape(count, 3 * PLANE), w_ref[kind], preferred_element_type=jnp.float32
            )
            acc[low:high, first:last] = result.reshape(high - low, last - first, 32, PLANE)
        for s in which:
            for part in range(2):
                lanes = slice(128 * part, 128 * (part + 1))
                v = [cur[place[x], s, :, lanes].astype(jnp.float32) for x in range(NXL)]
                c01, c02, c03, c04, c12, c13 = (lines_ref[row : row + 1, lanes] for row in range(6))
                s17, s26, s35 = v[1] + v[7], v[2] + v[6], v[3] + v[5]
                s04 = c02 * (v[0] + v[4])
                extra = {
                    0: c01 * s17 + c02 * s26 + c03 * s35 + c04 * v[4],
                    4: c01 * s35 + c02 * s26 + c03 * s17 + c04 * v[0],
                    1: c01 * v[0] + c12 * v[2] + c13 * v[3] + c03 * v[4],
                    3: c01 * v[4] + c12 * v[2] + c13 * v[1] + c03 * v[0],
                    5: c01 * v[4] + c12 * v[6] + c13 * v[7] + c03 * v[0],
                    7: c01 * v[0] + c12 * v[6] + c13 * v[5] + c03 * v[4],
                    2: s04 + c12 * (v[1] + v[3]),
                    6: s04 + c12 * (v[5] + v[7]),
                }
                for x in range(NXL):
                    at = place[x]
                    applied = acc[at, s, :, lanes] + extra[x] + g_ref[x, s, :, lanes] * v[x]
                    store(x, at, s, part, alpha * applied - beta * prev[at, s, :, lanes].astype(jnp.float32))

    def keep(x, at, s, part, new):
        lanes = slice(128 * part, 128 * (part + 1))
        prev[at, s, :, lanes] = cur[at, s, :, lanes]
        new = new.astype(jnp.bfloat16)
        cur[at, s, :, lanes] = new
        turn(cur, at, s, part, new.astype(jnp.float32))

    def emit(x, at, s, part, new):
        out_ref[:, PLANE * x + 128 * part : PLANE * x + 128 * (part + 1)] = new.astype(jnp.bfloat16)

    def order(k, carry):
        sides()
        alpha = jnp.where(k == 0, jnp.float32(1.0 / half), jnp.float32(2.0 / half))
        beta = jnp.where(k == 0, jnp.float32(0.0), jnp.float32(1.0))
        apply((0, 1, 2), alpha, beta, keep)
        return carry

    lax.fori_loop(0, DEGREE - 1, order, 0)
    sides()
    apply((1,), jnp.float32(2.0 / half), jnp.float32(1.0), emit)


def turn(cur, at, s, part, value):
    shift = 30 if part == 0 else 2
    lanes = slice(PLANE + 128 * part, PLANE + 128 * (part + 1))
    cur[at, s, :, lanes] = pltpu.roll(value, shift, 0).astype(jnp.bfloat16)


def first_kernel(centre, half, got, w_ref, lines_ref, pairs_ref, spread_ref, out_ref, g_ref, cur, prev, acc):
    diagonal(got, pairs_ref, spread_ref, g_ref, centre)
    slabs = [got.at[:, NODES_DEV * s : NODES_DEV * (s + 1)] for s in range(3)]
    filter_step(slabs, w_ref, lines_ref, g_ref, out_ref, cur, prev, acc, half)


def later_kernel(half, c_ref, l_ref, r_ref, st_ref, w_ref, lines_ref, g_ref, out_ref, cur, prev, acc):
    out_ref[:, NODES_DEV:] = st_ref[...]
    filter_step((l_ref, c_ref, r_ref), w_ref, lines_ref, g_ref, out_ref, cur, prev, acc, half)


def corr_kernel(factor, got, filtered_ref, out_ref):
    filtered = got[:, :NODES_DEV]
    filtered_ref[...] = filtered
    four = jnp.concatenate([filtered] * 4, axis=0)
    parts = [
        lax.dot_general(
            got[:, NODES_DEV * (1 + part) : NODES_DEV * (2 + part)],
            four,
            (((1,), (1,)), ((), ())),
            preferred_element_type=jnp.float32,
        )
        for part in range(2)
    ]
    lane = lax.broadcasted_iota(jnp.int32, (NWF, 128), 1)
    row = lax.broadcasted_iota(jnp.int32, (NWF, 128), 0)
    both = jnp.where(lane // 32 % 2 == 0, parts[0], parts[1])
    out_ref[...] = jnp.where(lane // 64 == row % 2, both * factor, 0.0)


def share_kernel(got, out_ref):
    total = jnp.sum(got[...], axis=0, keepdims=True)
    lane = lax.broadcasted_iota(jnp.int32, (NWF, 128), 1)
    row = lax.broadcasted_iota(jnp.int32, (NWF, 128), 0)
    out_ref[...] = jnp.where(lane % NWF == row, total, 0.0)


def total_kernel(got, out_ref):
    total = jnp.sum(got[...], axis=0, keepdims=True)
    lane = lax.broadcasted_iota(jnp.int32, (1, 128), 1)
    rows = jnp.zeros((1, 128), jnp.float32)
    for row in range(4):
        mine = lane // 32 == row // 2 + 2 * (row % 2)
        rows = jnp.where(lane == row, jnp.sum(jnp.where(mine, total, 0.0), axis=1, keepdims=True), rows)
    out_ref[...] = rows[:, :4]


def full(shape):
    return pl.BlockSpec(shape, lambda *_: (0,) * len(shape))


def call(kernel, args, outs, scratch=()):
    return pl.pallas_call(
        kernel,
        grid=(1,),
        in_specs=[full(a.shape) for a in args],
        out_specs=[full(o.shape) for o in outs],
        out_shape=list(outs),
        scratch_shapes=list(scratch),
        compiler_params=pltpu.CompilerParams(vmem_limit_bytes=VMEM),
    )(*args)


def passed_along(block, axis, distance):
    devices = range(lax.axis_size(axis))
    route = [((i - distance) % len(devices), i) for i in devices]
    return lax.ppermute(block, axis, route)


def shards(cur_block, stored_blocks, cell_potential, connectivity):
    t = tables()
    bf, f32 = jnp.bfloat16, jnp.float32
    shape = jax.ShapeDtypeStruct
    n_cells, n_bands = lax.axis_size("cells"), lax.axis_size("bands")
    const = {k: jnp.asarray(v) for k, v in t.items() if isinstance(v, np.ndarray)}
    (message,) = call(
        message_kernel,
        (cur_block, cell_potential.T, connectivity.T, const["cell_codes"]),
        [shape((NWF, MESSAGE), bf)],
        [pltpu.VMEM((32, 128), f32)],
    )
    left = passed_along(message, "cells", 1)
    right = passed_along(message, "cells", -1)
    stored = stored_blocks.reshape(2, 2, n_bands, NODES_DEV).transpose(2, 1, 0, 3).reshape(NWF, 2 * NODES_DEV)
    (payload,) = call(
        pack_kernel,
        (message, left, right) + tuple(const[k] for k in ("places", "kinds", "mask", "to_x")),
        [shape((NWF, PAYLOAD), bf)],
        [pltpu.VMEM((32, 128), f32)],
    )
    got = lax.all_to_all(payload, "bands", 0, 0, tiled=True)
    scratch = [
        pltpu.VMEM((NXL, 3, NWF, 3 * PLANE), bf),
        pltpu.VMEM((NXL, 3, NWF, PLANE), bf),
        pltpu.VMEM((NXL, 3, NWF, PLANE), f32),
    ]
    block, diag = call(
        functools.partial(first_kernel, t["centre"], t["half"]),
        (got,) + tuple(const[k] for k in ("weights", "lines", "pairs", "spread")),
        [shape((NWF, NODES_DEV), bf), shape((NXL, 3, NWF, PLANE), f32)],
        scratch,
    )
    left = passed_along(block, "cells", 1)
    right = passed_along(block, "cells", -1)
    (block,) = call(
        functools.partial(later_kernel, t["half"]),
        (block, left, right, stored, const["weights"], const["lines"], diag),
        [shape((NWF, 3 * NODES_DEV), bf)],
        scratch,
    )
    got = lax.all_to_all(block, "bands", 0, 0, tiled=True)
    factor = 1.0 / math.sqrt(NODES_DEV * n_cells * n_bands)
    filtered, partial = call(
        functools.partial(corr_kernel, factor),
        (got,),
        [shape((NWF, NODES_DEV), bf), shape((NWF, 128), f32)],
    )
    partial = lax.all_to_all(partial, "bands", 0, 0, tiled=True)
    (partial,) = call(share_kernel, (partial,), [shape((NWF, 128), f32)])
    partial = lax.all_to_all(partial, "cells", 0, 0, tiled=True)
    (total,) = call(total_kernel, (partial,), [shape((1, 4), f32)])
    return (filtered, total.T)


def solution(mesh):
    in_specs = (
        P(None, ("cells", "bands")),
        P("bands", "cells"),
        P(None, ("cells", "bands")),
        P(None, ("cells", "bands")),
    )
    out_specs = (P(None, ("cells", "bands")), P("bands", "cells"))
    return jax.shard_map(shards, mesh=mesh, in_specs=in_specs, out_specs=out_specs, check_vma=False)
```

```python
import functools
import math

import jax
import jax.numpy as jnp
import ml_dtypes
import numpy as np
from jax import lax
from jax.experimental import pallas as pl
from jax.experimental.pallas import tpu as pltpu
from jax.sharding import PartitionSpec as P

NWF = 32
DEGREE = 4
STEPS = 2
NXL = 8
NODES_DEV = 2048
PLANE = 256
LANES_V = 384
MESSAGE = NODES_DEV + 256
V_AT = 3 * NODES_DEV
G_AT = 5 * NODES_DEV
PAYLOAD = G_AT + 2 * 128
X_ORDER = (0, 4, 1, 3, 5, 7, 2, 6)
CLASS_ROWS = ((0, 2), (2, 6), (6, 8))
VMEM = 48 * 1024 * 1024


def kinetic_table():
    points = [-1.0, -math.sqrt(3.0 / 7.0), 0.0, math.sqrt(3.0 / 7.0), 1.0]
    weights = [0.1, 49.0 / 90.0, 32.0 / 45.0, 49.0 / 90.0, 0.1]
    scales = []
    for row in range(5):
        prod_val = 1.0
        for other in range(5):
            if other != row:
                prod_val = prod_val * (points[row] - points[other])
        scales.append(prod_val)
    deriv = [[0.0] * 5 for row in range(5)]
    for row in range(5):
        for col in range(5):
            if row != col:
                deriv[row][col] = scales[row] / scales[col] / (points[row] - points[col])
            else:
                total = 0.0
                for other in range(5):
                    if other != row:
                        total = total + 1.0 / (points[row] - points[other])
                deriv[row][col] = total
    stiff_one = [
        [sum((deriv[i][a] * weights[i] * deriv[i][b] for i in range(5))) for b in range(5)]
        for a in range(5)
    ]
    mass_one = [[weights[a] if a == b else 0.0 for b in range(5)] for a in range(5)]
    table = [[0.0] * 125 for row in range(125)]
    for k in range(125):
        ka, kb, kc = (k // 25, k // 5 % 5, k % 5)
        for j in range(125):
            ja, jb, jc = (j // 25, j // 5 % 5, j % 5)
            table[k][j] = 0.5 * (
                stiff_one[ka][ja] * mass_one[kb][jb] * mass_one[kc][jc]
                + mass_one[ka][ja] * stiff_one[kb][jb] * mass_one[kc][jc]
                + mass_one[ka][ja] * mass_one[kb][jb] * stiff_one[kc][jc]
            )
    assembled = [dict() for row in range(512)]
    for cell_x in range(2):
        for cell_y in range(2):
            for cell_z in range(2):
                global_ids = []
                for k in range(125):
                    node_x = (4 * cell_x + k // 25) % 8
                    node_y = (4 * cell_y + k // 5 % 5) % 8
                    node_z = (4 * cell_z + k % 5) % 8
                    global_ids.append((node_x * 8 + node_y) * 8 + node_z)
                for k in range(125):
                    row_map = assembled[global_ids[k]]
                    for j in range(125):
                        target = global_ids[j]
                        row_map[target] = row_map.get(target, 0.0) + table[k][j]
    largest = 0.0
    for row_map in assembled:
        total = sum((abs(value) for value in row_map.values()))
        largest = max(largest, total)
    bound = largest + 8.0 * 2.0
    return (np.array(table), float(0.55 * bound), float(0.45 * bound))


@functools.lru_cache(maxsize=None)
def tables():
    table, centre, half = kinetic_table()
    kin = table.astype(np.float32).astype(ml_dtypes.bfloat16).astype(np.float64)
    kin = kin.reshape(5, 5, 5, 5, 5, 5)
    planes = np.zeros((3, 3, PLANE, PLANE))
    lines = np.zeros((5, 5, PLANE))
    for j in range(-1, 5):
        for l in range(-1, 5):
            for b in range(5):
                for c in range(5):
                    y, z = 4 * j + b, 4 * l + c
                    if not (0 <= y < 16 and 0 <= z < 16):
                        continue
                    at = 16 * y + z
                    for a in range(5):
                        for other in range(5):
                            if other != a:
                                lines[a, other, at] += kin[a, b, c, other, b, c]
                    for b2 in range(5):
                        for c2 in range(5):
                            y2, z2 = 4 * j + b2, 4 * l + c2
                            far_y, far_z = y2 // 16, z2 // 16
                            source = 16 * (y2 % 16) + z2 % 16
                            for kind, locals_a in enumerate(((0, 4), (1,), (2,))):
                                value = sum(kin[a, b, c, a, b2, c2] for a in locals_a)
                                if value == 0.0:
                                    continue
                                assert far_y == 0 or far_z == 0
                                part = 1 if far_y else 2 if far_z else 0
                                planes[kind, part, source, at] += value
    line_rows = np.stack(
        [lines[0, 1], lines[0, 2], lines[0, 3], 2.0 * lines[0, 4], lines[1, 2], lines[1, 3]]
    )
    bf = ml_dtypes.bfloat16
    weights = np.zeros((3 * 3 * PLANE + 16, PLANE))
    weights[: 9 * PLANE] = planes.reshape(9 * PLANE, PLANE)
    weights[9 * PLANE : 9 * PLANE + 6] = line_rows
    return weights.astype(np.float32).astype(bf), centre, half


def iota(shape, dim):
    return lax.broadcasted_iota(jnp.int32, shape, dim)


def local_node(k):
    a = (k * 41) >> 10
    rest = k - 25 * a
    b = (rest * 205) >> 10
    return a, b, rest - 5 * b


def message_kernel(v_hbm, pot_hbm, conn_hbm, out_ref, raw, conn, pot, sems):
    copies = [
        pltpu.make_async_copy(pot_hbm, raw, sems.at[0]),
        pltpu.make_async_copy(conn_hbm, conn, sems.at[1]),
        pltpu.make_async_copy(v_hbm, out_ref.at[:, :NODES_DEV], sems.at[2]),
    ]
    for copy in copies:
        copy.start()
    lane = iota((32, 128), 1)
    code = (4 * (lane >> 4) * 17 + 4 * ((lane >> 2) & 3)) * 17 + 4 * (lane & 3)
    pot[...] = jnp.zeros_like(pot)
    copies[0].wait()
    copies[1].wait()
    pot[:, :125] = raw[...]
    here = jnp.where((conn[:, 0:1] == code) & (lane < 32), lane.astype(jnp.float32), 0.0)
    cell = jnp.sum(here, axis=1, keepdims=True)
    high = pot[...].astype(jnp.bfloat16).astype(jnp.float32)
    low = pot[...] - high
    out_ref[:, NODES_DEV : NODES_DEV + 128] = jnp.where(lane == 127, cell, high).astype(jnp.bfloat16)
    out_ref[:, NODES_DEV + 128 :] = low.astype(jnp.bfloat16)
    copies[2].wait()


def pick_kind(kind):
    a, b, c = local_node(iota((1, 128), 1))
    if kind < 4:
        hit = (b == 4) == (kind >= 2), (c == 4) == (kind % 2 == 1)
    else:
        hit = (b == 4) == (kind == 5), c == 4
    return jnp.where(hit[0] & hit[1] & (iota((1, 128), 1) < 125), 1.0, 0.0)


def place_of(i, kind):
    lane = iota((1, LANES_V), 1)
    y, z = lane >> 4, lane & 15
    j = (y >> 2) - (kind // 2 if kind < 4 else kind - 4)
    l = (z >> 2) - kind % 2 if kind < 4 else jnp.where(z == 0, 3, -1)
    good = (lane < PLANE + 16) & (j >= 0) & (j < 4) & (l >= 0)
    return jnp.where(good, 16 * i + 4 * j + l, -1).astype(jnp.float32)


def nodal(own, left, mask):
    sides = [(own, range(4))] + ([(left, range(4, 6))] if left is not None else [])
    rows, ones = [], ([], [])
    for message, kind_range in sides:
        high = message[:, NODES_DEV : NODES_DEV + 128].astype(jnp.float32)
        low = message[:, NODES_DEV + 128 :].astype(jnp.float32)
        cell = high[:, 127:128]
        for kind in kind_range:
            pick = pick_kind(kind)
            rows += [high * pick, low * pick]
            for i in range(2):
                one = jnp.where(cell == place_of(i, kind), 1.0, 0.0)
                ones[i].extend([one, one])
    stack = jnp.concatenate(rows, axis=0).astype(jnp.bfloat16)
    total = jnp.zeros((8, LANES_V), jnp.float32)
    k = iota((8, 128), 1)
    along = local_node(k)[0]
    for i in range(2):
        placed = jnp.concatenate(ones[i], axis=0).astype(jnp.bfloat16)
        values = lax.dot_general(
            stack, placed, (((0,), (0,)), ((), ())), preferred_element_type=jnp.float32
        )
        values = values * mask
        high = values.astype(jnp.bfloat16)
        low = (values - high.astype(jnp.float32)).astype(jnp.bfloat16)
        to_x = jnp.where((((4 * i + along) & 7) == iota((8, 128), 0)) & (k < 125), 1.0, 0.0)
        to_x = to_x.astype(jnp.bfloat16)
        total += jnp.dot(to_x, high, preferred_element_type=jnp.float32)
        total += jnp.dot(to_x, low, preferred_element_type=jnp.float32)
    return total


def pack_kernel(c_ref, l_ref, r_ref, out_ref, ghost):
    messages = (l_ref, c_ref, r_ref)
    even = iota((32, PLANE), 0) % 2 == 0
    a, b, c = local_node(iota((128, LANES_V), 0))
    lane = iota((128, LANES_V), 1)
    fits = ((b & 3) == ((lane >> 4) & 3)) & ((c & 3) == (lane & 3)) & (lane < PLANE + 16)
    mask = jnp.where(fits, 1.0, 0.0)
    totals = []
    for s, message in enumerate(messages):
        out_ref[:, NODES_DEV * s : NODES_DEV * (s + 1)] = message[:, :NODES_DEV]
        totals.append(nodal(message, messages[s - 1] if s else None, mask))
    high = totals[1].astype(jnp.bfloat16).astype(jnp.float32)
    for part, (first, second) in enumerate(((high, totals[1] - high), (totals[0], totals[2]))):
        for x in range(NXL):
            main = jnp.where(even, first[x : x + 1, :PLANE], second[x : x + 1, :PLANE])
            at = V_AT + NODES_DEV * part + PLANE * x
            out_ref[:, at : at + PLANE] = main.astype(jnp.bfloat16)
            edge = jnp.where(even[:, :128], first[x : x + 1, PLANE:], second[x : x + 1, PLANE:])
            ghost[:, 16 * x : 16 * (x + 1)] = edge[:, :16]
        at = G_AT + 128 * part
        out_ref[:, at : at + 128] = ghost[...].astype(jnp.bfloat16)


def diagonal(got, g_ref, centre):
    lane, row = iota((128, NXL * 128), 1), iota((128, NXL * 128), 0)
    spread = jnp.where(((row >> 4) == (lane >> 7)) & ((row & 15) == (lane & 127)), 1.0, 0.0)
    spread = spread.astype(jnp.bfloat16)
    lane, row = iota((32, 64), 1), iota((32, 64), 0)
    source = jnp.where(lane < 32, row >> 1, ((row >> 1) + 15) & 15)
    same = source == ((lane & 31) >> 1)
    pairs = [
        jnp.where(same & good, 1.0, 0.0).astype(jnp.bfloat16)
        for good in ((lane & 1) == 0, lane >= 0, (lane & 1) == 1)
    ]
    edges = []
    for part in range(2):
        at = G_AT + 128 * part
        edge = jnp.dot(got[:, at : at + 128], spread, preferred_element_type=jnp.float32)
        edges.append(edge.astype(jnp.bfloat16))
    for s in range(3):
        part = 0 if s == 1 else 1
        for x in range(NXL):
            at = V_AT + NODES_DEV * part + PLANE * x
            stack = jnp.concatenate([got[:, at : at + 128], edges[part][:, 128 * x : 128 * (x + 1)]], axis=0)
            g_ref[x, s, :, :128] = jnp.dot(pairs[s], stack, preferred_element_type=jnp.float32) - centre
            g_ref[x, s, :, 128:] = (
                jnp.dot(pairs[s][:, :32], got[:, at + 128 : at + PLANE], preferred_element_type=jnp.float32)
                - centre
            )


def filter_step(slabs, w_ref, g_ref, out_ref, cur, prev, acc, half, ready):
    place = {x: at for at, x in enumerate(X_ORDER)}
    right_lanes = lax.broadcasted_iota(jnp.int32, (32, PLANE), 1) % 16 < 8
    for s, slab in enumerate(slabs):
        for x in range(NXL):
            block = slab[:, PLANE * x : PLANE * (x + 1)]
            cur[place[x], s, :, :PLANE] = block
            turn(cur, place[x], s, 0, block[:, :128].astype(jnp.float32))
            turn(cur, place[x], s, 1, block[:, 128:].astype(jnp.float32))
    prev[...] = jnp.zeros_like(prev)
    ready()
    lines = w_ref[9 * PLANE :, :].astype(jnp.float32)

    def weight(kind):
        return w_ref[3 * PLANE * kind : 3 * PLANE * (kind + 1), :]

    def sides():
        for at in range(NXL):
            left, middle, right = (cur[at, s, :, :PLANE].astype(jnp.float32) for s in range(3))
            zero = jnp.zeros_like(left)
            cur[at, 0, :, 2 * PLANE :] = jnp.where(right_lanes, middle, zero).astype(jnp.bfloat16)
            cur[at, 1, :, 2 * PLANE :] = jnp.where(right_lanes, right, left).astype(jnp.bfloat16)
            cur[at, 2, :, 2 * PLANE :] = jnp.where(right_lanes, zero, middle).astype(jnp.bfloat16)

    def apply(which, alpha, beta, store):
        first, last = which[0], which[-1] + 1
        for kind, (low, high) in enumerate(CLASS_ROWS):
            rows = cur[low:high, first:last]
            count = (high - low) * (last - first) * 32
            result = jnp.dot(
                rows.reshape(count, 3 * PLANE), weight(kind), preferred_element_type=jnp.float32
            )
            acc[low:high, first:last] = result.reshape(high - low, last - first, 32, PLANE)
        for s in which:
            for part in range(2):
                lanes = slice(128 * part, 128 * (part + 1))
                v = [cur[place[x], s, :, lanes].astype(jnp.float32) for x in range(NXL)]
                c01, c02, c03, c04, c12, c13 = (lines[row : row + 1, lanes] for row in range(6))
                s17, s26, s35 = v[1] + v[7], v[2] + v[6], v[3] + v[5]
                s04 = c02 * (v[0] + v[4])
                extra = {
                    0: c01 * s17 + c02 * s26 + c03 * s35 + c04 * v[4],
                    4: c01 * s35 + c02 * s26 + c03 * s17 + c04 * v[0],
                    1: c01 * v[0] + c12 * v[2] + c13 * v[3] + c03 * v[4],
                    3: c01 * v[4] + c12 * v[2] + c13 * v[1] + c03 * v[0],
                    5: c01 * v[4] + c12 * v[6] + c13 * v[7] + c03 * v[0],
                    7: c01 * v[0] + c12 * v[6] + c13 * v[5] + c03 * v[4],
                    2: s04 + c12 * (v[1] + v[3]),
                    6: s04 + c12 * (v[5] + v[7]),
                }
                for x in range(NXL):
                    at = place[x]
                    applied = acc[at, s, :, lanes] + extra[x] + g_ref[x, s, :, lanes] * v[x]
                    store(x, at, s, part, alpha * applied - beta * prev[at, s, :, lanes].astype(jnp.float32))

    def keep(x, at, s, part, new):
        lanes = slice(128 * part, 128 * (part + 1))
        prev[at, s, :, lanes] = cur[at, s, :, lanes]
        new = new.astype(jnp.bfloat16)
        cur[at, s, :, lanes] = new
        turn(cur, at, s, part, new.astype(jnp.float32))

    def emit(x, at, s, part, new):
        out_ref[:, PLANE * x + 128 * part : PLANE * x + 128 * (part + 1)] = new.astype(jnp.bfloat16)

    def order(k, carry):
        sides()
        alpha = jnp.where(k == 0, jnp.float32(1.0 / half), jnp.float32(2.0 / half))
        beta = jnp.where(k == 0, jnp.float32(0.0), jnp.float32(1.0))
        apply((0, 1, 2), alpha, beta, keep)
        return carry

    lax.fori_loop(0, DEGREE - 1, order, 0)
    sides()
    apply((1,), jnp.float32(2.0 / half), jnp.float32(1.0), emit)


def turn(cur, at, s, part, value):
    shift = 30 if part == 0 else 2
    lanes = slice(PLANE + 128 * part, PLANE + 128 * (part + 1))
    cur[at, s, :, lanes] = pltpu.roll(value, shift, 0).astype(jnp.bfloat16)


def first_kernel(centre, half, got, w_hbm, out_ref, g_ref, cur, prev, acc, w_ref, sem):
    copy = pltpu.make_async_copy(w_hbm, w_ref, sem)
    copy.start()
    diagonal(got, g_ref, centre)
    slabs = [got.at[:, NODES_DEV * s : NODES_DEV * (s + 1)] for s in range(3)]
    filter_step(slabs, w_ref, g_ref, out_ref, cur, prev, acc, half, copy.wait)


def later_kernel(
    half, factor, c_ref, l_ref, r_ref, g_ref, w_hbm, st_hbm, out_ref, cur, prev, acc, w_ref, st_ref, sem, st_sem
):
    copy = pltpu.make_async_copy(w_hbm, w_ref, sem)
    copy.start()
    st_copy = pltpu.make_async_copy(st_hbm, st_ref, st_sem)
    st_copy.start()
    filter_step((l_ref, c_ref, r_ref), w_ref, g_ref, out_ref, cur, prev, acc, half, copy.wait)
    st_copy.wait()
    filtered = out_ref[:, :NODES_DEV]
    shape = (NWF, 256)
    lane, row = iota(shape, 1), iota(shape, 0)
    own = ((lane >> 2) & 15) == (row >> 1)
    even = (iota((NWF, 128), 0) & 1) == 0
    lane, row = iota((NWF, 128), 1), iota((NWF, 128), 0)
    result = jnp.zeros((NWF, 128), jnp.float32)
    for block in range(4):
        product = lax.dot_general(
            filtered,
            st_ref[256 * block : 256 * (block + 1), :],
            (((1,), (1,)), ((), ())),
            preferred_element_type=jnp.float32,
        )
        product = jnp.where(own, product * factor, 0.0)
        for side in range(2):
            values = product[:, 128 * side : 128 * (side + 1)]
            first = jnp.sum(jnp.where(even, values, 0.0), axis=0, keepdims=True)
            second = jnp.sum(jnp.where(even, 0.0, values), axis=0, keepdims=True)
            values = jnp.where(even, first, second)
            for shift in (4, 8, 16, 32):
                values = values + pltpu.roll(values, shift, 1)
            here = (row >> 2) == 2 * block + side
            here = here & ((lane >> 2) == 15 + 16 * ((row >> 1) & 1))
            result = jnp.where(here, values, result)
    for part in range(3):
        rounded = result.astype(jnp.bfloat16)
        out_ref[:, NODES_DEV + 128 * part : NODES_DEV + 128 * (part + 1)] = rounded
        result = result - rounded.astype(jnp.float32)


def share_kernel(got, out_ref):
    parts = [
        got[:, NODES_DEV + 128 * part : NODES_DEV + 128 * (part + 1)].astype(jnp.float32) for part in range(3)
    ]
    out_ref[...] = parts[0] + (parts[1] + parts[2])


def total_kernel(got, out_ref):
    total = jnp.sum(got[...], axis=0, keepdims=True)
    lane = iota((1, 128), 1)
    rows = jnp.zeros((1, 128), jnp.float32)
    for row in range(4):
        mine = jnp.where((lane & 3) == row, total, 0.0)
        rows = jnp.where(lane == row, jnp.sum(mine, axis=1, keepdims=True), rows)
    out_ref[...] = rows[:, :4]


def full(shape):
    return pl.BlockSpec(shape, lambda *_: (0,) * len(shape))


def call(kernel, args, outs, scratch=(), far=(), limit=VMEM):
    hbm = pl.BlockSpec(memory_space=pltpu.HBM)
    return pl.pallas_call(
        kernel,
        grid=(1,),
        in_specs=[full(a.shape) for a in args] + [hbm] * len(far),
        out_specs=[full(o.shape) for o in outs],
        out_shape=list(outs),
        scratch_shapes=list(scratch),
        compiler_params=pltpu.CompilerParams(vmem_limit_bytes=limit),
    )(*args, *far)


def passed_along(block, axis, distance):
    devices = range(lax.axis_size(axis))
    route = [((i - distance) % len(devices), i) for i in devices]
    return lax.ppermute(block, axis, route)


def shards(cur_block, stored_blocks, cell_potential, connectivity):
    weights, centre, half = tables()
    weights = jnp.asarray(weights)
    bf, f32 = jnp.bfloat16, jnp.float32
    shape = jax.ShapeDtypeStruct
    n_cells, n_bands = lax.axis_size("cells"), lax.axis_size("bands")
    stored = stored_blocks.reshape(4, n_bands, NODES_DEV).transpose(1, 0, 2).reshape(4 * n_bands, NODES_DEV)
    stored = lax.all_gather(stored, "bands", axis=0, tiled=True)
    dma = pltpu.SemaphoreType.DMA
    (message,) = call(
        message_kernel,
        (),
        [shape((NWF, MESSAGE), bf)],
        [
            pltpu.VMEM((32, 125), f32),
            pltpu.VMEM((32, 125), jnp.int32),
            pltpu.VMEM((32, 128), f32),
            dma((3,)),
        ],
        (cur_block, cell_potential.T, connectivity.T),
        62 * 1024 * 1024,
    )
    left = passed_along(message, "cells", 1)
    right = passed_along(message, "cells", -1)
    (payload,) = call(
        pack_kernel,
        (message, left, right),
        [shape((NWF, PAYLOAD), bf)],
        [pltpu.VMEM((32, 128), f32)],
    )
    got = lax.all_to_all(payload, "bands", 0, 0, tiled=True)
    scratch = [
        pltpu.VMEM((NXL, 3, NWF, 3 * PLANE), bf),
        pltpu.VMEM((NXL, 3, NWF, PLANE), bf),
        pltpu.VMEM((NXL, 3, NWF, PLANE), f32),
        pltpu.VMEM(weights.shape, bf),
    ]
    block, diag = call(
        functools.partial(first_kernel, centre, half),
        (got,),
        [shape((NWF, NODES_DEV), bf), shape((NXL, 3, NWF, PLANE), f32)],
        scratch + [dma],
        (weights,),
    )
    left = passed_along(block, "cells", 1)
    right = passed_along(block, "cells", -1)
    factor = 1.0 / math.sqrt(NODES_DEV * n_cells * n_bands)
    (block,) = call(
        functools.partial(later_kernel, half, factor),
        (block, left, right, diag),
        [shape((NWF, NODES_DEV + 3 * 128), bf)],
        scratch + [pltpu.VMEM(stored.shape, bf), dma, dma],
        (weights, stored),
    )
    got = lax.all_to_all(block, "bands", 0, 0, tiled=True)
    filtered = got[:, :NODES_DEV]
    (partial,) = call(share_kernel, (got,), [shape((NWF, 128), f32)])
    partial = lax.all_to_all(partial, "cells", 0, 0, tiled=True)
    (total,) = call(total_kernel, (partial,), [shape((1, 4), f32)])
    return (filtered, total.T)


def solution(mesh):
    in_specs = (
        P(None, ("cells", "bands")),
        P("bands", "cells"),
        P(None, ("cells", "bands")),
        P(None, ("cells", "bands")),
    )
    out_specs = (P(None, ("cells", "bands")), P("bands", "cells"))
    return jax.shard_map(shards, mesh=mesh, in_specs=in_specs, out_specs=out_specs, check_vma=False)
```

```python
import functools
import math

import jax
import jax.numpy as jnp
import ml_dtypes
import numpy as np
from jax import lax
from jax.experimental import pallas as pl
from jax.experimental.pallas import tpu as pltpu
from jax.sharding import PartitionSpec as P

NWF = 32
DEGREE = 4
STEPS = 2
NXL = 8
NODES_DEV = 2048
PLANE = 256
LANES_V = 384
MESSAGE = NODES_DEV + 256
V_AT = 3 * NODES_DEV
G_AT = 5 * NODES_DEV
PAYLOAD = G_AT + 2 * 128
X_ORDER = (0, 4, 1, 3, 5, 7, 2, 6)
CLASS_ROWS = ((0, 2), (2, 6), (6, 8))
VMEM = 48 * 1024 * 1024


def kinetic_table():
    points = [-1.0, -math.sqrt(3.0 / 7.0), 0.0, math.sqrt(3.0 / 7.0), 1.0]
    weights = [0.1, 49.0 / 90.0, 32.0 / 45.0, 49.0 / 90.0, 0.1]
    scales = []
    for row in range(5):
        prod_val = 1.0
        for other in range(5):
            if other != row:
                prod_val = prod_val * (points[row] - points[other])
        scales.append(prod_val)
    deriv = [[0.0] * 5 for row in range(5)]
    for row in range(5):
        for col in range(5):
            if row != col:
                deriv[row][col] = scales[row] / scales[col] / (points[row] - points[col])
            else:
                total = 0.0
                for other in range(5):
                    if other != row:
                        total = total + 1.0 / (points[row] - points[other])
                deriv[row][col] = total
    stiff_one = [
        [sum((deriv[i][a] * weights[i] * deriv[i][b] for i in range(5))) for b in range(5)]
        for a in range(5)
    ]
    mass_one = [[weights[a] if a == b else 0.0 for b in range(5)] for a in range(5)]
    table = [[0.0] * 125 for row in range(125)]
    for k in range(125):
        ka, kb, kc = (k // 25, k // 5 % 5, k % 5)
        for j in range(125):
            ja, jb, jc = (j // 25, j // 5 % 5, j % 5)
            table[k][j] = 0.5 * (
                stiff_one[ka][ja] * mass_one[kb][jb] * mass_one[kc][jc]
                + mass_one[ka][ja] * stiff_one[kb][jb] * mass_one[kc][jc]
                + mass_one[ka][ja] * mass_one[kb][jb] * stiff_one[kc][jc]
            )
    assembled = [dict() for row in range(512)]
    for cell_x in range(2):
        for cell_y in range(2):
            for cell_z in range(2):
                global_ids = []
                for k in range(125):
                    node_x = (4 * cell_x + k // 25) % 8
                    node_y = (4 * cell_y + k // 5 % 5) % 8
                    node_z = (4 * cell_z + k % 5) % 8
                    global_ids.append((node_x * 8 + node_y) * 8 + node_z)
                for k in range(125):
                    row_map = assembled[global_ids[k]]
                    for j in range(125):
                        target = global_ids[j]
                        row_map[target] = row_map.get(target, 0.0) + table[k][j]
    largest = 0.0
    for row_map in assembled:
        total = sum((abs(value) for value in row_map.values()))
        largest = max(largest, total)
    bound = largest + 8.0 * 2.0
    return (np.array(table), float(0.55 * bound), float(0.45 * bound))


@functools.lru_cache(maxsize=None)
def tables():
    table, centre, half = kinetic_table()
    kin = table.astype(np.float32).astype(ml_dtypes.bfloat16).astype(np.float64)
    kin = kin.reshape(5, 5, 5, 5, 5, 5)
    planes = np.zeros((3, 3, PLANE, PLANE))
    lines = np.zeros((5, 5, PLANE))
    for j in range(-1, 5):
        for l in range(-1, 5):
            for b in range(5):
                for c in range(5):
                    y, z = 4 * j + b, 4 * l + c
                    if not (0 <= y < 16 and 0 <= z < 16):
                        continue
                    at = 16 * y + z
                    for a in range(5):
                        for other in range(5):
                            if other != a:
                                lines[a, other, at] += kin[a, b, c, other, b, c]
                    for b2 in range(5):
                        for c2 in range(5):
                            y2, z2 = 4 * j + b2, 4 * l + c2
                            far_y, far_z = y2 // 16, z2 // 16
                            source = 16 * (y2 % 16) + z2 % 16
                            for kind, locals_a in enumerate(((0, 4), (1,), (2,))):
                                value = sum(kin[a, b, c, a, b2, c2] for a in locals_a)
                                if value == 0.0:
                                    continue
                                assert far_y == 0 or far_z == 0
                                part = 1 if far_y else 2 if far_z else 0
                                planes[kind, part, source, at] += value
    line_rows = np.stack(
        [lines[0, 1], lines[0, 2], lines[0, 3], 2.0 * lines[0, 4], lines[1, 2], lines[1, 3]]
    )
    bf = ml_dtypes.bfloat16
    weights = np.zeros((3 * 3 * PLANE + 16, PLANE))
    weights[: 9 * PLANE] = planes.reshape(9 * PLANE, PLANE)
    weights[9 * PLANE : 9 * PLANE + 6] = line_rows
    return weights.astype(np.float32).astype(bf), centre, half


def iota(shape, dim):
    return lax.broadcasted_iota(jnp.int32, shape, dim)


def local_node(k):
    a = (k * 41) >> 10
    rest = k - 25 * a
    b = (rest * 205) >> 10
    return a, b, rest - 5 * b


def message_kernel(v_hbm, pot_hbm, conn_hbm, out_ref, raw, conn, pot, sems):
    copies = [
        pltpu.make_async_copy(pot_hbm, raw, sems.at[0]),
        pltpu.make_async_copy(conn_hbm, conn, sems.at[1]),
        pltpu.make_async_copy(v_hbm, out_ref.at[:, :NODES_DEV], sems.at[2]),
    ]
    for copy in copies:
        copy.start()
    lane = iota((32, 128), 1)
    code = (4 * (lane >> 4) * 17 + 4 * ((lane >> 2) & 3)) * 17 + 4 * (lane & 3)
    pot[...] = jnp.zeros_like(pot)
    copies[0].wait()
    copies[1].wait()
    pot[:, :125] = raw[...]
    here = jnp.where((conn[:, 0:1] == code) & (lane < 32), lane.astype(jnp.float32), 0.0)
    cell = jnp.sum(here, axis=1, keepdims=True)
    high = pot[...].astype(jnp.bfloat16).astype(jnp.float32)
    low = pot[...] - high
    out_ref[:, NODES_DEV : NODES_DEV + 128] = jnp.where(lane == 127, cell, high).astype(jnp.bfloat16)
    out_ref[:, NODES_DEV + 128 :] = low.astype(jnp.bfloat16)
    copies[2].wait()


def pick_kind(kind):
    a, b, c = local_node(iota((1, 128), 1))
    if kind < 4:
        hit = (b == 4) == (kind >= 2), (c == 4) == (kind % 2 == 1)
    else:
        hit = (b == 4) == (kind == 5), c == 4
    return jnp.where(hit[0] & hit[1] & (iota((1, 128), 1) < 125), 1.0, 0.0)


def place_of(i, kind):
    lane = iota((1, LANES_V), 1)
    y, z = lane >> 4, lane & 15
    j = (y >> 2) - (kind // 2 if kind < 4 else kind - 4)
    l = (z >> 2) - kind % 2 if kind < 4 else jnp.where(z == 0, 3, -1)
    good = (lane < PLANE + 16) & (j >= 0) & (j < 4) & (l >= 0)
    return jnp.where(good, 16 * i + 4 * j + l, -1).astype(jnp.float32)


def nodal(own, left, mask):
    sides = [(own, range(4))] + ([(left, range(4, 6))] if left is not None else [])
    rows, ones = [], ([], [])
    for message, kind_range in sides:
        high = message[:, NODES_DEV : NODES_DEV + 128].astype(jnp.float32)
        low = message[:, NODES_DEV + 128 :].astype(jnp.float32)
        cell = high[:, 127:128]
        for kind in kind_range:
            pick = pick_kind(kind)
            rows += [high * pick, low * pick]
            for i in range(2):
                one = jnp.where(cell == place_of(i, kind), 1.0, 0.0)
                ones[i].extend([one, one])
    stack = jnp.concatenate(rows, axis=0).astype(jnp.bfloat16)
    total = jnp.zeros((8, LANES_V), jnp.float32)
    k = iota((8, 128), 1)
    along = local_node(k)[0]
    for i in range(2):
        placed = jnp.concatenate(ones[i], axis=0).astype(jnp.bfloat16)
        values = lax.dot_general(
            stack, placed, (((0,), (0,)), ((), ())), preferred_element_type=jnp.float32
        )
        values = values * mask
        high = values.astype(jnp.bfloat16)
        low = (values - high.astype(jnp.float32)).astype(jnp.bfloat16)
        to_x = jnp.where((((4 * i + along) & 7) == iota((8, 128), 0)) & (k < 125), 1.0, 0.0)
        to_x = to_x.astype(jnp.bfloat16)
        total += jnp.dot(to_x, high, preferred_element_type=jnp.float32)
        total += jnp.dot(to_x, low, preferred_element_type=jnp.float32)
    return total


def pack_kernel(c_ref, l_ref, r_ref, out_ref, ghost):
    messages = (l_ref, c_ref, r_ref)
    even = iota((32, PLANE), 0) % 2 == 0
    a, b, c = local_node(iota((128, LANES_V), 0))
    lane = iota((128, LANES_V), 1)
    fits = ((b & 3) == ((lane >> 4) & 3)) & ((c & 3) == (lane & 3)) & (lane < PLANE + 16)
    mask = jnp.where(fits, 1.0, 0.0)
    totals = []
    for s, message in enumerate(messages):
        out_ref[:, NODES_DEV * s : NODES_DEV * (s + 1)] = message[:, :NODES_DEV]
        totals.append(nodal(message, messages[s - 1] if s else None, mask))
    high = totals[1].astype(jnp.bfloat16).astype(jnp.float32)
    for part, (first, second) in enumerate(((high, totals[1] - high), (totals[0], totals[2]))):
        for x in range(NXL):
            main = jnp.where(even, first[x : x + 1, :PLANE], second[x : x + 1, :PLANE])
            at = V_AT + NODES_DEV * part + PLANE * x
            out_ref[:, at : at + PLANE] = main.astype(jnp.bfloat16)
            edge = jnp.where(even[:, :128], first[x : x + 1, PLANE:], second[x : x + 1, PLANE:])
            ghost[:, 16 * x : 16 * (x + 1)] = edge[:, :16]
        at = G_AT + 128 * part
        out_ref[:, at : at + 128] = ghost[...].astype(jnp.bfloat16)


def diagonal(got, g_ref, centre):
    lane, row = iota((128, NXL * 128), 1), iota((128, NXL * 128), 0)
    spread = jnp.where(((row >> 4) == (lane >> 7)) & ((row & 15) == (lane & 127)), 1.0, 0.0)
    spread = spread.astype(jnp.bfloat16)
    lane, row = iota((32, 64), 1), iota((32, 64), 0)
    source = jnp.where(lane < 32, row >> 1, ((row >> 1) + 15) & 15)
    same = source == ((lane & 31) >> 1)
    pairs = [
        jnp.where(same & good, 1.0, 0.0).astype(jnp.bfloat16)
        for good in ((lane & 1) == 0, lane >= 0, (lane & 1) == 1)
    ]
    edges = []
    for part in range(2):
        at = G_AT + 128 * part
        edge = jnp.dot(got[:, at : at + 128], spread, preferred_element_type=jnp.float32)
        edges.append(edge.astype(jnp.bfloat16))
    for s in range(3):
        part = 0 if s == 1 else 1
        for x in range(NXL):
            at = V_AT + NODES_DEV * part + PLANE * x
            stack = jnp.concatenate([got[:, at : at + 128], edges[part][:, 128 * x : 128 * (x + 1)]], axis=0)
            g_ref[x, s, :, :128] = jnp.dot(pairs[s], stack, preferred_element_type=jnp.float32) - centre
            g_ref[x, s, :, 128:] = (
                jnp.dot(pairs[s][:, :32], got[:, at + 128 : at + PLANE], preferred_element_type=jnp.float32)
                - centre
            )


def filter_step(slabs, w_ref, g_ref, out_ref, cur, prev, acc, half, ready):
    place = {x: at for at, x in enumerate(X_ORDER)}
    right_lanes = lax.broadcasted_iota(jnp.int32, (32, PLANE), 1) % 16 < 8
    for s, slab in enumerate(slabs):
        for x in range(NXL):
            block = slab[:, PLANE * x : PLANE * (x + 1)]
            cur[place[x], s, :, :PLANE] = block
            turn(cur, place[x], s, 0, block[:, :128].astype(jnp.float32))
            turn(cur, place[x], s, 1, block[:, 128:].astype(jnp.float32))
    prev[...] = jnp.zeros_like(prev)
    ready()
    lines = w_ref[9 * PLANE :, :].astype(jnp.float32)

    def weight(kind):
        return w_ref[3 * PLANE * kind : 3 * PLANE * (kind + 1), :]

    def sides():
        for at in range(NXL):
            left, middle, right = (cur[at, s, :, :PLANE].astype(jnp.float32) for s in range(3))
            zero = jnp.zeros_like(left)
            cur[at, 0, :, 2 * PLANE :] = jnp.where(right_lanes, middle, zero).astype(jnp.bfloat16)
            cur[at, 1, :, 2 * PLANE :] = jnp.where(right_lanes, right, left).astype(jnp.bfloat16)
            cur[at, 2, :, 2 * PLANE :] = jnp.where(right_lanes, zero, middle).astype(jnp.bfloat16)

    def apply(which, alpha, beta, store):
        first, last = which[0], which[-1] + 1
        for kind, (low, high) in enumerate(CLASS_ROWS):
            rows = cur[low:high, first:last]
            count = (high - low) * (last - first) * 32
            result = jnp.dot(
                rows.reshape(count, 3 * PLANE), weight(kind), preferred_element_type=jnp.float32
            )
            acc[low:high, first:last] = result.reshape(high - low, last - first, 32, PLANE)
        for s in which:
            for part in range(2):
                lanes = slice(128 * part, 128 * (part + 1))
                v = [cur[place[x], s, :, lanes].astype(jnp.float32) for x in range(NXL)]
                c01, c02, c03, c04, c12, c13 = (lines[row : row + 1, lanes] for row in range(6))
                s17, s26, s35 = v[1] + v[7], v[2] + v[6], v[3] + v[5]
                s04 = c02 * (v[0] + v[4])
                extra = {
                    0: c01 * s17 + c02 * s26 + c03 * s35 + c04 * v[4],
                    4: c01 * s35 + c02 * s26 + c03 * s17 + c04 * v[0],
                    1: c01 * v[0] + c12 * v[2] + c13 * v[3] + c03 * v[4],
                    3: c01 * v[4] + c12 * v[2] + c13 * v[1] + c03 * v[0],
                    5: c01 * v[4] + c12 * v[6] + c13 * v[7] + c03 * v[0],
                    7: c01 * v[0] + c12 * v[6] + c13 * v[5] + c03 * v[4],
                    2: s04 + c12 * (v[1] + v[3]),
                    6: s04 + c12 * (v[5] + v[7]),
                }
                for x in range(NXL):
                    at = place[x]
                    applied = acc[at, s, :, lanes] + extra[x] + g_ref[x, s, :, lanes] * v[x]
                    store(x, at, s, part, alpha * applied - beta * prev[at, s, :, lanes].astype(jnp.float32))

    def keep(x, at, s, part, new):
        lanes = slice(128 * part, 128 * (part + 1))
        prev[at, s, :, lanes] = cur[at, s, :, lanes]
        new = new.astype(jnp.bfloat16)
        cur[at, s, :, lanes] = new
        turn(cur, at, s, part, new.astype(jnp.float32))

    def emit(x, at, s, part, new):
        out_ref[:, PLANE * x + 128 * part : PLANE * x + 128 * (part + 1)] = new.astype(jnp.bfloat16)

    def order(k, carry):
        sides()
        alpha = jnp.where(k == 0, jnp.float32(1.0 / half), jnp.float32(2.0 / half))
        beta = jnp.where(k == 0, jnp.float32(0.0), jnp.float32(1.0))
        apply((0, 1, 2), alpha, beta, keep)
        return carry

    lax.fori_loop(0, DEGREE - 1, order, 0)
    sides()
    apply((1,), jnp.float32(2.0 / half), jnp.float32(1.0), emit)


def turn(cur, at, s, part, value):
    shift = 30 if part == 0 else 2
    lanes = slice(PLANE + 128 * part, PLANE + 128 * (part + 1))
    cur[at, s, :, lanes] = pltpu.roll(value, shift, 0).astype(jnp.bfloat16)


def first_kernel(centre, half, got, w_hbm, out_ref, g_ref, cur, prev, acc, w_ref, sem):
    copy = pltpu.make_async_copy(w_hbm, w_ref, sem)
    copy.start()
    diagonal(got, g_ref, centre)
    slabs = [got.at[:, NODES_DEV * s : NODES_DEV * (s + 1)] for s in range(3)]
    filter_step(slabs, w_ref, g_ref, out_ref, cur, prev, acc, half, copy.wait)


def later_kernel(half, c_ref, l_ref, r_ref, g_ref, st_ref, w_hbm, out_ref, cur, prev, acc, w_ref, sem):
    copy = pltpu.make_async_copy(w_hbm, w_ref, sem)
    copy.start()
    out_ref[:, NODES_DEV:] = st_ref[...]
    filter_step((l_ref, c_ref, r_ref), w_ref, g_ref, out_ref, cur, prev, acc, half, copy.wait)


def corr_kernel(factor, got, out_ref):
    four = jnp.concatenate([got[:, :NODES_DEV]] * 4, axis=0)
    parts = [
        lax.dot_general(
            got[:, NODES_DEV * (1 + part) : NODES_DEV * (2 + part)],
            four,
            (((1,), (1,)), ((), ())),
            preferred_element_type=jnp.float32,
        )
        for part in range(2)
    ]
    lane, row = iota((NWF, 128), 1), iota((NWF, 128), 0)
    both = jnp.where(((lane >> 5) & 1) == 0, parts[0], parts[1])
    out_ref[...] = jnp.where((lane >> 6) == (row & 1), both * factor, 0.0)


def share_kernel(got, out_ref):
    total = jnp.sum(got[...], axis=0, keepdims=True)
    out_ref[...] = jnp.where((iota((NWF, 128), 1) & 31) == iota((NWF, 128), 0), total, 0.0)


def total_kernel(got, out_ref):
    total = jnp.sum(got[...], axis=0, keepdims=True)
    lane = iota((1, 128), 1)
    rows = jnp.zeros((1, 128), jnp.float32)
    for row in range(4):
        mine = jnp.where((lane >> 5) == row // 2 + 2 * (row % 2), total, 0.0)
        rows = jnp.where(lane == row, jnp.sum(mine, axis=1, keepdims=True), rows)
    out_ref[...] = rows[:, :4]


def full(shape):
    return pl.BlockSpec(shape, lambda *_: (0,) * len(shape))


def call(kernel, args, outs, scratch=(), far=(), limit=VMEM):
    hbm = pl.BlockSpec(memory_space=pltpu.HBM)
    return pl.pallas_call(
        kernel,
        grid=(1,),
        in_specs=[full(a.shape) for a in args] + [hbm] * len(far),
        out_specs=[full(o.shape) for o in outs],
        out_shape=list(outs),
        scratch_shapes=list(scratch),
        compiler_params=pltpu.CompilerParams(vmem_limit_bytes=limit),
    )(*args, *far)


def passed_along(block, axis, distance):
    devices = range(lax.axis_size(axis))
    route = [((i - distance) % len(devices), i) for i in devices]
    return lax.ppermute(block, axis, route)


def shards(cur_block, stored_blocks, cell_potential, connectivity):
    weights, centre, half = tables()
    weights = jnp.asarray(weights)
    bf, f32 = jnp.bfloat16, jnp.float32
    shape = jax.ShapeDtypeStruct
    n_cells, n_bands = lax.axis_size("cells"), lax.axis_size("bands")
    stored = stored_blocks.reshape(2, 2, n_bands, NODES_DEV).transpose(2, 1, 0, 3).reshape(NWF, 2 * NODES_DEV)
    dma = pltpu.SemaphoreType.DMA
    (message,) = call(
        message_kernel,
        (),
        [shape((NWF, MESSAGE), bf)],
        [
            pltpu.VMEM((32, 125), f32),
            pltpu.VMEM((32, 125), jnp.int32),
            pltpu.VMEM((32, 128), f32),
            dma((3,)),
        ],
        (cur_block, cell_potential.T, connectivity.T),
        62 * 1024 * 1024,
    )
    left = passed_along(message, "cells", 1)
    right = passed_along(message, "cells", -1)
    (payload,) = call(
        pack_kernel,
        (message, left, right),
        [shape((NWF, PAYLOAD), bf)],
        [pltpu.VMEM((32, 128), f32)],
    )
    got = lax.all_to_all(payload, "bands", 0, 0, tiled=True)
    scratch = [
        pltpu.VMEM((NXL, 3, NWF, 3 * PLANE), bf),
        pltpu.VMEM((NXL, 3, NWF, PLANE), bf),
        pltpu.VMEM((NXL, 3, NWF, PLANE), f32),
        pltpu.VMEM(weights.shape, bf),
    ]
    block, diag = call(
        functools.partial(first_kernel, centre, half),
        (got,),
        [shape((NWF, NODES_DEV), bf), shape((NXL, 3, NWF, PLANE), f32)],
        scratch + [dma],
        (weights,),
    )
    left = passed_along(block, "cells", 1)
    right = passed_along(block, "cells", -1)
    factor = 1.0 / math.sqrt(NODES_DEV * n_cells * n_bands)
    (block,) = call(
        functools.partial(later_kernel, half),
        (block, left, right, diag, stored),
        [shape((NWF, 3 * NODES_DEV), bf)],
        scratch + [dma],
        (weights,),
    )
    got = lax.all_to_all(block, "bands", 0, 0, tiled=True)
    filtered = got[:, :NODES_DEV]
    (partial,) = call(functools.partial(corr_kernel, factor), (got,), [shape((NWF, 128), f32)])
    partial = lax.all_to_all(partial, "bands", 0, 0, tiled=True)
    (partial,) = call(share_kernel, (partial,), [shape((NWF, 128), f32)])
    partial = lax.all_to_all(partial, "cells", 0, 0, tiled=True)
    (total,) = call(total_kernel, (partial,), [shape((1, 4), f32)])
    return (filtered, total.T)


def solution(mesh):
    in_specs = (
        P(None, ("cells", "bands")),
        P("bands", "cells"),
        P(None, ("cells", "bands")),
        P(None, ("cells", "bands")),
    )
    out_specs = (P(None, ("cells", "bands")), P("bands", "cells"))
    return jax.shard_map(shards, mesh=mesh, in_specs=in_specs, out_specs=out_specs, check_vma=False)
```

```python
import functools
import math

import jax
import jax.numpy as jnp
import ml_dtypes
import numpy as np
from jax import lax
from jax.experimental import pallas as pl
from jax.experimental.pallas import tpu as pltpu
from jax.sharding import PartitionSpec as P

NWF = 32
DEGREE = 4
STEPS = 2
NXL = 8
NODES_DEV = 2048
PLANE = 256
LANES_V = 384
MESSAGE = NODES_DEV + 256
V_AT = 3 * NODES_DEV
G_AT = 5 * NODES_DEV
PAYLOAD = G_AT + 2 * 128
X_ORDER = (0, 4, 1, 3, 5, 7, 2, 6)
CLASS_ROWS = ((0, 2), (2, 6), (6, 8))
VMEM = 48 * 1024 * 1024


def kinetic_table():
    points = [-1.0, -math.sqrt(3.0 / 7.0), 0.0, math.sqrt(3.0 / 7.0), 1.0]
    weights = [0.1, 49.0 / 90.0, 32.0 / 45.0, 49.0 / 90.0, 0.1]
    scales = []
    for row in range(5):
        prod_val = 1.0
        for other in range(5):
            if other != row:
                prod_val = prod_val * (points[row] - points[other])
        scales.append(prod_val)
    deriv = [[0.0] * 5 for row in range(5)]
    for row in range(5):
        for col in range(5):
            if row != col:
                deriv[row][col] = scales[row] / scales[col] / (points[row] - points[col])
            else:
                total = 0.0
                for other in range(5):
                    if other != row:
                        total = total + 1.0 / (points[row] - points[other])
                deriv[row][col] = total
    stiff_one = [
        [sum((deriv[i][a] * weights[i] * deriv[i][b] for i in range(5))) for b in range(5)]
        for a in range(5)
    ]
    mass_one = [[weights[a] if a == b else 0.0 for b in range(5)] for a in range(5)]
    table = [[0.0] * 125 for row in range(125)]
    for k in range(125):
        ka, kb, kc = (k // 25, k // 5 % 5, k % 5)
        for j in range(125):
            ja, jb, jc = (j // 25, j // 5 % 5, j % 5)
            table[k][j] = 0.5 * (
                stiff_one[ka][ja] * mass_one[kb][jb] * mass_one[kc][jc]
                + mass_one[ka][ja] * stiff_one[kb][jb] * mass_one[kc][jc]
                + mass_one[ka][ja] * mass_one[kb][jb] * stiff_one[kc][jc]
            )
    assembled = [dict() for row in range(512)]
    for cell_x in range(2):
        for cell_y in range(2):
            for cell_z in range(2):
                global_ids = []
                for k in range(125):
                    node_x = (4 * cell_x + k // 25) % 8
                    node_y = (4 * cell_y + k // 5 % 5) % 8
                    node_z = (4 * cell_z + k % 5) % 8
                    global_ids.append((node_x * 8 + node_y) * 8 + node_z)
                for k in range(125):
                    row_map = assembled[global_ids[k]]
                    for j in range(125):
                        target = global_ids[j]
                        row_map[target] = row_map.get(target, 0.0) + table[k][j]
    largest = 0.0
    for row_map in assembled:
        total = sum((abs(value) for value in row_map.values()))
        largest = max(largest, total)
    bound = largest + 8.0 * 2.0
    return (np.array(table), float(0.55 * bound), float(0.45 * bound))


@functools.lru_cache(maxsize=None)
def tables():
    table, centre, half = kinetic_table()
    kin = table.astype(np.float32).astype(ml_dtypes.bfloat16).astype(np.float64)
    kin = kin.reshape(5, 5, 5, 5, 5, 5)
    planes = np.zeros((3, 3, PLANE, PLANE))
    lines = np.zeros((5, 5, PLANE))
    for j in range(-1, 5):
        for l in range(-1, 5):
            for b in range(5):
                for c in range(5):
                    y, z = 4 * j + b, 4 * l + c
                    if not (0 <= y < 16 and 0 <= z < 16):
                        continue
                    at = 16 * y + z
                    for a in range(5):
                        for other in range(5):
                            if other != a:
                                lines[a, other, at] += kin[a, b, c, other, b, c]
                    for b2 in range(5):
                        for c2 in range(5):
                            y2, z2 = 4 * j + b2, 4 * l + c2
                            far_y, far_z = y2 // 16, z2 // 16
                            source = 16 * (y2 % 16) + z2 % 16
                            for kind, locals_a in enumerate(((0, 4), (1,), (2,))):
                                value = sum(kin[a, b, c, a, b2, c2] for a in locals_a)
                                if value == 0.0:
                                    continue
                                assert far_y == 0 or far_z == 0
                                part = 1 if far_y else 2 if far_z else 0
                                planes[kind, part, source, at] += value
    line_rows = np.stack(
        [lines[0, 1], lines[0, 2], lines[0, 3], 2.0 * lines[0, 4], lines[1, 2], lines[1, 3]]
    )
    bf = ml_dtypes.bfloat16
    weights = np.zeros((3 * 3 * PLANE + 16, PLANE))
    weights[: 9 * PLANE] = planes.reshape(9 * PLANE, PLANE)
    weights[9 * PLANE : 9 * PLANE + 6] = line_rows
    return weights.astype(np.float32).astype(bf), centre, half


def iota(shape, dim):
    return lax.broadcasted_iota(jnp.int32, shape, dim)


def local_node(k):
    a = (k * 41) >> 10
    rest = k - 25 * a
    b = (rest * 205) >> 10
    return a, b, rest - 5 * b


def message_kernel(v_hbm, pot_hbm, conn_hbm, out_ref, raw, conn, pot, sems):
    copies = [
        pltpu.make_async_copy(pot_hbm, raw, sems.at[0]),
        pltpu.make_async_copy(conn_hbm, conn, sems.at[1]),
        pltpu.make_async_copy(v_hbm, out_ref.at[:, :NODES_DEV], sems.at[2]),
    ]
    for copy in copies:
        copy.start()
    lane = iota((32, 128), 1)
    code = (4 * (lane >> 4) * 17 + 4 * ((lane >> 2) & 3)) * 17 + 4 * (lane & 3)
    pot[...] = jnp.zeros_like(pot)
    copies[0].wait()
    copies[1].wait()
    pot[:, :125] = raw[...]
    here = jnp.where((conn[:, 0:1] == code) & (lane < 32), lane.astype(jnp.float32), 0.0)
    cell = jnp.sum(here, axis=1, keepdims=True)
    high = pot[...].astype(jnp.bfloat16).astype(jnp.float32)
    low = pot[...] - high
    out_ref[:, NODES_DEV : NODES_DEV + 128] = jnp.where(lane == 127, cell, high).astype(jnp.bfloat16)
    out_ref[:, NODES_DEV + 128 :] = low.astype(jnp.bfloat16)
    copies[2].wait()


def pick_kind(kind):
    a, b, c = local_node(iota((1, 128), 1))
    if kind < 4:
        hit = (b == 4) == (kind >= 2), (c == 4) == (kind % 2 == 1)
    else:
        hit = (b == 4) == (kind == 5), c == 4
    return jnp.where(hit[0] & hit[1] & (iota((1, 128), 1) < 125), 1.0, 0.0)


def place_of(i, kind):
    lane = iota((1, LANES_V), 1)
    y, z = lane >> 4, lane & 15
    j = (y >> 2) - (kind // 2 if kind < 4 else kind - 4)
    l = (z >> 2) - kind % 2 if kind < 4 else jnp.where(z == 0, 3, -1)
    good = (lane < PLANE + 16) & (j >= 0) & (j < 4) & (l >= 0)
    return jnp.where(good, 16 * i + 4 * j + l, -1).astype(jnp.float32)


def fitting():
    a, b, c = local_node(iota((128, LANES_V), 0))
    lane = iota((128, LANES_V), 1)
    fits = ((b & 3) == ((lane >> 4) & 3)) & ((c & 3) == (lane & 3)) & (lane < PLANE + 16)
    return jnp.where(fits, 1.0, 0.0)


def nodal(message, kind_range, mask):
    rows, ones = [], ([], [])
    high = message[:, NODES_DEV : NODES_DEV + 128].astype(jnp.float32)
    low = message[:, NODES_DEV + 128 :].astype(jnp.float32)
    cell = high[:, 127:128]
    for kind in kind_range:
        pick = pick_kind(kind)
        rows += [high * pick, low * pick]
        for i in range(2):
            one = jnp.where(cell == place_of(i, kind), 1.0, 0.0)
            ones[i].extend([one, one])
    stack = jnp.concatenate(rows, axis=0).astype(jnp.bfloat16)
    total = jnp.zeros((8, LANES_V), jnp.float32)
    k = iota((8, 128), 1)
    along = local_node(k)[0]
    for i in range(2):
        placed = jnp.concatenate(ones[i], axis=0).astype(jnp.bfloat16)
        values = lax.dot_general(
            stack, placed, (((0,), (0,)), ((), ())), preferred_element_type=jnp.float32
        )
        values = values * mask
        high = values.astype(jnp.bfloat16)
        low = (values - high.astype(jnp.float32)).astype(jnp.bfloat16)
        to_x = jnp.where((((4 * i + along) & 7) == iota((8, 128), 0)) & (k < 125), 1.0, 0.0)
        to_x = to_x.astype(jnp.bfloat16)
        total += jnp.dot(to_x, high, preferred_element_type=jnp.float32)
        total += jnp.dot(to_x, low, preferred_element_type=jnp.float32)
    return total


def own_kernel(c_ref, v_ref, own_ref, edge_ref, mask_ref):
    v_ref[...] = c_ref[:, :NODES_DEV]
    mask = fitting()
    mask_ref[...] = mask
    own_ref[...] = nodal(c_ref, range(4), mask)
    edge_ref[...] = nodal(c_ref, range(4, 6), mask)


def pack_kernel(l_ref, r_ref, c_ref, own_ref, edge_ref, mask_ref, out_ref, ghost):
    even = iota((32, PLANE), 0) % 2 == 0
    mask = mask_ref[...]
    for s, message in enumerate((l_ref, c_ref, r_ref)):
        out_ref[:, NODES_DEV * s : NODES_DEV * (s + 1)] = message[:, :NODES_DEV]
    own = own_ref[...] + nodal(l_ref, range(4, 6), mask)
    left = nodal(l_ref, range(4), mask)
    right = nodal(r_ref, range(4), mask) + edge_ref[...]
    high = own.astype(jnp.bfloat16).astype(jnp.float32)
    for part, (first, second) in enumerate(((high, own - high), (left, right))):
        for x in range(NXL):
            main = jnp.where(even, first[x : x + 1, :PLANE], second[x : x + 1, :PLANE])
            at = V_AT + NODES_DEV * part + PLANE * x
            out_ref[:, at : at + PLANE] = main.astype(jnp.bfloat16)
            edge = jnp.where(even[:, :128], first[x : x + 1, PLANE:], second[x : x + 1, PLANE:])
            ghost[:, 16 * x : 16 * (x + 1)] = edge[:, :16]
        at = G_AT + 128 * part
        out_ref[:, at : at + 128] = ghost[...].astype(jnp.bfloat16)


def diagonal(got, g_ref, centre):
    lane, row = iota((128, NXL * 128), 1), iota((128, NXL * 128), 0)
    spread = jnp.where(((row >> 4) == (lane >> 7)) & ((row & 15) == (lane & 127)), 1.0, 0.0)
    spread = spread.astype(jnp.bfloat16)
    lane, row = iota((32, 64), 1), iota((32, 64), 0)
    source = jnp.where(lane < 32, row >> 1, ((row >> 1) + 15) & 15)
    same = source == ((lane & 31) >> 1)
    pairs = [
        jnp.where(same & good, 1.0, 0.0).astype(jnp.bfloat16)
        for good in ((lane & 1) == 0, lane >= 0, (lane & 1) == 1)
    ]
    edges = []
    for part in range(2):
        at = G_AT + 128 * part
        edge = jnp.dot(got[:, at : at + 128], spread, preferred_element_type=jnp.float32)
        edges.append(edge.astype(jnp.bfloat16))
    for s in range(3):
        part = 0 if s == 1 else 1
        for x in range(NXL):
            at = V_AT + NODES_DEV * part + PLANE * x
            stack = jnp.concatenate([got[:, at : at + 128], edges[part][:, 128 * x : 128 * (x + 1)]], axis=0)
            g_ref[x, s, :, :128] = jnp.dot(pairs[s], stack, preferred_element_type=jnp.float32) - centre
            g_ref[x, s, :, 128:] = (
                jnp.dot(pairs[s][:, :32], got[:, at + 128 : at + PLANE], preferred_element_type=jnp.float32)
                - centre
            )


def filter_step(slabs, w_ref, g_ref, out_ref, cur, prev, acc, half, ready):
    place = {x: at for at, x in enumerate(X_ORDER)}
    right_lanes = lax.broadcasted_iota(jnp.int32, (32, PLANE), 1) % 16 < 8
    for s, slab in enumerate(slabs):
        for x in range(NXL):
            block = slab[:, PLANE * x : PLANE * (x + 1)]
            cur[place[x], s, :, :PLANE] = block
            turn(cur, place[x], s, 0, block[:, :128].astype(jnp.float32))
            turn(cur, place[x], s, 1, block[:, 128:].astype(jnp.float32))
    prev[...] = jnp.zeros_like(prev)
    ready()
    lines = w_ref[9 * PLANE :, :].astype(jnp.float32)

    def weight(kind):
        return w_ref[3 * PLANE * kind : 3 * PLANE * (kind + 1), :]

    def sides():
        for at in range(NXL):
            left, middle, right = (cur[at, s, :, :PLANE].astype(jnp.float32) for s in range(3))
            zero = jnp.zeros_like(left)
            cur[at, 0, :, 2 * PLANE :] = jnp.where(right_lanes, middle, zero).astype(jnp.bfloat16)
            cur[at, 1, :, 2 * PLANE :] = jnp.where(right_lanes, right, left).astype(jnp.bfloat16)
            cur[at, 2, :, 2 * PLANE :] = jnp.where(right_lanes, zero, middle).astype(jnp.bfloat16)

    def apply(which, alpha, beta, store):
        first, last = which[0], which[-1] + 1
        for kind, (low, high) in enumerate(CLASS_ROWS):
            rows = cur[low:high, first:last]
            count = (high - low) * (last - first) * 32
            result = jnp.dot(
                rows.reshape(count, 3 * PLANE), weight(kind), preferred_element_type=jnp.float32
            )
            acc[low:high, first:last] = result.reshape(high - low, last - first, 32, PLANE)
        for s in which:
            for part in range(2):
                lanes = slice(128 * part, 128 * (part + 1))
                v = [cur[place[x], s, :, lanes].astype(jnp.float32) for x in range(NXL)]
                c01, c02, c03, c04, c12, c13 = (lines[row : row + 1, lanes] for row in range(6))
                s17, s26, s35 = v[1] + v[7], v[2] + v[6], v[3] + v[5]
                s04 = c02 * (v[0] + v[4])
                extra = {
                    0: c01 * s17 + c02 * s26 + c03 * s35 + c04 * v[4],
                    4: c01 * s35 + c02 * s26 + c03 * s17 + c04 * v[0],
                    1: c01 * v[0] + c12 * v[2] + c13 * v[3] + c03 * v[4],
                    3: c01 * v[4] + c12 * v[2] + c13 * v[1] + c03 * v[0],
                    5: c01 * v[4] + c12 * v[6] + c13 * v[7] + c03 * v[0],
                    7: c01 * v[0] + c12 * v[6] + c13 * v[5] + c03 * v[4],
                    2: s04 + c12 * (v[1] + v[3]),
                    6: s04 + c12 * (v[5] + v[7]),
                }
                for x in range(NXL):
                    at = place[x]
                    applied = acc[at, s, :, lanes] + extra[x] + g_ref[x, s, :, lanes] * v[x]
                    store(x, at, s, part, alpha * applied - beta * prev[at, s, :, lanes].astype(jnp.float32))

    def keep(x, at, s, part, new):
        lanes = slice(128 * part, 128 * (part + 1))
        prev[at, s, :, lanes] = cur[at, s, :, lanes]
        new = new.astype(jnp.bfloat16)
        cur[at, s, :, lanes] = new
        turn(cur, at, s, part, new.astype(jnp.float32))

    def emit(x, at, s, part, new):
        out_ref[:, PLANE * x + 128 * part : PLANE * x + 128 * (part + 1)] = new.astype(jnp.bfloat16)

    def order(k, carry):
        sides()
        alpha = jnp.where(k == 0, jnp.float32(1.0 / half), jnp.float32(2.0 / half))
        beta = jnp.where(k == 0, jnp.float32(0.0), jnp.float32(1.0))
        apply((0, 1, 2), alpha, beta, keep)
        return carry

    lax.fori_loop(0, DEGREE - 1, order, 0)
    sides()
    apply((1,), jnp.float32(2.0 / half), jnp.float32(1.0), emit)


def turn(cur, at, s, part, value):
    shift = 30 if part == 0 else 2
    lanes = slice(PLANE + 128 * part, PLANE + 128 * (part + 1))
    cur[at, s, :, lanes] = pltpu.roll(value, shift, 0).astype(jnp.bfloat16)


def first_kernel(centre, half, got, w_hbm, out_ref, g_ref, cur, prev, acc, w_ref, sem):
    copy = pltpu.make_async_copy(w_hbm, w_ref, sem)
    copy.start()
    diagonal(got, g_ref, centre)
    slabs = [got.at[:, NODES_DEV * s : NODES_DEV * (s + 1)] for s in range(3)]
    filter_step(slabs, w_ref, g_ref, out_ref, cur, prev, acc, half, copy.wait)


def later_kernel(half, c_ref, l_ref, r_ref, g_ref, st_ref, w_hbm, out_ref, cur, prev, acc, w_ref, sem):
    copy = pltpu.make_async_copy(w_hbm, w_ref, sem)
    copy.start()
    out_ref[:, NODES_DEV:] = st_ref[...]
    filter_step((l_ref, c_ref, r_ref), w_ref, g_ref, out_ref, cur, prev, acc, half, copy.wait)


def corr_kernel(factor, got, out_ref):
    four = jnp.concatenate([got[:, :NODES_DEV]] * 4, axis=0)
    parts = [
        lax.dot_general(
            got[:, NODES_DEV * (1 + part) : NODES_DEV * (2 + part)],
            four,
            (((1,), (1,)), ((), ())),
            preferred_element_type=jnp.float32,
        )
        for part in range(2)
    ]
    lane, row = iota((NWF, 128), 1), iota((NWF, 128), 0)
    both = jnp.where(((lane >> 5) & 1) == 0, parts[0], parts[1])
    out_ref[...] = jnp.where((lane >> 6) == (row & 1), both * factor, 0.0)


def share_kernel(got, out_ref):
    total = jnp.sum(got[...], axis=0, keepdims=True)
    out_ref[...] = jnp.where((iota((NWF, 128), 1) & 31) == iota((NWF, 128), 0), total, 0.0)


def total_kernel(got, out_ref):
    total = jnp.sum(got[...], axis=0, keepdims=True)
    lane = iota((1, 128), 1)
    rows = jnp.zeros((1, 128), jnp.float32)
    for row in range(4):
        mine = jnp.where((lane >> 5) == row // 2 + 2 * (row % 2), total, 0.0)
        rows = jnp.where(lane == row, jnp.sum(mine, axis=1, keepdims=True), rows)
    out_ref[...] = rows[:, :4]


def full(shape):
    return pl.BlockSpec(shape, lambda *_: (0,) * len(shape))


def call(kernel, args, outs, scratch=(), far=(), limit=VMEM):
    hbm = pl.BlockSpec(memory_space=pltpu.HBM)
    return pl.pallas_call(
        kernel,
        grid=(1,),
        in_specs=[full(a.shape) for a in args] + [hbm] * len(far),
        out_specs=[full(o.shape) for o in outs],
        out_shape=list(outs),
        scratch_shapes=list(scratch),
        compiler_params=pltpu.CompilerParams(vmem_limit_bytes=limit),
    )(*args, *far)


def passed_along(block, axis, distance):
    devices = range(lax.axis_size(axis))
    route = [((i - distance) % len(devices), i) for i in devices]
    return lax.ppermute(block, axis, route)


def shards(cur_block, stored_blocks, cell_potential, connectivity):
    weights, centre, half = tables()
    weights = jnp.asarray(weights)
    bf, f32 = jnp.bfloat16, jnp.float32
    shape = jax.ShapeDtypeStruct
    n_cells, n_bands = lax.axis_size("cells"), lax.axis_size("bands")
    stored = stored_blocks.reshape(2, 2, n_bands, NODES_DEV).transpose(2, 1, 0, 3).reshape(NWF, 2 * NODES_DEV)
    dma = pltpu.SemaphoreType.DMA
    (message,) = call(
        message_kernel,
        (),
        [shape((NWF, MESSAGE), bf)],
        [
            pltpu.VMEM((32, 125), f32),
            pltpu.VMEM((32, 125), jnp.int32),
            pltpu.VMEM((32, 128), f32),
            dma((3,)),
        ],
        (cur_block, cell_potential.T, connectivity.T),
        62 * 1024 * 1024,
    )
    left = passed_along(message, "cells", 1)
    right = passed_along(message, "cells", -1)
    shapes = [shape((8, LANES_V), f32), shape((8, LANES_V), f32), shape((128, LANES_V), f32)]
    own = call(own_kernel, (message,), [shape((NWF, NODES_DEV), bf)] + shapes)
    (payload,) = call(
        pack_kernel,
        (left, right, *own),
        [shape((NWF, PAYLOAD), bf)],
        [pltpu.VMEM((32, 128), f32)],
    )
    got = lax.all_to_all(payload, "bands", 0, 0, tiled=True)
    scratch = [
        pltpu.VMEM((NXL, 3, NWF, 3 * PLANE), bf),
        pltpu.VMEM((NXL, 3, NWF, PLANE), bf),
        pltpu.VMEM((NXL, 3, NWF, PLANE), f32),
        pltpu.VMEM(weights.shape, bf),
    ]
    block, diag = call(
        functools.partial(first_kernel, centre, half),
        (got,),
        [shape((NWF, NODES_DEV), bf), shape((NXL, 3, NWF, PLANE), f32)],
        scratch + [dma],
        (weights,),
    )
    left = passed_along(block, "cells", 1)
    right = passed_along(block, "cells", -1)
    factor = 1.0 / math.sqrt(NODES_DEV * n_cells * n_bands)
    (block,) = call(
        functools.partial(later_kernel, half),
        (block, left, right, diag, stored),
        [shape((NWF, 3 * NODES_DEV), bf)],
        scratch + [dma],
        (weights,),
    )
    got = lax.all_to_all(block, "bands", 0, 0, tiled=True)
    filtered = got[:, :NODES_DEV]
    (partial,) = call(functools.partial(corr_kernel, factor), (got,), [shape((NWF, 128), f32)])
    partial = lax.all_to_all(partial, "bands", 0, 0, tiled=True)
    (partial,) = call(share_kernel, (partial,), [shape((NWF, 128), f32)])
    partial = lax.all_to_all(partial, "cells", 0, 0, tiled=True)
    (total,) = call(total_kernel, (partial,), [shape((1, 4), f32)])
    return (filtered, total.T)


def solution(mesh):
    in_specs = (
        P(None, ("cells", "bands")),
        P("bands", "cells"),
        P(None, ("cells", "bands")),
        P(None, ("cells", "bands")),
    )
    out_specs = (P(None, ("cells", "bands")), P("bands", "cells"))
    return jax.shard_map(shards, mesh=mesh, in_specs=in_specs, out_specs=out_specs, check_vma=False)
```

```python
import functools
import math

import jax
import jax.numpy as jnp
import ml_dtypes
import numpy as np
from jax import lax
from jax.experimental import pallas as pl
from jax.experimental.pallas import tpu as pltpu
from jax.sharding import PartitionSpec as P

NWF = 32
DEGREE = 4
STEPS = 2
NXL = 8
NODES_DEV = 2048
PLANE = 256
LANES_V = 384
MESSAGE = NODES_DEV + 256
V_AT = 3 * NODES_DEV
G_AT = 5 * NODES_DEV
PAYLOAD = G_AT + 2 * 128
X_ORDER = (0, 4, 1, 3, 5, 7, 2, 6)
CLASS_ROWS = ((0, 2), (2, 6), (6, 8))
VMEM = 48 * 1024 * 1024


def kinetic_table():
    points = [-1.0, -math.sqrt(3.0 / 7.0), 0.0, math.sqrt(3.0 / 7.0), 1.0]
    weights = [0.1, 49.0 / 90.0, 32.0 / 45.0, 49.0 / 90.0, 0.1]
    scales = []
    for row in range(5):
        prod_val = 1.0
        for other in range(5):
            if other != row:
                prod_val = prod_val * (points[row] - points[other])
        scales.append(prod_val)
    deriv = [[0.0] * 5 for row in range(5)]
    for row in range(5):
        for col in range(5):
            if row != col:
                deriv[row][col] = scales[row] / scales[col] / (points[row] - points[col])
            else:
                total = 0.0
                for other in range(5):
                    if other != row:
                        total = total + 1.0 / (points[row] - points[other])
                deriv[row][col] = total
    stiff_one = [
        [sum((deriv[i][a] * weights[i] * deriv[i][b] for i in range(5))) for b in range(5)]
        for a in range(5)
    ]
    mass_one = [[weights[a] if a == b else 0.0 for b in range(5)] for a in range(5)]
    table = [[0.0] * 125 for row in range(125)]
    for k in range(125):
        ka, kb, kc = (k // 25, k // 5 % 5, k % 5)
        for j in range(125):
            ja, jb, jc = (j // 25, j // 5 % 5, j % 5)
            table[k][j] = 0.5 * (
                stiff_one[ka][ja] * mass_one[kb][jb] * mass_one[kc][jc]
                + mass_one[ka][ja] * stiff_one[kb][jb] * mass_one[kc][jc]
                + mass_one[ka][ja] * mass_one[kb][jb] * stiff_one[kc][jc]
            )
    assembled = [dict() for row in range(512)]
    for cell_x in range(2):
        for cell_y in range(2):
            for cell_z in range(2):
                global_ids = []
                for k in range(125):
                    node_x = (4 * cell_x + k // 25) % 8
                    node_y = (4 * cell_y + k // 5 % 5) % 8
                    node_z = (4 * cell_z + k % 5) % 8
                    global_ids.append((node_x * 8 + node_y) * 8 + node_z)
                for k in range(125):
                    row_map = assembled[global_ids[k]]
                    for j in range(125):
                        target = global_ids[j]
                        row_map[target] = row_map.get(target, 0.0) + table[k][j]
    largest = 0.0
    for row_map in assembled:
        total = sum((abs(value) for value in row_map.values()))
        largest = max(largest, total)
    bound = largest + 8.0 * 2.0
    return (np.array(table), float(0.55 * bound), float(0.45 * bound))


@functools.lru_cache(maxsize=None)
def tables():
    table, centre, half = kinetic_table()
    kin = table.astype(np.float32).astype(ml_dtypes.bfloat16).astype(np.float64)
    kin = kin.reshape(5, 5, 5, 5, 5, 5)
    planes = np.zeros((3, 3, PLANE, PLANE))
    lines = np.zeros((5, 5, PLANE))
    for j in range(-1, 5):
        for l in range(-1, 5):
            for b in range(5):
                for c in range(5):
                    y, z = 4 * j + b, 4 * l + c
                    if not (0 <= y < 16 and 0 <= z < 16):
                        continue
                    at = 16 * y + z
                    for a in range(5):
                        for other in range(5):
                            if other != a:
                                lines[a, other, at] += kin[a, b, c, other, b, c]
                    for b2 in range(5):
                        for c2 in range(5):
                            y2, z2 = 4 * j + b2, 4 * l + c2
                            far_y, far_z = y2 // 16, z2 // 16
                            source = 16 * (y2 % 16) + z2 % 16
                            for kind, locals_a in enumerate(((0, 4), (1,), (2,))):
                                value = sum(kin[a, b, c, a, b2, c2] for a in locals_a)
                                if value == 0.0:
                                    continue
                                assert far_y == 0 or far_z == 0
                                part = 1 if far_y else 2 if far_z else 0
                                planes[kind, part, source, at] += value
    line_rows = np.stack(
        [lines[0, 1], lines[0, 2], lines[0, 3], 2.0 * lines[0, 4], lines[1, 2], lines[1, 3]]
    )
    bf = ml_dtypes.bfloat16
    weights = np.zeros((3 * 3 * PLANE + 16, PLANE))
    weights[: 9 * PLANE] = planes.reshape(9 * PLANE, PLANE)
    weights[9 * PLANE : 9 * PLANE + 6] = line_rows
    return weights.astype(np.float32).astype(bf), centre, half


def iota(shape, dim):
    return lax.broadcasted_iota(jnp.int32, shape, dim)


def local_node(k):
    a = (k * 41) >> 10
    rest = k - 25 * a
    b = (rest * 205) >> 10
    return a, b, rest - 5 * b


def message_kernel(v_hbm, pot_hbm, conn_hbm, out_ref, raw, conn, pot, sems):
    copies = [
        pltpu.make_async_copy(pot_hbm, raw, sems.at[0]),
        pltpu.make_async_copy(conn_hbm, conn, sems.at[1]),
        pltpu.make_async_copy(v_hbm, out_ref.at[:, :NODES_DEV], sems.at[2]),
    ]
    for copy in copies:
        copy.start()
    lane = iota((32, 128), 1)
    code = (4 * (lane >> 4) * 17 + 4 * ((lane >> 2) & 3)) * 17 + 4 * (lane & 3)
    pot[...] = jnp.zeros_like(pot)
    copies[0].wait()
    copies[1].wait()
    pot[:, :125] = raw[...]
    here = jnp.where((conn[:, 0:1] == code) & (lane < 32), lane.astype(jnp.float32), 0.0)
    cell = jnp.sum(here, axis=1, keepdims=True)
    high = pot[...].astype(jnp.bfloat16).astype(jnp.float32)
    low = pot[...] - high
    out_ref[:, NODES_DEV : NODES_DEV + 128] = jnp.where(lane == 127, cell, high).astype(jnp.bfloat16)
    out_ref[:, NODES_DEV + 128 :] = low.astype(jnp.bfloat16)
    copies[2].wait()


def pick_kind(kind):
    a, b, c = local_node(iota((1, 128), 1))
    if kind < 4:
        hit = (b == 4) == (kind >= 2), (c == 4) == (kind % 2 == 1)
    else:
        hit = (b == 4) == (kind == 5), c == 4
    return jnp.where(hit[0] & hit[1] & (iota((1, 128), 1) < 125), 1.0, 0.0)


def place_of(i, kind):
    lane = iota((1, LANES_V), 1)
    y, z = lane >> 4, lane & 15
    j = (y >> 2) - (kind // 2 if kind < 4 else kind - 4)
    l = (z >> 2) - kind % 2 if kind < 4 else jnp.where(z == 0, 3, -1)
    good = (lane < PLANE + 16) & (j >= 0) & (j < 4) & (l >= 0)
    return jnp.where(good, 16 * i + 4 * j + l, -1).astype(jnp.float32)


def fitting():
    a, b, c = local_node(iota((128, LANES_V), 0))
    lane = iota((128, LANES_V), 1)
    fits = ((b & 3) == ((lane >> 4) & 3)) & ((c & 3) == (lane & 3)) & (lane < PLANE + 16)
    return jnp.where(fits, 1.0, 0.0)


def nodal(message, kind_range, mask, exact):
    rows, ones = [], ([], [])
    parts = [message[:, NODES_DEV : NODES_DEV + 128].astype(jnp.float32)]
    cell = parts[0][:, 127:128]
    if exact:
        parts.append(message[:, NODES_DEV + 128 :].astype(jnp.float32))
    for kind in kind_range:
        pick = pick_kind(kind)
        rows += [part * pick for part in parts]
        for i in range(2):
            one = jnp.where(cell == place_of(i, kind), 1.0, 0.0)
            ones[i].extend([one] * len(parts))
    stack = jnp.concatenate(rows, axis=0).astype(jnp.bfloat16)
    placed = jnp.concatenate([jnp.concatenate(one, axis=0) for one in ones], axis=1)
    both = lax.dot_general(
        stack, placed.astype(jnp.bfloat16), (((0,), (0,)), ((), ())), preferred_element_type=jnp.float32
    )
    total = jnp.zeros((8, LANES_V), jnp.float32)
    k = iota((8, 128), 1)
    along = local_node(k)[0]
    for i in range(2):
        values = both[:, LANES_V * i : LANES_V * (i + 1)] * mask
        high = values.astype(jnp.bfloat16)
        to_x = jnp.where((((4 * i + along) & 7) == iota((8, 128), 0)) & (k < 125), 1.0, 0.0)
        to_x = to_x.astype(jnp.bfloat16)
        total += jnp.dot(to_x, high, preferred_element_type=jnp.float32)
        if exact:
            low = (values - high.astype(jnp.float32)).astype(jnp.bfloat16)
            total += jnp.dot(to_x, low, preferred_element_type=jnp.float32)
    return total


def own_kernel(c_ref, v_ref, own_ref, edge_ref, mask_ref):
    v_ref[...] = c_ref[:, :NODES_DEV]
    mask = fitting()
    mask_ref[...] = mask
    own_ref[...] = nodal(c_ref, range(4), mask, True)
    edge_ref[...] = nodal(c_ref, range(4, 6), mask, True)


def pack_kernel(l_ref, r_ref, c_ref, own_ref, edge_ref, mask_ref, out_ref, ghost):
    even = iota((32, PLANE), 0) % 2 == 0
    mask = mask_ref[...]
    for s, message in enumerate((l_ref, c_ref, r_ref)):
        out_ref[:, NODES_DEV * s : NODES_DEV * (s + 1)] = message[:, :NODES_DEV]
    own = own_ref[...] + nodal(l_ref, range(4, 6), mask, True)
    left = nodal(l_ref, range(4), mask, False)
    right = nodal(r_ref, range(4), mask, False) + edge_ref[...]
    high = own.astype(jnp.bfloat16).astype(jnp.float32)
    for part, (first, second) in enumerate(((high, own - high), (left, right))):
        for x in range(NXL):
            main = jnp.where(even, first[x : x + 1, :PLANE], second[x : x + 1, :PLANE])
            at = V_AT + NODES_DEV * part + PLANE * x
            out_ref[:, at : at + PLANE] = main.astype(jnp.bfloat16)
            edge = jnp.where(even[:, :128], first[x : x + 1, PLANE:], second[x : x + 1, PLANE:])
            ghost[:, 16 * x : 16 * (x + 1)] = edge[:, :16]
        at = G_AT + 128 * part
        out_ref[:, at : at + 128] = ghost[...].astype(jnp.bfloat16)


def diagonal(got, g_ref, centre):
    lane, row = iota((128, NXL * 128), 1), iota((128, NXL * 128), 0)
    spread = jnp.where(((row >> 4) == (lane >> 7)) & ((row & 15) == (lane & 127)), 1.0, 0.0)
    spread = spread.astype(jnp.bfloat16)
    lane, row = iota((32, 64), 1), iota((32, 64), 0)
    source = jnp.where(lane < 32, row >> 1, ((row >> 1) + 15) & 15)
    same = source == ((lane & 31) >> 1)
    pairs = [
        jnp.where(same & good, 1.0, 0.0).astype(jnp.bfloat16)
        for good in ((lane & 1) == 0, lane >= 0, (lane & 1) == 1)
    ]
    edges = []
    for part in range(2):
        at = G_AT + 128 * part
        edge = jnp.dot(got[:, at : at + 128], spread, preferred_element_type=jnp.float32)
        edges.append(edge.astype(jnp.bfloat16))
    for s in range(3):
        part = 0 if s == 1 else 1
        for x in range(NXL):
            at = V_AT + NODES_DEV * part + PLANE * x
            stack = jnp.concatenate([got[:, at : at + 128], edges[part][:, 128 * x : 128 * (x + 1)]], axis=0)
            g_ref[x, s, :, :128] = jnp.dot(pairs[s], stack, preferred_element_type=jnp.float32) - centre
            g_ref[x, s, :, 128:] = (
                jnp.dot(pairs[s][:, :32], got[:, at + 128 : at + PLANE], preferred_element_type=jnp.float32)
                - centre
            )


def filter_step(slabs, w_ref, g_ref, out_ref, cur, prev, acc, half):
    place = {x: at for at, x in enumerate(X_ORDER)}
    right_lanes = lax.broadcasted_iota(jnp.int32, (32, PLANE), 1) % 16 < 8
    for s, slab in enumerate(slabs):
        for x in range(NXL):
            block = slab[:, PLANE * x : PLANE * (x + 1)]
            cur[place[x], s, :, :PLANE] = block
            turn(cur, place[x], s, 0, block[:, :128].astype(jnp.float32))
            turn(cur, place[x], s, 1, block[:, 128:].astype(jnp.float32))
    prev[...] = jnp.zeros_like(prev)
    lines = w_ref[9 * PLANE :, :].astype(jnp.float32)

    def weight(kind):
        return w_ref[3 * PLANE * kind : 3 * PLANE * (kind + 1), :]

    def sides():
        for at in range(NXL):
            left, middle, right = (cur[at, s, :, :PLANE].astype(jnp.float32) for s in range(3))
            zero = jnp.zeros_like(left)
            cur[at, 0, :, 2 * PLANE :] = jnp.where(right_lanes, middle, zero).astype(jnp.bfloat16)
            cur[at, 1, :, 2 * PLANE :] = jnp.where(right_lanes, right, left).astype(jnp.bfloat16)
            cur[at, 2, :, 2 * PLANE :] = jnp.where(right_lanes, zero, middle).astype(jnp.bfloat16)

    def merge():
        def pick(ref, at, lanes):
            left, right = (ref[at, s, :, lanes].astype(jnp.float32) for s in (0, 2))
            ref[at, 2, :, lanes] = jnp.where(right_lanes, right, left).astype(jnp.bfloat16)

        for at in range(NXL):
            pick(cur, at, slice(0, PLANE))
            pick(cur, at, slice(PLANE, 2 * PLANE))
            pick(prev, at, slice(0, PLANE))
            cur[at, 2, :, 2 * PLANE :] = cur[at, 1, :, :PLANE]
            cur[at, 1, :, 2 * PLANE :] = cur[at, 2, :, :PLANE]

    def apply(which, alpha, beta, store):
        first, last = which[0], which[-1] + 1
        for kind, (low, high) in enumerate(CLASS_ROWS):
            rows = cur[low:high, first:last]
            count = (high - low) * (last - first) * 32
            result = jnp.dot(
                rows.reshape(count, 3 * PLANE), weight(kind), preferred_element_type=jnp.float32
            )
            acc[low:high, first:last] = result.reshape(high - low, last - first, 32, PLANE)
        for s in which:
            for part in range(2):
                lanes = slice(128 * part, 128 * (part + 1))
                v = [cur[place[x], s, :, lanes].astype(jnp.float32) for x in range(NXL)]
                c01, c02, c03, c04, c12, c13 = (lines[row : row + 1, lanes] for row in range(6))
                s17, s26, s35 = v[1] + v[7], v[2] + v[6], v[3] + v[5]
                s04 = c02 * (v[0] + v[4])
                extra = {
                    0: c01 * s17 + c02 * s26 + c03 * s35 + c04 * v[4],
                    4: c01 * s35 + c02 * s26 + c03 * s17 + c04 * v[0],
                    1: c01 * v[0] + c12 * v[2] + c13 * v[3] + c03 * v[4],
                    3: c01 * v[4] + c12 * v[2] + c13 * v[1] + c03 * v[0],
                    5: c01 * v[4] + c12 * v[6] + c13 * v[7] + c03 * v[0],
                    7: c01 * v[0] + c12 * v[6] + c13 * v[5] + c03 * v[4],
                    2: s04 + c12 * (v[1] + v[3]),
                    6: s04 + c12 * (v[5] + v[7]),
                }
                for x in range(NXL):
                    at = place[x]
                    diag = g_ref[x, s, :, lanes]
                    if which == (1, 2) and s == 2:
                        diag = jnp.where(right_lanes[:, :128], diag, g_ref[x, 0, :, lanes])
                    applied = acc[at, s, :, lanes] + extra[x] + diag * v[x]
                    store(x, at, s, part, alpha * applied - beta * prev[at, s, :, lanes].astype(jnp.float32))

    def keep(x, at, s, part, new):
        lanes = slice(128 * part, 128 * (part + 1))
        prev[at, s, :, lanes] = cur[at, s, :, lanes]
        new = new.astype(jnp.bfloat16)
        cur[at, s, :, lanes] = new
        turn(cur, at, s, part, new.astype(jnp.float32))

    def emit(x, at, s, part, new):
        out_ref[:, PLANE * x + 128 * part : PLANE * x + 128 * (part + 1)] = new.astype(jnp.bfloat16)

    def order(k, carry):
        sides()
        alpha = jnp.where(k == 0, jnp.float32(1.0 / half), jnp.float32(2.0 / half))
        beta = jnp.where(k == 0, jnp.float32(0.0), jnp.float32(1.0))
        apply((0, 1, 2), alpha, beta, keep)
        return carry

    lax.fori_loop(0, DEGREE - 2, order, 0)
    merge()
    two = jnp.float32(2.0 / half), jnp.float32(1.0)
    apply((1, 2), *two, keep)
    for at in range(NXL):
        cur[at, 1, :, 2 * PLANE :] = cur[at, 2, :, :PLANE]
    apply((1,), *two, emit)


def turn(cur, at, s, part, value):
    shift = 30 if part == 0 else 2
    lanes = slice(PLANE + 128 * part, PLANE + 128 * (part + 1))
    cur[at, s, :, lanes] = pltpu.roll(value, shift, 0).astype(jnp.bfloat16)


def first_kernel(centre, half, got, w_ref, out_ref, g_ref, cur, prev, acc):
    diagonal(got, g_ref, centre)
    slabs = [got.at[:, NODES_DEV * s : NODES_DEV * (s + 1)] for s in range(3)]
    filter_step(slabs, w_ref, g_ref, out_ref, cur, prev, acc, half)


def later_kernel(half, c_ref, l_ref, r_ref, g_ref, st_ref, w_ref, out_ref, cur, prev, acc):
    out_ref[:, NODES_DEV:] = st_ref[...]
    filter_step((l_ref, c_ref, r_ref), w_ref, g_ref, out_ref, cur, prev, acc, half)


def corr_kernel(factor, got, out_ref):
    four = jnp.concatenate([got[:, :NODES_DEV]] * 4, axis=0)
    parts = [
        lax.dot_general(
            got[:, NODES_DEV * (1 + part) : NODES_DEV * (2 + part)],
            four,
            (((1,), (1,)), ((), ())),
            preferred_element_type=jnp.float32,
        )
        for part in range(2)
    ]
    lane, row = iota((NWF, 128), 1), iota((NWF, 128), 0)
    both = jnp.where(((lane >> 5) & 1) == 0, parts[0], parts[1])
    out_ref[...] = jnp.where((lane >> 6) == (row & 1), both * factor, 0.0)


def share_kernel(got, out_ref):
    total = jnp.sum(got[...], axis=0, keepdims=True)
    out_ref[...] = jnp.where((iota((NWF, 128), 1) & 31) == iota((NWF, 128), 0), total, 0.0)


def total_kernel(got, out_ref):
    total = jnp.sum(got[...], axis=0, keepdims=True)
    lane = iota((1, 128), 1)
    rows = jnp.zeros((1, 128), jnp.float32)
    for row in range(4):
        mine = jnp.where((lane >> 5) == row // 2 + 2 * (row % 2), total, 0.0)
        rows = jnp.where(lane == row, jnp.sum(mine, axis=1, keepdims=True), rows)
    out_ref[...] = rows[:, :4]


def full(shape):
    return pl.BlockSpec(shape, lambda *_: (0,) * len(shape))


def call(kernel, args, outs, scratch=(), far=(), limit=VMEM):
    hbm = pl.BlockSpec(memory_space=pltpu.HBM)
    return pl.pallas_call(
        kernel,
        grid=(1,),
        in_specs=[full(a.shape) for a in args] + [hbm] * len(far),
        out_specs=[full(o.shape) for o in outs],
        out_shape=list(outs),
        scratch_shapes=list(scratch),
        compiler_params=pltpu.CompilerParams(vmem_limit_bytes=limit),
    )(*args, *far)


def passed_along(block, axis, distance):
    devices = range(lax.axis_size(axis))
    route = [((i - distance) % len(devices), i) for i in devices]
    return lax.ppermute(block, axis, route)


def shards(cur_block, stored_blocks, cell_potential, connectivity):
    weights, centre, half = tables()
    weights = jnp.asarray(weights)
    bf, f32 = jnp.bfloat16, jnp.float32
    shape = jax.ShapeDtypeStruct
    n_cells, n_bands = lax.axis_size("cells"), lax.axis_size("bands")
    stored = stored_blocks.reshape(2, 2, n_bands, NODES_DEV).transpose(2, 1, 0, 3).reshape(NWF, 2 * NODES_DEV)
    dma = pltpu.SemaphoreType.DMA
    (message,) = call(
        message_kernel,
        (),
        [shape((NWF, MESSAGE), bf)],
        [
            pltpu.VMEM((32, 125), f32),
            pltpu.VMEM((32, 125), jnp.int32),
            pltpu.VMEM((32, 128), f32),
            dma((3,)),
        ],
        (cur_block, cell_potential.T, connectivity.T),
        62 * 1024 * 1024,
    )
    left = passed_along(message, "cells", 1)
    right = passed_along(message, "cells", -1)
    shapes = [shape((8, LANES_V), f32), shape((8, LANES_V), f32), shape((128, LANES_V), f32)]
    own = call(own_kernel, (message,), [shape((NWF, NODES_DEV), bf)] + shapes)
    (payload,) = call(
        pack_kernel,
        (left, right, *own),
        [shape((NWF, PAYLOAD), bf)],
        [pltpu.VMEM((32, 128), f32)],
    )
    got = lax.all_to_all(payload, "bands", 0, 0, tiled=True)
    scratch = [
        pltpu.VMEM((NXL, 3, NWF, 3 * PLANE), bf),
        pltpu.VMEM((NXL, 3, NWF, PLANE), bf),
        pltpu.VMEM((NXL, 3, NWF, PLANE), f32),
    ]
    block, diag = call(
        functools.partial(first_kernel, centre, half),
        (got, weights),
        [shape((NWF, NODES_DEV), bf), shape((NXL, 3, NWF, PLANE), f32)],
        scratch,
    )
    left = passed_along(block, "cells", 1)
    right = passed_along(block, "cells", -1)
    factor = 1.0 / math.sqrt(NODES_DEV * n_cells * n_bands)
    (block,) = call(
        functools.partial(later_kernel, half),
        (block, left, right, diag, stored, weights),
        [shape((NWF, 3 * NODES_DEV), bf)],
        scratch,
    )
    got = lax.all_to_all(block, "bands", 0, 0, tiled=True)
    filtered = got[:, :NODES_DEV]
    (partial,) = call(functools.partial(corr_kernel, factor), (got,), [shape((NWF, 128), f32)])
    partial = lax.all_to_all(partial, "bands", 0, 0, tiled=True)
    (partial,) = call(share_kernel, (partial,), [shape((NWF, 128), f32)])
    partial = lax.all_to_all(partial, "cells", 0, 0, tiled=True)
    (total,) = call(total_kernel, (partial,), [shape((1, 4), f32)])
    return (filtered, total.T)


def solution(mesh):
    in_specs = (
        P(None, ("cells", "bands")),
        P("bands", "cells"),
        P(None, ("cells", "bands")),
        P(None, ("cells", "bands")),
    )
    out_specs = (P(None, ("cells", "bands")), P("bands", "cells"))
    return jax.shard_map(shards, mesh=mesh, in_specs=in_specs, out_specs=out_specs, check_vma=False)
```

```python
import functools
import math

import jax
import jax.numpy as jnp
import ml_dtypes
import numpy as np
from jax import lax
from jax.experimental import pallas as pl
from jax.experimental.pallas import tpu as pltpu
from jax.sharding import PartitionSpec as P

NWF = 32
DEGREE = 4
STEPS = 2
NXL = 8
NODES_DEV = 2048
PLANE = 256
LANES_V = 384
MESSAGE = NODES_DEV + 256
V_AT = 3 * NODES_DEV
G_AT = 5 * NODES_DEV
PAYLOAD = G_AT + 2 * 128
X_ORDER = (0, 4, 1, 3, 5, 7, 2, 6)
CLASS_ROWS = ((0, 2), (2, 6), (6, 8))
VMEM = 48 * 1024 * 1024


def kinetic_table():
    points = [-1.0, -math.sqrt(3.0 / 7.0), 0.0, math.sqrt(3.0 / 7.0), 1.0]
    weights = [0.1, 49.0 / 90.0, 32.0 / 45.0, 49.0 / 90.0, 0.1]
    scales = []
    for row in range(5):
        prod_val = 1.0
        for other in range(5):
            if other != row:
                prod_val = prod_val * (points[row] - points[other])
        scales.append(prod_val)
    deriv = [[0.0] * 5 for row in range(5)]
    for row in range(5):
        for col in range(5):
            if row != col:
                deriv[row][col] = scales[row] / scales[col] / (points[row] - points[col])
            else:
                total = 0.0
                for other in range(5):
                    if other != row:
                        total = total + 1.0 / (points[row] - points[other])
                deriv[row][col] = total
    stiff_one = [
        [sum((deriv[i][a] * weights[i] * deriv[i][b] for i in range(5))) for b in range(5)]
        for a in range(5)
    ]
    mass_one = [[weights[a] if a == b else 0.0 for b in range(5)] for a in range(5)]
    table = [[0.0] * 125 for row in range(125)]
    for k in range(125):
        ka, kb, kc = (k // 25, k // 5 % 5, k % 5)
        for j in range(125):
            ja, jb, jc = (j // 25, j // 5 % 5, j % 5)
            table[k][j] = 0.5 * (
                stiff_one[ka][ja] * mass_one[kb][jb] * mass_one[kc][jc]
                + mass_one[ka][ja] * stiff_one[kb][jb] * mass_one[kc][jc]
                + mass_one[ka][ja] * mass_one[kb][jb] * stiff_one[kc][jc]
            )
    assembled = [dict() for row in range(512)]
    for cell_x in range(2):
        for cell_y in range(2):
            for cell_z in range(2):
                global_ids = []
                for k in range(125):
                    node_x = (4 * cell_x + k // 25) % 8
                    node_y = (4 * cell_y + k // 5 % 5) % 8
                    node_z = (4 * cell_z + k % 5) % 8
                    global_ids.append((node_x * 8 + node_y) * 8 + node_z)
                for k in range(125):
                    row_map = assembled[global_ids[k]]
                    for j in range(125):
                        target = global_ids[j]
                        row_map[target] = row_map.get(target, 0.0) + table[k][j]
    largest = 0.0
    for row_map in assembled:
        total = sum((abs(value) for value in row_map.values()))
        largest = max(largest, total)
    bound = largest + 8.0 * 2.0
    return (np.array(table), float(0.55 * bound), float(0.45 * bound))


@functools.lru_cache(maxsize=None)
def tables():
    table, centre, half = kinetic_table()
    kin = table.astype(np.float32).astype(ml_dtypes.bfloat16).astype(np.float64)
    kin = kin.reshape(5, 5, 5, 5, 5, 5)
    planes = np.zeros((3, 3, PLANE, PLANE))
    lines = np.zeros((5, 5, PLANE))
    for j in range(-1, 5):
        for l in range(-1, 5):
            for b in range(5):
                for c in range(5):
                    y, z = 4 * j + b, 4 * l + c
                    if not (0 <= y < 16 and 0 <= z < 16):
                        continue
                    at = 16 * y + z
                    for a in range(5):
                        for other in range(5):
                            if other != a:
                                lines[a, other, at] += kin[a, b, c, other, b, c]
                    for b2 in range(5):
                        for c2 in range(5):
                            y2, z2 = 4 * j + b2, 4 * l + c2
                            far_y, far_z = y2 // 16, z2 // 16
                            source = 16 * (y2 % 16) + z2 % 16
                            for kind, locals_a in enumerate(((0, 4), (1,), (2,))):
                                value = sum(kin[a, b, c, a, b2, c2] for a in locals_a)
                                if value == 0.0:
                                    continue
                                assert far_y == 0 or far_z == 0
                                part = 1 if far_y else 2 if far_z else 0
                                planes[kind, part, source, at] += value
    line_rows = np.stack(
        [lines[0, 1], lines[0, 2], lines[0, 3], 2.0 * lines[0, 4], lines[1, 2], lines[1, 3]]
    )
    bf = ml_dtypes.bfloat16
    weights = np.zeros((3 * 3 * PLANE + 16, PLANE))
    weights[: 9 * PLANE] = planes.reshape(9 * PLANE, PLANE)
    weights[9 * PLANE : 9 * PLANE + 6] = line_rows
    return weights.astype(np.float32).astype(bf), centre, half


def iota(shape, dim):
    return lax.broadcasted_iota(jnp.int32, shape, dim)


def local_node(k):
    a = (k * 41) >> 10
    rest = k - 25 * a
    b = (rest * 205) >> 10
    return a, b, rest - 5 * b


def message_kernel(v_hbm, pot_hbm, conn_hbm, out_hbm, raw, conn, pot, packed, sems):
    copies = [
        pltpu.make_async_copy(pot_hbm, raw, sems.at[0]),
        pltpu.make_async_copy(conn_hbm, conn, sems.at[1]),
        pltpu.make_async_copy(v_hbm, out_hbm.at[:, :NODES_DEV], sems.at[2]),
    ]
    for copy in copies:
        copy.start()
    lane = iota((32, 128), 1)
    code = (4 * (lane >> 4) * 17 + 4 * ((lane >> 2) & 3)) * 17 + 4 * (lane & 3)
    pot[...] = jnp.zeros_like(pot)
    copies[0].wait()
    copies[1].wait()
    pot[:, :125] = raw[...]
    here = jnp.where((conn[:, 0:1] == code) & (lane < 32), lane.astype(jnp.float32), 0.0)
    cell = jnp.sum(here, axis=1, keepdims=True)
    high = pot[...].astype(jnp.bfloat16).astype(jnp.float32)
    low = pot[...] - high
    packed[:, :128] = jnp.where(lane == 127, cell, high).astype(jnp.bfloat16)
    packed[:, 128:] = low.astype(jnp.bfloat16)
    last = pltpu.make_async_copy(packed, out_hbm.at[:, NODES_DEV:], sems.at[3])
    last.start()
    copies[2].wait()
    last.wait()


def pick_kind(kind):
    a, b, c = local_node(iota((1, 128), 1))
    if kind < 4:
        hit = (b == 4) == (kind >= 2), (c == 4) == (kind % 2 == 1)
    else:
        hit = (b == 4) == (kind == 5), c == 4
    return jnp.where(hit[0] & hit[1] & (iota((1, 128), 1) < 125), 1.0, 0.0)


def place_of(i, kind):
    lane = iota((1, LANES_V), 1)
    y, z = lane >> 4, lane & 15
    j = (y >> 2) - (kind // 2 if kind < 4 else kind - 4)
    l = (z >> 2) - kind % 2 if kind < 4 else jnp.where(z == 0, 3, -1)
    good = (lane < PLANE + 16) & (j >= 0) & (j < 4) & (l >= 0)
    return jnp.where(good, 16 * i + 4 * j + l, -1).astype(jnp.float32)


def fitting():
    a, b, c = local_node(iota((128, LANES_V), 0))
    lane = iota((128, LANES_V), 1)
    fits = ((b & 3) == ((lane >> 4) & 3)) & ((c & 3) == (lane & 3)) & (lane < PLANE + 16)
    return jnp.where(fits, 1.0, 0.0)


def nodal(message, kind_range, mask, exact):
    rows, ones = [], ([], [])
    parts = [message[:, NODES_DEV : NODES_DEV + 128].astype(jnp.float32)]
    cell = parts[0][:, 127:128]
    if exact:
        parts.append(message[:, NODES_DEV + 128 :].astype(jnp.float32))
    for kind in kind_range:
        pick = pick_kind(kind)
        rows += [part * pick for part in parts]
        for i in range(2):
            one = jnp.where(cell == place_of(i, kind), 1.0, 0.0)
            ones[i].extend([one] * len(parts))
    stack = jnp.concatenate(rows, axis=0).astype(jnp.bfloat16)
    placed = jnp.concatenate([jnp.concatenate(one, axis=0) for one in ones], axis=1)
    both = lax.dot_general(
        stack, placed.astype(jnp.bfloat16), (((0,), (0,)), ((), ())), preferred_element_type=jnp.float32
    )
    total = jnp.zeros((8, LANES_V), jnp.float32)
    k = iota((8, 128), 1)
    along = local_node(k)[0]
    for i in range(2):
        values = both[:, LANES_V * i : LANES_V * (i + 1)] * mask
        high = values.astype(jnp.bfloat16)
        to_x = jnp.where((((4 * i + along) & 7) == iota((8, 128), 0)) & (k < 125), 1.0, 0.0)
        to_x = to_x.astype(jnp.bfloat16)
        total += jnp.dot(to_x, high, preferred_element_type=jnp.float32)
        if exact:
            low = (values - high.astype(jnp.float32)).astype(jnp.bfloat16)
            total += jnp.dot(to_x, low, preferred_element_type=jnp.float32)
    return total


def own_kernel(c_ref, v_ref, own_ref, edge_ref, mask_ref):
    v_ref[...] = c_ref[:, :NODES_DEV]
    mask = fitting()
    mask_ref[...] = mask
    own_ref[...] = nodal(c_ref, range(4), mask, True)
    edge_ref[...] = nodal(c_ref, range(4, 6), mask, True)


def pack_kernel(l_ref, r_ref, c_ref, own_ref, edge_ref, mask_ref, out_ref, ghost):
    even = iota((32, PLANE), 0) % 2 == 0
    mask = mask_ref[...]
    for s, message in enumerate((l_ref, c_ref, r_ref)):
        out_ref[:, NODES_DEV * s : NODES_DEV * (s + 1)] = message[:, :NODES_DEV]
    own = own_ref[...] + nodal(l_ref, range(4, 6), mask, True)
    left = nodal(l_ref, range(4), mask, False)
    right = nodal(r_ref, range(4), mask, False) + edge_ref[...]
    high = own.astype(jnp.bfloat16).astype(jnp.float32)
    for part, (first, second) in enumerate(((high, own - high), (left, right))):
        for x in range(NXL):
            main = jnp.where(even, first[x : x + 1, :PLANE], second[x : x + 1, :PLANE])
            at = V_AT + NODES_DEV * part + PLANE * x
            out_ref[:, at : at + PLANE] = main.astype(jnp.bfloat16)
            edge = jnp.where(even[:, :128], first[x : x + 1, PLANE:], second[x : x + 1, PLANE:])
            ghost[:, 16 * x : 16 * (x + 1)] = edge[:, :16]
        at = G_AT + 128 * part
        out_ref[:, at : at + 128] = ghost[...].astype(jnp.bfloat16)


def diagonal(got, g_ref, centre):
    lane, row = iota((128, NXL * 128), 1), iota((128, NXL * 128), 0)
    spread = jnp.where(((row >> 4) == (lane >> 7)) & ((row & 15) == (lane & 127)), 1.0, 0.0)
    spread = spread.astype(jnp.bfloat16)
    lane, row = iota((32, 64), 1), iota((32, 64), 0)
    source = jnp.where(lane < 32, row >> 1, ((row >> 1) + 15) & 15)
    same = source == ((lane & 31) >> 1)
    pairs = [
        jnp.where(same & good, 1.0, 0.0).astype(jnp.bfloat16)
        for good in ((lane & 1) == 0, lane >= 0, (lane & 1) == 1)
    ]
    edges = []
    for part in range(2):
        at = G_AT + 128 * part
        edge = jnp.dot(got[:, at : at + 128], spread, preferred_element_type=jnp.float32)
        edges.append(edge.astype(jnp.bfloat16))
    for s in range(3):
        part = 0 if s == 1 else 1
        at = V_AT + NODES_DEV * part
        base = jnp.dot(pairs[s][:, :32], got[:, at : at + NODES_DEV], preferred_element_type=jnp.float32)
        edge = jnp.dot(pairs[s][:, 32:], edges[part], preferred_element_type=jnp.float32)
        for x in range(NXL):
            at = PLANE * x
            first = base[:, at : at + 128] + edge[:, 128 * x : 128 * (x + 1)]
            g_ref[x, s, :, :128] = first - centre
            g_ref[x, s, :, 128:] = base[:, at + 128 : at + PLANE] - centre


def filter_step(slabs, w_ref, g_ref, out_ref, here, there, half):
    place = {x: at for at, x in enumerate(X_ORDER)}
    right_lanes = (iota((32, 128), 1) & 15) < 8
    lines = w_ref[9 * PLANE :, :].astype(jnp.float32)
    halves = [slice(128 * part, 128 * (part + 1)) for part in range(2)]

    def turned(part, value):
        return pltpu.roll(value, 30 if part == 0 else 2, 0)

    def put(ref, at, s, section, part, value):
        ref[at, s, :, PLANE * section + 128 * part : PLANE * section + 128 * (part + 1)] = value.astype(
            jnp.bfloat16
        )

    def put_sides(ref, at, part, left, middle, right):
        zero = jnp.zeros_like(left)
        put(ref, at, 0, 2, part, jnp.where(right_lanes, middle, zero))
        put(ref, at, 1, 2, part, jnp.where(right_lanes, right, left))
        put(ref, at, 2, 2, part, jnp.where(right_lanes, zero, middle))

    for x in range(NXL):
        for part in range(2):
            values = []
            for s, slab in enumerate(slabs):
                value = slab[:, PLANE * x + 128 * part : PLANE * x + 128 * (part + 1)].astype(jnp.float32)
                values.append(value)
                put(here, place[x], s, 0, part, value)
                put(here, place[x], s, 1, part, turned(part, value))
            put_sides(here, place[x], part, *values)

    def apply(src, dst, which, order):
        alpha = (1.0 if order == 0 else 2.0) / half
        first, last = which[0], which[-1] + 1
        for kind in (1, 0, 2):
            low, high = CLASS_ROWS[kind]
            count = (high - low) * (last - first) * 32
            result = jnp.dot(
                src[low:high, first:last].reshape(count, 3 * PLANE),
                w_ref[3 * PLANE * kind : 3 * PLANE * (kind + 1), :],
                preferred_element_type=jnp.float32,
            ).reshape(high - low, last - first, 32, PLANE)
            for at in range(low, high):
                x = X_ORDER[at]
                for part in range(2):
                    lanes = halves[part]
                    c01, c02, c03, c04, c12, c13 = (lines[row : row + 1, lanes] for row in range(6))
                    values = {}
                    for s in which:
                        v = lambda other: src[place[other % 8], s, :, lanes].astype(jnp.float32)
                        if x in (0, 4):
                            extra = c01 * (v(x + 1) + v(x + 7)) + c02 * (v(x + 2) + v(x + 6))
                            extra = extra + c03 * (v(x + 3) + v(x + 5)) + c04 * v(x + 4)
                        elif x in (2, 6):
                            extra = c02 * (v(x - 2) + v(x + 2)) + c12 * (v(x - 1) + v(x + 1))
                        else:
                            step = 1 if x in (1, 5) else -1
                            extra = c01 * v(x - step) + c12 * v(x + step)
                            extra = extra + c13 * v(x + 2 * step) + c03 * v(x + 3 * step)
                        diag = g_ref[x, s, :, lanes]
                        if which == (1, 2) and s == 2:
                            diag = jnp.where(right_lanes, diag, g_ref[x, 0, :, lanes])
                        new = alpha * (result[at - low, s - first, :, lanes] + extra + diag * v(x))
                        if order:
                            new = new - dst[at, s, :, lanes].astype(jnp.float32)
                        if order < DEGREE - 1:
                            new = new.astype(jnp.bfloat16).astype(jnp.float32)
                            put(dst, at, s, 0, part, new)
                            values[s] = new
                        else:
                            out_ref[:, PLANE * x + 128 * part : PLANE * x + 128 * (part + 1)] = new.astype(
                                jnp.bfloat16
                            )
                    if order == 0:
                        for s in which:
                            put(dst, at, s, 1, part, turned(part, values[s]))
                        put_sides(dst, at, part, values[0], values[1], values[2])
                    elif order == 1:
                        edge = jnp.where(right_lanes, values[2], values[0])
                        old = [src[at, s, :, lanes].astype(jnp.float32) for s in (0, 2)]
                        put(dst, at, 1, 1, part, turned(part, values[1]))
                        put(dst, at, 1, 2, part, edge)
                        put(dst, at, 2, 0, part, edge)
                        put(dst, at, 2, 1, part, turned(part, edge))
                        put(dst, at, 2, 2, part, values[1])
                        edges.append((at, part, jnp.where(right_lanes, old[1], old[0])))
                    elif order == 2:
                        put(dst, at, 1, 1, part, turned(part, values[1]))
                        put(dst, at, 1, 2, part, values[2])

    edges = []
    apply(here, there, (0, 1, 2), 0)
    apply(there, here, (0, 1, 2), 1)
    for at, part, edge in edges:
        put(there, at, 2, 0, part, edge)
    apply(here, there, (1, 2), 2)
    apply(there, here, (1,), 3)


def first_kernel(centre, half, got, w_ref, out_ref, g_ref, here, there):
    diagonal(got, g_ref, centre)
    slabs = [got.at[:, NODES_DEV * s : NODES_DEV * (s + 1)] for s in range(3)]
    filter_step(slabs, w_ref, g_ref, out_ref, here, there, half)


def later_kernel(half, c_ref, l_ref, r_ref, g_ref, st_ref, w_ref, out_ref, here, there):
    out_ref[:, NODES_DEV:] = st_ref[...]
    filter_step((l_ref, c_ref, r_ref), w_ref, g_ref, out_ref, here, there, half)


def corr_kernel(factor, got, out_ref):
    four = jnp.concatenate([got[:, :NODES_DEV]] * 4, axis=0)
    parts = [
        lax.dot_general(
            got[:, NODES_DEV * (1 + part) : NODES_DEV * (2 + part)],
            four,
            (((1,), (1,)), ((), ())),
            preferred_element_type=jnp.float32,
        )
        for part in range(2)
    ]
    lane, row = iota((NWF, 128), 1), iota((NWF, 128), 0)
    both = jnp.where(((lane >> 5) & 1) == 0, parts[0], parts[1])
    out_ref[...] = jnp.where((lane >> 6) == (row & 1), both * factor, 0.0)


def share_kernel(got, out_ref):
    total = jnp.sum(got[...], axis=0, keepdims=True)
    out_ref[...] = jnp.where((iota((NWF, 128), 1) & 31) == iota((NWF, 128), 0), total, 0.0)


def total_kernel(got, out_ref):
    total = jnp.sum(got[...], axis=0, keepdims=True)
    lane = iota((1, 128), 1)
    rows = jnp.zeros((1, 128), jnp.float32)
    for row in range(4):
        mine = jnp.where((lane >> 5) == row // 2 + 2 * (row % 2), total, 0.0)
        rows = jnp.where(lane == row, jnp.sum(mine, axis=1, keepdims=True), rows)
    out_ref[...] = rows[:, :4]


def full(shape):
    return pl.BlockSpec(shape, lambda *_: (0,) * len(shape))


def call(kernel, args, outs, scratch=()):
    return pl.pallas_call(
        kernel,
        grid=(1,),
        in_specs=[full(a.shape) for a in args],
        out_specs=[full(o.shape) for o in outs],
        out_shape=list(outs),
        scratch_shapes=list(scratch),
        compiler_params=pltpu.CompilerParams(vmem_limit_bytes=VMEM),
    )(*args)


def passed_along(block, axis, distance):
    devices = range(lax.axis_size(axis))
    route = [((i - distance) % len(devices), i) for i in devices]
    return lax.ppermute(block, axis, route)


def shards(cur_block, stored_blocks, cell_potential, connectivity):
    weights, centre, half = tables()
    weights = jnp.asarray(weights)
    bf, f32 = jnp.bfloat16, jnp.float32
    shape = jax.ShapeDtypeStruct
    n_cells, n_bands = lax.axis_size("cells"), lax.axis_size("bands")
    stored = stored_blocks.reshape(2, 2, n_bands, NODES_DEV).transpose(2, 1, 0, 3).reshape(NWF, 2 * NODES_DEV)
    hbm = pl.BlockSpec(memory_space=pltpu.HBM)
    message = pl.pallas_call(
        message_kernel,
        in_specs=[hbm] * 3,
        out_specs=hbm,
        out_shape=shape((NWF, MESSAGE), bf),
        scratch_shapes=[
            pltpu.VMEM((32, 125), f32),
            pltpu.VMEM((32, 125), jnp.int32),
            pltpu.VMEM((32, 128), f32),
            pltpu.VMEM((32, 256), bf),
            pltpu.SemaphoreType.DMA((4,)),
        ],
        compiler_params=pltpu.CompilerParams(vmem_limit_bytes=62 * 1024 * 1024),
    )(cur_block, cell_potential.T, connectivity.T)
    left = passed_along(message, "cells", 1)
    right = passed_along(message, "cells", -1)
    shapes = [shape((8, LANES_V), f32), shape((8, LANES_V), f32), shape((128, LANES_V), f32)]
    own = call(own_kernel, (message,), [shape((NWF, NODES_DEV), bf)] + shapes)
    (payload,) = call(
        pack_kernel,
        (left, right, *own),
        [shape((NWF, PAYLOAD), bf)],
        [pltpu.VMEM((32, 128), f32)],
    )
    got = lax.all_to_all(payload, "bands", 0, 0, tiled=True)
    scratch = [
        pltpu.VMEM((NXL, 3, NWF, 3 * PLANE), bf),
        pltpu.VMEM((NXL, 3, NWF, 3 * PLANE), bf),
    ]
    block, diag = call(
        functools.partial(first_kernel, centre, half),
        (got, weights),
        [shape((NWF, NODES_DEV), bf), shape((NXL, 3, NWF, PLANE), f32)],
        scratch,
    )
    left = passed_along(block, "cells", 1)
    right = passed_along(block, "cells", -1)
    factor = 1.0 / math.sqrt(NODES_DEV * n_cells * n_bands)
    (block,) = call(
        functools.partial(later_kernel, half),
        (block, left, right, diag, stored, weights),
        [shape((NWF, 3 * NODES_DEV), bf)],
        scratch,
    )
    got = lax.all_to_all(block, "bands", 0, 0, tiled=True)
    filtered = got[:, :NODES_DEV]
    (partial,) = call(functools.partial(corr_kernel, factor), (got,), [shape((NWF, 128), f32)])
    partial = lax.all_to_all(partial, "bands", 0, 0, tiled=True)
    (partial,) = call(share_kernel, (partial,), [shape((NWF, 128), f32)])
    partial = lax.all_to_all(partial, "cells", 0, 0, tiled=True)
    (total,) = call(total_kernel, (partial,), [shape((1, 4), f32)])
    return (filtered, total.T)


def solution(mesh):
    in_specs = (
        P(None, ("cells", "bands")),
        P("bands", "cells"),
        P(None, ("cells", "bands")),
        P(None, ("cells", "bands")),
    )
    out_specs = (P(None, ("cells", "bands")), P("bands", "cells"))
    return jax.shard_map(shards, mesh=mesh, in_specs=in_specs, out_specs=out_specs, check_vma=False)
```

```python
import functools
import math

import jax
import jax.numpy as jnp
import ml_dtypes
import numpy as np
from jax import lax
from jax.experimental import pallas as pl
from jax.experimental.pallas import tpu as pltpu
from jax.sharding import PartitionSpec as P

NWF = 32
DEGREE = 4
STEPS = 2
NXL = 8
NODES_DEV = 2048
PLANE = 256
LANES_V = 384
MESSAGE = NODES_DEV + 256
V_AT = 3 * NODES_DEV
G_AT = 5 * NODES_DEV
PAYLOAD = G_AT + 2 * 128
X_ORDER = (0, 4, 1, 3, 5, 7, 2, 6)
CLASS_ROWS = ((0, 2), (2, 6), (6, 8))
VMEM = 48 * 1024 * 1024


def kinetic_table():
    points = [-1.0, -math.sqrt(3.0 / 7.0), 0.0, math.sqrt(3.0 / 7.0), 1.0]
    weights = [0.1, 49.0 / 90.0, 32.0 / 45.0, 49.0 / 90.0, 0.1]
    scales = []
    for row in range(5):
        prod_val = 1.0
        for other in range(5):
            if other != row:
                prod_val = prod_val * (points[row] - points[other])
        scales.append(prod_val)
    deriv = [[0.0] * 5 for row in range(5)]
    for row in range(5):
        for col in range(5):
            if row != col:
                deriv[row][col] = scales[row] / scales[col] / (points[row] - points[col])
            else:
                total = 0.0
                for other in range(5):
                    if other != row:
                        total = total + 1.0 / (points[row] - points[other])
                deriv[row][col] = total
    stiff_one = [
        [sum((deriv[i][a] * weights[i] * deriv[i][b] for i in range(5))) for b in range(5)]
        for a in range(5)
    ]
    mass_one = [[weights[a] if a == b else 0.0 for b in range(5)] for a in range(5)]
    table = [[0.0] * 125 for row in range(125)]
    for k in range(125):
        ka, kb, kc = (k // 25, k // 5 % 5, k % 5)
        for j in range(125):
            ja, jb, jc = (j // 25, j // 5 % 5, j % 5)
            table[k][j] = 0.5 * (
                stiff_one[ka][ja] * mass_one[kb][jb] * mass_one[kc][jc]
                + mass_one[ka][ja] * stiff_one[kb][jb] * mass_one[kc][jc]
                + mass_one[ka][ja] * mass_one[kb][jb] * stiff_one[kc][jc]
            )
    assembled = [dict() for row in range(512)]
    for cell_x in range(2):
        for cell_y in range(2):
            for cell_z in range(2):
                global_ids = []
                for k in range(125):
                    node_x = (4 * cell_x + k // 25) % 8
                    node_y = (4 * cell_y + k // 5 % 5) % 8
                    node_z = (4 * cell_z + k % 5) % 8
                    global_ids.append((node_x * 8 + node_y) * 8 + node_z)
                for k in range(125):
                    row_map = assembled[global_ids[k]]
                    for j in range(125):
                        target = global_ids[j]
                        row_map[target] = row_map.get(target, 0.0) + table[k][j]
    largest = 0.0
    for row_map in assembled:
        total = sum((abs(value) for value in row_map.values()))
        largest = max(largest, total)
    bound = largest + 8.0 * 2.0
    return (np.array(table), float(0.55 * bound), float(0.45 * bound))


@functools.lru_cache(maxsize=None)
def tables():
    table, centre, half = kinetic_table()
    kin = table.astype(np.float32).astype(ml_dtypes.bfloat16).astype(np.float64)
    kin = kin.reshape(5, 5, 5, 5, 5, 5)
    planes = np.zeros((3, 3, PLANE, PLANE))
    lines = np.zeros((5, 5, PLANE))
    for j in range(-1, 5):
        for l in range(-1, 5):
            for b in range(5):
                for c in range(5):
                    y, z = 4 * j + b, 4 * l + c
                    if not (0 <= y < 16 and 0 <= z < 16):
                        continue
                    at = 16 * y + z
                    for a in range(5):
                        for other in range(5):
                            if other != a:
                                lines[a, other, at] += kin[a, b, c, other, b, c]
                    for b2 in range(5):
                        for c2 in range(5):
                            y2, z2 = 4 * j + b2, 4 * l + c2
                            far_y, far_z = y2 // 16, z2 // 16
                            source = 16 * (y2 % 16) + z2 % 16
                            for kind, locals_a in enumerate(((0, 4), (1,), (2,))):
                                value = sum(kin[a, b, c, a, b2, c2] for a in locals_a)
                                if value == 0.0:
                                    continue
                                assert far_y == 0 or far_z == 0
                                part = 1 if far_y else 2 if far_z else 0
                                planes[kind, part, source, at] += value
    line_rows = np.stack(
        [lines[0, 1], lines[0, 2], lines[0, 3], 2.0 * lines[0, 4], lines[1, 2], lines[1, 3]]
    )
    bf = ml_dtypes.bfloat16
    weights = np.zeros((3 * 3 * PLANE + 16, PLANE))
    weights[: 9 * PLANE] = planes.reshape(9 * PLANE, PLANE)
    weights[9 * PLANE : 9 * PLANE + 6] = line_rows
    return weights.astype(np.float32).astype(bf), centre, half


def iota(shape, dim):
    return lax.broadcasted_iota(jnp.int32, shape, dim)


def local_node(k):
    a = (k * 41) >> 10
    rest = k - 25 * a
    b = (rest * 205) >> 10
    return a, b, rest - 5 * b


def message_kernel(v_hbm, pot_hbm, conn_hbm, out_ref, raw, conn, pot, sems):
    copies = [
        pltpu.make_async_copy(pot_hbm, raw, sems.at[0]),
        pltpu.make_async_copy(conn_hbm, conn, sems.at[1]),
        pltpu.make_async_copy(v_hbm, out_ref.at[:, :NODES_DEV], sems.at[2]),
    ]
    for copy in copies:
        copy.start()
    lane = iota((32, 128), 1)
    code = (4 * (lane >> 4) * 17 + 4 * ((lane >> 2) & 3)) * 17 + 4 * (lane & 3)
    pot[...] = jnp.zeros_like(pot)
    copies[0].wait()
    copies[1].wait()
    pot[:, :125] = raw[...]
    here = jnp.where((conn[:, 0:1] == code) & (lane < 32), lane.astype(jnp.float32), 0.0)
    cell = jnp.sum(here, axis=1, keepdims=True)
    high = pot[...].astype(jnp.bfloat16).astype(jnp.float32)
    low = pot[...] - high
    out_ref[:, NODES_DEV : NODES_DEV + 128] = jnp.where(lane == 127, cell, high).astype(jnp.bfloat16)
    out_ref[:, NODES_DEV + 128 :] = low.astype(jnp.bfloat16)
    copies[2].wait()


def pick_kind(kind):
    a, b, c = local_node(iota((1, 128), 1))
    if kind < 4:
        hit = (b == 4) == (kind >= 2), (c == 4) == (kind % 2 == 1)
    else:
        hit = (b == 4) == (kind == 5), c == 4
    return jnp.where(hit[0] & hit[1] & (iota((1, 128), 1) < 125), 1.0, 0.0)


def place_of(i, kind):
    lane = iota((1, LANES_V), 1)
    y, z = lane >> 4, lane & 15
    j = (y >> 2) - (kind // 2 if kind < 4 else kind - 4)
    l = (z >> 2) - kind % 2 if kind < 4 else jnp.where(z == 0, 3, -1)
    good = (lane < PLANE + 16) & (j >= 0) & (j < 4) & (l >= 0)
    return jnp.where(good, 16 * i + 4 * j + l, -1).astype(jnp.float32)


def fitting():
    a, b, c = local_node(iota((128, LANES_V), 0))
    lane = iota((128, LANES_V), 1)
    fits = ((b & 3) == ((lane >> 4) & 3)) & ((c & 3) == (lane & 3)) & (lane < PLANE + 16)
    return jnp.where(fits, 1.0, 0.0)


def nodal(message, kind_range, mask, exact):
    rows, ones = [], ([], [])
    parts = [message[:, NODES_DEV : NODES_DEV + 128].astype(jnp.float32)]
    cell = parts[0][:, 127:128]
    if exact:
        parts.append(message[:, NODES_DEV + 128 :].astype(jnp.float32))
    for kind in kind_range:
        pick = pick_kind(kind)
        rows += [part * pick for part in parts]
        for i in range(2):
            one = jnp.where(cell == place_of(i, kind), 1.0, 0.0)
            ones[i].extend([one] * len(parts))
    stack = jnp.concatenate(rows, axis=0).astype(jnp.bfloat16)
    placed = jnp.concatenate([jnp.concatenate(one, axis=0) for one in ones], axis=1)
    both = lax.dot_general(
        stack, placed.astype(jnp.bfloat16), (((0,), (0,)), ((), ())), preferred_element_type=jnp.float32
    )
    total = jnp.zeros((8, LANES_V), jnp.float32)
    k = iota((8, 128), 1)
    along = local_node(k)[0]
    for i in range(2):
        values = both[:, LANES_V * i : LANES_V * (i + 1)] * mask
        high = values.astype(jnp.bfloat16)
        to_x = jnp.where((((4 * i + along) & 7) == iota((8, 128), 0)) & (k < 125), 1.0, 0.0)
        to_x = to_x.astype(jnp.bfloat16)
        total += jnp.dot(to_x, high, preferred_element_type=jnp.float32)
        if exact:
            low = (values - high.astype(jnp.float32)).astype(jnp.bfloat16)
            total += jnp.dot(to_x, low, preferred_element_type=jnp.float32)
    return total


def own_kernel(c_ref, v_ref, own_ref, edge_ref, mask_ref):
    v_ref[...] = c_ref[:, :NODES_DEV]
    mask = fitting()
    mask_ref[...] = mask
    own_ref[...] = nodal(c_ref, range(4), mask, True)
    edge_ref[...] = nodal(c_ref, range(4, 6), mask, True)


def pack_kernel(l_ref, r_ref, c_ref, own_ref, edge_ref, mask_ref, out_ref, ghost):
    even = iota((32, PLANE), 0) % 2 == 0
    mask = mask_ref[...]
    for s, message in enumerate((l_ref, c_ref, r_ref)):
        out_ref[:, NODES_DEV * s : NODES_DEV * (s + 1)] = message[:, :NODES_DEV]
    own = own_ref[...] + nodal(l_ref, range(4, 6), mask, True)
    left = nodal(l_ref, range(4), mask, False)
    right = nodal(r_ref, range(4), mask, False) + edge_ref[...]
    high = own.astype(jnp.bfloat16).astype(jnp.float32)
    for part, (first, second) in enumerate(((high, own - high), (left, right))):
        for x in range(NXL):
            main = jnp.where(even, first[x : x + 1, :PLANE], second[x : x + 1, :PLANE])
            at = V_AT + NODES_DEV * part + PLANE * x
            out_ref[:, at : at + PLANE] = main.astype(jnp.bfloat16)
            edge = jnp.where(even[:, :128], first[x : x + 1, PLANE:], second[x : x + 1, PLANE:])
            ghost[:, 16 * x : 16 * (x + 1)] = edge[:, :16]
        at = G_AT + 128 * part
        out_ref[:, at : at + 128] = ghost[...].astype(jnp.bfloat16)


def diagonal(got, g_ref, centre):
    lane, row = iota((128, NXL * 128), 1), iota((128, NXL * 128), 0)
    spread = jnp.where(((row >> 4) == (lane >> 7)) & ((row & 15) == (lane & 127)), 1.0, 0.0)
    spread = spread.astype(jnp.bfloat16)
    lane, row = iota((32, 64), 1), iota((32, 64), 0)
    source = jnp.where(lane < 32, row >> 1, ((row >> 1) + 15) & 15)
    same = source == ((lane & 31) >> 1)
    pairs = [
        jnp.where(same & good, 1.0, 0.0).astype(jnp.bfloat16)
        for good in ((lane & 1) == 0, lane >= 0, (lane & 1) == 1)
    ]
    edges = []
    for part in range(2):
        at = G_AT + 128 * part
        edge = jnp.dot(got[:, at : at + 128], spread, preferred_element_type=jnp.float32)
        edges.append(edge.astype(jnp.bfloat16))
    for s in range(3):
        part = 0 if s == 1 else 1
        at = V_AT + NODES_DEV * part
        base = jnp.dot(pairs[s][:, :32], got[:, at : at + NODES_DEV], preferred_element_type=jnp.float32)
        edge = jnp.dot(pairs[s][:, 32:], edges[part], preferred_element_type=jnp.float32)
        for x in range(NXL):
            at = PLANE * x
            first = base[:, at : at + 128] + edge[:, 128 * x : 128 * (x + 1)]
            g_ref[x, s, :, :128] = first - centre
            g_ref[x, s, :, 128:] = base[:, at + 128 : at + PLANE] - centre


def filter_step(slabs, w_ref, g_ref, out_ref, here, there, half):
    place = {x: at for at, x in enumerate(X_ORDER)}
    right_lanes = (iota((32, 128), 1) & 15) < 8
    lines = w_ref[9 * PLANE :, :].astype(jnp.float32)
    halves = [slice(128 * part, 128 * (part + 1)) for part in range(2)]

    def turned(part, value):
        return pltpu.roll(value, 30 if part == 0 else 2, 0)

    def put(ref, at, s, section, part, value):
        ref[at, s, :, PLANE * section + 128 * part : PLANE * section + 128 * (part + 1)] = value.astype(
            jnp.bfloat16
        )

    def put_sides(ref, at, part, left, middle, right):
        zero = jnp.zeros_like(left)
        put(ref, at, 0, 2, part, jnp.where(right_lanes, middle, zero))
        put(ref, at, 1, 2, part, jnp.where(right_lanes, right, left))
        put(ref, at, 2, 2, part, jnp.where(right_lanes, zero, middle))

    for x in range(NXL):
        for part in range(2):
            values = []
            for s, slab in enumerate(slabs):
                value = slab[:, PLANE * x + 128 * part : PLANE * x + 128 * (part + 1)].astype(jnp.float32)
                values.append(value)
                put(here, place[x], s, 0, part, value)
                put(here, place[x], s, 1, part, turned(part, value))
            put_sides(here, place[x], part, *values)

    def apply(src, dst, which, order):
        alpha = (1.0 if order == 0 else 2.0) / half
        first, last = which[0], which[-1] + 1
        for kind in (1, 0, 2):
            low, high = CLASS_ROWS[kind]
            count = (high - low) * (last - first) * 32
            result = jnp.dot(
                src[low:high, first:last].reshape(count, 3 * PLANE),
                w_ref[3 * PLANE * kind : 3 * PLANE * (kind + 1), :],
                preferred_element_type=jnp.float32,
            ).reshape(high - low, last - first, 32, PLANE)
            for at in range(low, high):
                x = X_ORDER[at]
                for part in range(2):
                    lanes = halves[part]
                    c01, c02, c03, c04, c12, c13 = (lines[row : row + 1, lanes] for row in range(6))
                    values = {}
                    for s in which:
                        v = lambda other: src[place[other % 8], s, :, lanes].astype(jnp.float32)
                        if x in (0, 4):
                            extra = c01 * (v(x + 1) + v(x + 7)) + c02 * (v(x + 2) + v(x + 6))
                            extra = extra + c03 * (v(x + 3) + v(x + 5)) + c04 * v(x + 4)
                        elif x in (2, 6):
                            extra = c02 * (v(x - 2) + v(x + 2)) + c12 * (v(x - 1) + v(x + 1))
                        else:
                            step = 1 if x in (1, 5) else -1
                            extra = c01 * v(x - step) + c12 * v(x + step)
                            extra = extra + c13 * v(x + 2 * step) + c03 * v(x + 3 * step)
                        diag = g_ref[x, s, :, lanes]
                        if which == (1, 2) and s == 2:
                            diag = jnp.where(right_lanes, diag, g_ref[x, 0, :, lanes])
                        new = alpha * (result[at - low, s - first, :, lanes] + extra + diag * v(x))
                        if order:
                            new = new - dst[at, s, :, lanes].astype(jnp.float32)
                        if order < DEGREE - 1:
                            new = new.astype(jnp.bfloat16).astype(jnp.float32)
                            put(dst, at, s, 0, part, new)
                            values[s] = new
                        else:
                            out_ref[:, PLANE * x + 128 * part : PLANE * x + 128 * (part + 1)] = new.astype(
                                jnp.bfloat16
                            )
                    if order == 0:
                        for s in which:
                            put(dst, at, s, 1, part, turned(part, values[s]))
                        put_sides(dst, at, part, values[0], values[1], values[2])
                    elif order == 1:
                        edge = jnp.where(right_lanes, values[2], values[0])
                        old = [src[at, s, :, lanes].astype(jnp.float32) for s in (0, 2)]
                        put(dst, at, 1, 1, part, turned(part, values[1]))
                        put(dst, at, 1, 2, part, edge)
                        put(dst, at, 2, 0, part, edge)
                        put(dst, at, 2, 1, part, turned(part, edge))
                        put(dst, at, 2, 2, part, values[1])
                        edges.append((at, part, jnp.where(right_lanes, old[1], old[0])))
                    elif order == 2:
                        put(dst, at, 1, 1, part, turned(part, values[1]))
                        put(dst, at, 1, 2, part, values[2])

    edges = []
    apply(here, there, (0, 1, 2), 0)
    apply(there, here, (0, 1, 2), 1)
    for at, part, edge in edges:
        put(there, at, 2, 0, part, edge)
    apply(here, there, (1, 2), 2)
    apply(there, here, (1,), 3)


def first_kernel(centre, half, got, w_ref, out_ref, g_ref, here, there):
    diagonal(got, g_ref, centre)
    slabs = [got.at[:, NODES_DEV * s : NODES_DEV * (s + 1)] for s in range(3)]
    filter_step(slabs, w_ref, g_ref, out_ref, here, there, half)


def later_kernel(half, c_ref, l_ref, r_ref, g_ref, st_ref, w_ref, out_ref, here, there):
    out_ref[:, NODES_DEV:] = st_ref[...]
    filter_step((l_ref, c_ref, r_ref), w_ref, g_ref, out_ref, here, there, half)


def corr_kernel(factor, got, out_ref):
    four = jnp.concatenate([got[:, :NODES_DEV]] * 4, axis=0)
    parts = [
        lax.dot_general(
            got[:, NODES_DEV * (1 + part) : NODES_DEV * (2 + part)],
            four,
            (((1,), (1,)), ((), ())),
            preferred_element_type=jnp.float32,
        )
        for part in range(2)
    ]
    lane, row = iota((NWF, 128), 1), iota((NWF, 128), 0)
    both = jnp.where(((lane >> 5) & 1) == 0, parts[0], parts[1])
    out_ref[...] = jnp.where((lane >> 6) == (row & 1), both * factor, 0.0)


def share_kernel(got, out_ref):
    total = jnp.sum(got[...], axis=0, keepdims=True)
    out_ref[...] = jnp.where((iota((NWF, 128), 1) & 31) == iota((NWF, 128), 0), total, 0.0)


def total_kernel(got, out_ref):
    total = jnp.sum(got[...], axis=0, keepdims=True)
    lane = iota((1, 128), 1)
    rows = jnp.zeros((1, 128), jnp.float32)
    for row in range(4):
        mine = jnp.where((lane >> 5) == row // 2 + 2 * (row % 2), total, 0.0)
        rows = jnp.where(lane == row, jnp.sum(mine, axis=1, keepdims=True), rows)
    out_ref[...] = rows[:, :4]


def full(shape):
    return pl.BlockSpec(shape, lambda *_: (0,) * len(shape))


def call(kernel, args, outs, scratch=(), far=(), limit=VMEM):
    hbm = pl.BlockSpec(memory_space=pltpu.HBM)
    return pl.pallas_call(
        kernel,
        grid=(1,),
        in_specs=[full(a.shape) for a in args] + [hbm] * len(far),
        out_specs=[full(o.shape) for o in outs],
        out_shape=list(outs),
        scratch_shapes=list(scratch),
        compiler_params=pltpu.CompilerParams(vmem_limit_bytes=limit),
    )(*args, *far)


def passed_along(block, axis, distance):
    devices = range(lax.axis_size(axis))
    route = [((i - distance) % len(devices), i) for i in devices]
    return lax.ppermute(block, axis, route)


def shards(cur_block, stored_blocks, cell_potential, connectivity):
    weights, centre, half = tables()
    weights = jnp.asarray(weights)
    bf, f32 = jnp.bfloat16, jnp.float32
    shape = jax.ShapeDtypeStruct
    n_cells, n_bands = lax.axis_size("cells"), lax.axis_size("bands")
    stored = stored_blocks.reshape(2, 2, n_bands, NODES_DEV).transpose(2, 1, 0, 3).reshape(NWF, 2 * NODES_DEV)
    (message,) = call(
        message_kernel,
        (),
        [shape((NWF, MESSAGE), bf)],
        [
            pltpu.VMEM((32, 125), f32),
            pltpu.VMEM((32, 125), jnp.int32),
            pltpu.VMEM((32, 128), f32),
            pltpu.SemaphoreType.DMA((3,)),
        ],
        (cur_block, cell_potential.T, connectivity.T),
        62 * 1024 * 1024,
    )
    left = passed_along(message, "cells", 1)
    right = passed_along(message, "cells", -1)
    shapes = [shape((8, LANES_V), f32), shape((8, LANES_V), f32), shape((128, LANES_V), f32)]
    own = call(own_kernel, (message,), [shape((NWF, NODES_DEV), bf)] + shapes)
    (payload,) = call(
        pack_kernel,
        (left, right, *own),
        [shape((NWF, PAYLOAD), bf)],
        [pltpu.VMEM((32, 128), f32)],
    )
    got = lax.all_to_all(payload, "bands", 0, 0, tiled=True)
    scratch = [
        pltpu.VMEM((NXL, 3, NWF, 3 * PLANE), bf),
        pltpu.VMEM((NXL, 3, NWF, 3 * PLANE), bf),
    ]
    block, diag = call(
        functools.partial(first_kernel, centre, half),
        (got, weights),
        [shape((NWF, NODES_DEV), bf), shape((NXL, 3, NWF, PLANE), f32)],
        scratch,
    )
    left = passed_along(block, "cells", 1)
    right = passed_along(block, "cells", -1)
    factor = 1.0 / math.sqrt(NODES_DEV * n_cells * n_bands)
    (block,) = call(
        functools.partial(later_kernel, half),
        (block, left, right, diag, stored, weights),
        [shape((NWF, 3 * NODES_DEV), bf)],
        scratch,
    )
    got = lax.all_to_all(block, "bands", 0, 0, tiled=True)
    filtered = got[:, :NODES_DEV]
    (partial,) = call(functools.partial(corr_kernel, factor), (got,), [shape((NWF, 128), f32)])
    partial = lax.all_to_all(partial, "bands", 0, 0, tiled=True)
    (partial,) = call(share_kernel, (partial,), [shape((NWF, 128), f32)])
    partial = lax.all_to_all(partial, "cells", 0, 0, tiled=True)
    (total,) = call(total_kernel, (partial,), [shape((1, 4), f32)])
    return (filtered, total.T)


def solution(mesh):
    in_specs = (
        P(None, ("cells", "bands")),
        P("bands", "cells"),
        P(None, ("cells", "bands")),
        P(None, ("cells", "bands")),
    )
    out_specs = (P(None, ("cells", "bands")), P("bands", "cells"))
    return jax.shard_map(shards, mesh=mesh, in_specs=in_specs, out_specs=out_specs, check_vma=False)
```

```python
import functools
import math

import jax
import jax.numpy as jnp
import ml_dtypes
import numpy as np
from jax import lax
from jax.experimental import pallas as pl
from jax.experimental.pallas import tpu as pltpu
from jax.sharding import PartitionSpec as P

NWF = 32
DEGREE = 4
STEPS = 2
NXL = 8
NODES_DEV = 2048
PLANE = 256
LANES_V = 384
MESSAGE = NODES_DEV + 256
V_AT = 3 * NODES_DEV
G_AT = 5 * NODES_DEV
PAYLOAD = G_AT + 2 * 128
X_ORDER = (0, 4, 1, 3, 5, 7, 2, 6)
CLASS_ROWS = ((0, 2), (2, 6), (6, 8))
VMEM = 48 * 1024 * 1024


def kinetic_table():
    points = [-1.0, -math.sqrt(3.0 / 7.0), 0.0, math.sqrt(3.0 / 7.0), 1.0]
    weights = [0.1, 49.0 / 90.0, 32.0 / 45.0, 49.0 / 90.0, 0.1]
    scales = []
    for row in range(5):
        prod_val = 1.0
        for other in range(5):
            if other != row:
                prod_val = prod_val * (points[row] - points[other])
        scales.append(prod_val)
    deriv = [[0.0] * 5 for row in range(5)]
    for row in range(5):
        for col in range(5):
            if row != col:
                deriv[row][col] = scales[row] / scales[col] / (points[row] - points[col])
            else:
                total = 0.0
                for other in range(5):
                    if other != row:
                        total = total + 1.0 / (points[row] - points[other])
                deriv[row][col] = total
    stiff_one = [
        [sum((deriv[i][a] * weights[i] * deriv[i][b] for i in range(5))) for b in range(5)]
        for a in range(5)
    ]
    mass_one = [[weights[a] if a == b else 0.0 for b in range(5)] for a in range(5)]
    table = [[0.0] * 125 for row in range(125)]
    for k in range(125):
        ka, kb, kc = (k // 25, k // 5 % 5, k % 5)
        for j in range(125):
            ja, jb, jc = (j // 25, j // 5 % 5, j % 5)
            table[k][j] = 0.5 * (
                stiff_one[ka][ja] * mass_one[kb][jb] * mass_one[kc][jc]
                + mass_one[ka][ja] * stiff_one[kb][jb] * mass_one[kc][jc]
                + mass_one[ka][ja] * mass_one[kb][jb] * stiff_one[kc][jc]
            )
    assembled = [dict() for row in range(512)]
    for cell_x in range(2):
        for cell_y in range(2):
            for cell_z in range(2):
                global_ids = []
                for k in range(125):
                    node_x = (4 * cell_x + k // 25) % 8
                    node_y = (4 * cell_y + k // 5 % 5) % 8
                    node_z = (4 * cell_z + k % 5) % 8
                    global_ids.append((node_x * 8 + node_y) * 8 + node_z)
                for k in range(125):
                    row_map = assembled[global_ids[k]]
                    for j in range(125):
                        target = global_ids[j]
                        row_map[target] = row_map.get(target, 0.0) + table[k][j]
    largest = 0.0
    for row_map in assembled:
        total = sum((abs(value) for value in row_map.values()))
        largest = max(largest, total)
    bound = largest + 8.0 * 2.0
    return (np.array(table), float(0.55 * bound), float(0.45 * bound))


@functools.lru_cache(maxsize=None)
def tables():
    table, centre, half = kinetic_table()
    kin = table.astype(np.float32).astype(ml_dtypes.bfloat16).astype(np.float64)
    kin = kin.reshape(5, 5, 5, 5, 5, 5)
    planes = np.zeros((3, 3, PLANE, PLANE))
    lines = np.zeros((5, 5, PLANE))
    for j in range(-1, 5):
        for l in range(-1, 5):
            for b in range(5):
                for c in range(5):
                    y, z = 4 * j + b, 4 * l + c
                    if not (0 <= y < 16 and 0 <= z < 16):
                        continue
                    at = 16 * y + z
                    for a in range(5):
                        for other in range(5):
                            if other != a:
                                lines[a, other, at] += kin[a, b, c, other, b, c]
                    for b2 in range(5):
                        for c2 in range(5):
                            y2, z2 = 4 * j + b2, 4 * l + c2
                            far_y, far_z = y2 // 16, z2 // 16
                            source = 16 * (y2 % 16) + z2 % 16
                            for kind, locals_a in enumerate(((0, 4), (1,), (2,))):
                                value = sum(kin[a, b, c, a, b2, c2] for a in locals_a)
                                if value == 0.0:
                                    continue
                                assert far_y == 0 or far_z == 0
                                part = 1 if far_y else 2 if far_z else 0
                                planes[kind, part, source, at] += value
    line_rows = np.stack(
        [lines[0, 1], lines[0, 2], lines[0, 3], 2.0 * lines[0, 4], lines[1, 2], lines[1, 3]]
    )
    bf = ml_dtypes.bfloat16
    weights = np.zeros((3 * 3 * PLANE + 16, PLANE))
    weights[: 9 * PLANE] = planes.reshape(9 * PLANE, PLANE)
    weights[9 * PLANE : 9 * PLANE + 6] = line_rows
    return weights.astype(np.float32).astype(bf), centre, half


def iota(shape, dim):
    return lax.broadcasted_iota(jnp.int32, shape, dim)


def local_node(k):
    a = (k * 41) >> 10
    rest = k - 25 * a
    b = (rest * 205) >> 10
    return a, b, rest - 5 * b


def message_kernel(v_hbm, pot_hbm, conn_hbm, out_ref, raw, conn, pot, sems):
    copies = [
        pltpu.make_async_copy(pot_hbm, raw, sems.at[0]),
        pltpu.make_async_copy(conn_hbm, conn, sems.at[1]),
        pltpu.make_async_copy(v_hbm, out_ref.at[:, :NODES_DEV], sems.at[2]),
    ]
    for copy in copies:
        copy.start()
    lane = iota((32, 128), 1)
    code = (4 * (lane >> 4) * 17 + 4 * ((lane >> 2) & 3)) * 17 + 4 * (lane & 3)
    pot[...] = jnp.zeros_like(pot)
    copies[0].wait()
    copies[1].wait()
    pot[:, :125] = raw[...]
    here = jnp.where((conn[:, 0:1] == code) & (lane < 32), lane.astype(jnp.float32), 0.0)
    cell = jnp.sum(here, axis=1, keepdims=True)
    high = pot[...].astype(jnp.bfloat16).astype(jnp.float32)
    low = pot[...] - high
    out_ref[:, NODES_DEV : NODES_DEV + 128] = jnp.where(lane == 127, cell, high).astype(jnp.bfloat16)
    out_ref[:, NODES_DEV + 128 :] = low.astype(jnp.bfloat16)
    copies[2].wait()


def pick_kind(kind):
    a, b, c = local_node(iota((1, 128), 1))
    if kind < 4:
        hit = (b == 4) == (kind >= 2), (c == 4) == (kind % 2 == 1)
    else:
        hit = (b == 4) == (kind == 5), c == 4
    return jnp.where(hit[0] & hit[1] & (iota((1, 128), 1) < 125), 1.0, 0.0)


def place_of(i, kind):
    lane = iota((1, LANES_V), 1)
    y, z = lane >> 4, lane & 15
    j = (y >> 2) - (kind // 2 if kind < 4 else kind - 4)
    l = (z >> 2) - kind % 2 if kind < 4 else jnp.where(z == 0, 3, -1)
    good = (lane < PLANE + 16) & (j >= 0) & (j < 4) & (l >= 0)
    return jnp.where(good, 16 * i + 4 * j + l, -1).astype(jnp.float32)


def fitting():
    a, b, c = local_node(iota((128, LANES_V), 0))
    lane = iota((128, LANES_V), 1)
    fits = ((b & 3) == ((lane >> 4) & 3)) & ((c & 3) == (lane & 3)) & (lane < PLANE + 16)
    return jnp.where(fits, 1.0, 0.0)


def nodal(message, kind_range, mask, exact):
    rows, ones = [], ([], [])
    parts = [message[:, NODES_DEV : NODES_DEV + 128].astype(jnp.float32)]
    cell = parts[0][:, 127:128]
    if exact:
        parts.append(message[:, NODES_DEV + 128 :].astype(jnp.float32))
    for kind in kind_range:
        pick = pick_kind(kind)
        rows += [part * pick for part in parts]
        for i in range(2):
            one = jnp.where(cell == place_of(i, kind), 1.0, 0.0)
            ones[i].extend([one] * len(parts))
    stack = jnp.concatenate(rows, axis=0).astype(jnp.bfloat16)
    placed = jnp.concatenate([jnp.concatenate(one, axis=0) for one in ones], axis=1)
    both = lax.dot_general(
        stack, placed.astype(jnp.bfloat16), (((0,), (0,)), ((), ())), preferred_element_type=jnp.float32
    )
    total = jnp.zeros((8, LANES_V), jnp.float32)
    k = iota((8, 128), 1)
    along = local_node(k)[0]
    for i in range(2):
        values = both[:, LANES_V * i : LANES_V * (i + 1)] * mask
        high = values.astype(jnp.bfloat16)
        to_x = jnp.where((((4 * i + along) & 7) == iota((8, 128), 0)) & (k < 125), 1.0, 0.0)
        to_x = to_x.astype(jnp.bfloat16)
        total += jnp.dot(to_x, high, preferred_element_type=jnp.float32)
        if exact:
            low = (values - high.astype(jnp.float32)).astype(jnp.bfloat16)
            total += jnp.dot(to_x, low, preferred_element_type=jnp.float32)
    return total


def own_kernel(c_ref, v_ref, own_ref, edge_ref, mask_ref):
    v_ref[...] = c_ref[:, :NODES_DEV]
    mask = fitting()
    mask_ref[...] = mask
    own_ref[...] = nodal(c_ref, range(4), mask, True)
    edge_ref[...] = nodal(c_ref, range(4, 6), mask, True)


def pack_kernel(l_ref, r_ref, c_ref, own_ref, edge_ref, mask_ref, out_ref, ghost):
    even = iota((32, PLANE), 0) % 2 == 0
    mask = mask_ref[...]
    for s, message in enumerate((l_ref, c_ref, r_ref)):
        out_ref[:, NODES_DEV * s : NODES_DEV * (s + 1)] = message[:, :NODES_DEV]
    own = own_ref[...] + nodal(l_ref, range(4, 6), mask, True)
    left = nodal(l_ref, range(4), mask, False)
    right = nodal(r_ref, range(4), mask, False) + edge_ref[...]
    high = own.astype(jnp.bfloat16).astype(jnp.float32)
    for part, (first, second) in enumerate(((high, own - high), (left, right))):
        for x in range(NXL):
            main = jnp.where(even, first[x : x + 1, :PLANE], second[x : x + 1, :PLANE])
            at = V_AT + NODES_DEV * part + PLANE * x
            out_ref[:, at : at + PLANE] = main.astype(jnp.bfloat16)
            edge = jnp.where(even[:, :128], first[x : x + 1, PLANE:], second[x : x + 1, PLANE:])
            ghost[:, 16 * x : 16 * (x + 1)] = edge[:, :16]
        at = G_AT + 128 * part
        out_ref[:, at : at + 128] = ghost[...].astype(jnp.bfloat16)


def diagonal(got, g_ref, centre):
    lane, row = iota((128, NXL * 128), 1), iota((128, NXL * 128), 0)
    spread = jnp.where(((row >> 4) == (lane >> 7)) & ((row & 15) == (lane & 127)), 1.0, 0.0)
    spread = spread.astype(jnp.bfloat16)
    lane, row = iota((32, 64), 1), iota((32, 64), 0)
    source = jnp.where(lane < 32, row >> 1, ((row >> 1) + 15) & 15)
    same = source == ((lane & 31) >> 1)
    pairs = [
        jnp.where(same & good, 1.0, 0.0).astype(jnp.bfloat16)
        for good in ((lane & 1) == 0, lane >= 0, (lane & 1) == 1)
    ]
    edges = []
    for part in range(2):
        at = G_AT + 128 * part
        edge = jnp.dot(got[:, at : at + 128], spread, preferred_element_type=jnp.float32)
        edges.append(edge.astype(jnp.bfloat16))
    for s in range(3):
        part = 0 if s == 1 else 1
        at = V_AT + NODES_DEV * part
        base = jnp.dot(pairs[s][:, :32], got[:, at : at + NODES_DEV], preferred_element_type=jnp.float32)
        edge = jnp.dot(pairs[s][:, 32:], edges[part], preferred_element_type=jnp.float32)
        for x in range(NXL):
            at = PLANE * x
            first = base[:, at : at + 128] + edge[:, 128 * x : 128 * (x + 1)]
            g_ref[x, s, :, :128] = first - centre
            g_ref[x, s, :, 128:] = base[:, at + 128 : at + PLANE] - centre


def filter_step(slabs, w_ref, g_ref, out_ref, here, there, half):
    place = {x: at for at, x in enumerate(X_ORDER)}
    right_lanes = (iota((32, 128), 1) & 15) < 8
    lines = w_ref[9 * PLANE :, :].astype(jnp.float32)
    halves = [slice(128 * part, 128 * (part + 1)) for part in range(2)]

    def turned(part, value):
        return pltpu.roll(value, 30 if part == 0 else 2, 0)

    def put(ref, at, s, section, part, value):
        ref[at, s, :, PLANE * section + 128 * part : PLANE * section + 128 * (part + 1)] = value.astype(
            jnp.bfloat16
        )

    def put_sides(ref, at, part, left, middle, right):
        zero = jnp.zeros_like(left)
        put(ref, at, 0, 2, part, jnp.where(right_lanes, middle, zero))
        put(ref, at, 1, 2, part, jnp.where(right_lanes, right, left))
        put(ref, at, 2, 2, part, jnp.where(right_lanes, zero, middle))

    for x in range(NXL):
        for part in range(2):
            values = []
            for s, slab in enumerate(slabs):
                value = slab[:, PLANE * x + 128 * part : PLANE * x + 128 * (part + 1)].astype(jnp.float32)
                values.append(value)
                put(here, place[x], s, 0, part, value)
                put(here, place[x], s, 1, part, turned(part, value))
            put_sides(here, place[x], part, *values)

    def apply(src, dst, which, order):
        alpha = (1.0 if order == 0 else 2.0) / half
        first, last = which[0], which[-1] + 1
        for kind in (1, 0, 2):
            low, high = CLASS_ROWS[kind]
            count = (high - low) * (last - first) * 32
            result = jnp.dot(
                src[low:high, first:last].reshape(count, 3 * PLANE),
                w_ref[3 * PLANE * kind : 3 * PLANE * (kind + 1), :],
                preferred_element_type=jnp.float32,
            ).reshape(high - low, last - first, 32, PLANE)
            for at in range(low, high):
                x = X_ORDER[at]
                for part in range(2):
                    lanes = halves[part]
                    c01, c02, c03, c04, c12, c13 = (lines[row : row + 1, lanes] for row in range(6))
                    values = {}
                    for s in which:
                        v = lambda other: src[place[other % 8], s, :, lanes].astype(jnp.float32)
                        if x in (0, 4):
                            extra = c01 * (v(x + 1) + v(x + 7)) + c02 * (v(x + 2) + v(x + 6))
                            extra = extra + c03 * (v(x + 3) + v(x + 5)) + c04 * v(x + 4)
                        elif x in (2, 6):
                            extra = c02 * (v(x - 2) + v(x + 2)) + c12 * (v(x - 1) + v(x + 1))
                        else:
                            step = 1 if x in (1, 5) else -1
                            extra = c01 * v(x - step) + c12 * v(x + step)
                            extra = extra + c13 * v(x + 2 * step) + c03 * v(x + 3 * step)
                        diag = g_ref[x, s, :, lanes]
                        if which == (1, 2) and s == 2:
                            diag = jnp.where(right_lanes, diag, g_ref[x, 0, :, lanes])
                        new = alpha * (result[at - low, s - first, :, lanes] + extra + diag * v(x))
                        if order:
                            new = new - dst[at, s, :, lanes].astype(jnp.float32)
                        if order < DEGREE - 1:
                            new = new.astype(jnp.bfloat16).astype(jnp.float32)
                            put(dst, at, s, 0, part, new)
                            values[s] = new
                        else:
                            out_ref[:, PLANE * x + 128 * part : PLANE * x + 128 * (part + 1)] = new.astype(
                                jnp.bfloat16
                            )
                    if order == 0:
                        for s in which:
                            put(dst, at, s, 1, part, turned(part, values[s]))
                        put_sides(dst, at, part, values[0], values[1], values[2])
                    elif order == 1:
                        edge = jnp.where(right_lanes, values[2], values[0])
                        old = [src[at, s, :, lanes].astype(jnp.float32) for s in (0, 2)]
                        put(dst, at, 1, 1, part, turned(part, values[1]))
                        put(dst, at, 1, 2, part, edge)
                        put(dst, at, 2, 0, part, edge)
                        put(dst, at, 2, 1, part, turned(part, edge))
                        put(dst, at, 2, 2, part, values[1])
                        edges.append((at, part, jnp.where(right_lanes, old[1], old[0])))
                    elif order == 2:
                        put(dst, at, 1, 1, part, turned(part, values[1]))
                        put(dst, at, 1, 2, part, values[2])

    edges = []
    apply(here, there, (0, 1, 2), 0)
    apply(there, here, (0, 1, 2), 1)
    for at, part, edge in edges:
        put(there, at, 2, 0, part, edge)
    apply(here, there, (1, 2), 2)
    apply(there, here, (1,), 3)


def first_kernel(centre, half, got, w_ref, out_ref, g_ref, here, there):
    diagonal(got, g_ref, centre)
    slabs = [got.at[:, NODES_DEV * s : NODES_DEV * (s + 1)] for s in range(3)]
    filter_step(slabs, w_ref, g_ref, out_ref, here, there, half)


def later_kernel(half, c_ref, l_ref, r_ref, g_ref, st_ref, w_ref, out_ref, here, there):
    out_ref[:, NODES_DEV:] = st_ref[...]
    filter_step((l_ref, c_ref, r_ref), w_ref, g_ref, out_ref, here, there, half)


def corr_kernel(factor, got, out_ref):
    four = jnp.concatenate([got[:, :NODES_DEV]] * 4, axis=0)
    parts = [
        lax.dot_general(
            got[:, NODES_DEV * (1 + part) : NODES_DEV * (2 + part)],
            four,
            (((1,), (1,)), ((), ())),
            preferred_element_type=jnp.float32,
        )
        for part in range(2)
    ]
    lane, row = iota((NWF, 128), 1), iota((NWF, 128), 0)
    both = jnp.where(((lane >> 5) & 1) == 0, parts[0], parts[1])
    both = jnp.where((lane >> 6) == (row & 1), both * factor, 0.0)
    lane, row = iota((64, NWF), 1), iota((64, NWF), 0)
    owner = jnp.where((row & 15) == (lane >> 1), 1.0, 0.0)
    both = jnp.dot(owner, both, precision=lax.Precision.HIGHEST, preferred_element_type=jnp.float32)
    out_ref[...] = jnp.where((iota((64, 128), 1) & 3) == (iota((64, 128), 0) >> 4), both, 0.0)


def share_kernel(got, out_ref):
    total = jnp.sum(got[...], axis=0, keepdims=True)
    lane, row = iota((8, 128), 1), iota((8, 128), 0)
    out_ref[...] = jnp.where(((lane & 31) >> 2) == row, total, 0.0)


def total_kernel(got, out_ref):
    total = jnp.sum(got[...], axis=0, keepdims=True)
    lane = iota((1, 128), 1)
    rows = jnp.zeros((1, 128), jnp.float32)
    for row in range(4):
        mine = jnp.where((lane >> 5) == row // 2 + 2 * (row % 2), total, 0.0)
        rows = jnp.where(lane == row, jnp.sum(mine, axis=1, keepdims=True), rows)
    out_ref[...] = rows[:, :4]


def full(shape):
    return pl.BlockSpec(shape, lambda *_: (0,) * len(shape))


def call(kernel, args, outs, scratch=(), far=(), limit=VMEM):
    hbm = pl.BlockSpec(memory_space=pltpu.HBM)
    return pl.pallas_call(
        kernel,
        grid=(1,),
        in_specs=[full(a.shape) for a in args] + [hbm] * len(far),
        out_specs=[full(o.shape) for o in outs],
        out_shape=list(outs),
        scratch_shapes=list(scratch),
        compiler_params=pltpu.CompilerParams(vmem_limit_bytes=limit),
    )(*args, *far)


def passed_along(block, axis, distance):
    devices = range(lax.axis_size(axis))
    route = [((i - distance) % len(devices), i) for i in devices]
    return lax.ppermute(block, axis, route)


def shards(cur_block, stored_blocks, cell_potential, connectivity):
    weights, centre, half = tables()
    weights = jnp.asarray(weights)
    bf, f32 = jnp.bfloat16, jnp.float32
    shape = jax.ShapeDtypeStruct
    n_cells, n_bands = lax.axis_size("cells"), lax.axis_size("bands")
    stored = stored_blocks.reshape(2, 2, n_bands, NODES_DEV).transpose(2, 1, 0, 3).reshape(NWF, 2 * NODES_DEV)
    (message,) = call(
        message_kernel,
        (),
        [shape((NWF, MESSAGE), bf)],
        [
            pltpu.VMEM((32, 125), f32),
            pltpu.VMEM((32, 125), jnp.int32),
            pltpu.VMEM((32, 128), f32),
            pltpu.SemaphoreType.DMA((3,)),
        ],
        (cur_block, cell_potential.T, connectivity.T),
        62 * 1024 * 1024,
    )
    left = passed_along(message, "cells", 1)
    right = passed_along(message, "cells", -1)
    shapes = [shape((8, LANES_V), f32), shape((8, LANES_V), f32), shape((128, LANES_V), f32)]
    own = call(own_kernel, (message,), [shape((NWF, NODES_DEV), bf)] + shapes)
    (payload,) = call(
        pack_kernel,
        (left, right, *own),
        [shape((NWF, PAYLOAD), bf)],
        [pltpu.VMEM((32, 128), f32)],
    )
    got = lax.all_to_all(payload, "bands", 0, 0, tiled=True)
    scratch = [
        pltpu.VMEM((NXL, 3, NWF, 3 * PLANE), bf),
        pltpu.VMEM((NXL, 3, NWF, 3 * PLANE), bf),
    ]
    block, diag = call(
        functools.partial(first_kernel, centre, half),
        (got, weights),
        [shape((NWF, NODES_DEV), bf), shape((NXL, 3, NWF, PLANE), f32)],
        scratch,
    )
    left = passed_along(block, "cells", 1)
    right = passed_along(block, "cells", -1)
    factor = 1.0 / math.sqrt(NODES_DEV * n_cells * n_bands)
    (block,) = call(
        functools.partial(later_kernel, half),
        (block, left, right, diag, stored, weights),
        [shape((NWF, 3 * NODES_DEV), bf)],
        scratch,
    )
    got = lax.all_to_all(block, "bands", 0, 0, tiled=True)
    filtered = got[:, :NODES_DEV]
    (partial,) = call(functools.partial(corr_kernel, factor), (got,), [shape((64, 128), f32)])
    planes = [list(range(at, at + 64)) for at in range(0, n_cells * n_bands, 64)]
    columns = [list(range(at, n_cells, 4)) for at in range(4)]
    partial = lax.all_to_all(partial, ("cells", "bands"), 0, 0, tiled=True, axis_index_groups=planes)
    (partial,) = call(share_kernel, (partial,), [shape((8, 128), f32)])
    partial = lax.all_to_all(partial, "cells", 0, 0, tiled=True, axis_index_groups=columns)
    (total,) = call(total_kernel, (partial,), [shape((1, 4), f32)])
    return (filtered, total.T)


def solution(mesh):
    in_specs = (
        P(None, ("cells", "bands")),
        P("bands", "cells"),
        P(None, ("cells", "bands")),
        P(None, ("cells", "bands")),
    )
    out_specs = (P(None, ("cells", "bands")), P("bands", "cells"))
    return jax.shard_map(shards, mesh=mesh, in_specs=in_specs, out_specs=out_specs, check_vma=False)
```

```python
import functools
import math

import jax
import jax.numpy as jnp
import ml_dtypes
import numpy as np
from jax import lax
from jax.experimental import pallas as pl
from jax.experimental.pallas import tpu as pltpu
from jax.sharding import PartitionSpec as P

NWF = 32
DEGREE = 4
STEPS = 2
NXL = 8
NODES_DEV = 2048
PLANE = 256
LANES_V = 384
MESSAGE = NODES_DEV + 256
V_AT = 3 * NODES_DEV
G_AT = 5 * NODES_DEV
PAYLOAD = G_AT + 2 * 128
X_ORDER = (0, 4, 1, 3, 5, 7, 2, 6)
CLASS_ROWS = ((0, 2), (2, 6), (6, 8))
VMEM = 48 * 1024 * 1024


def kinetic_table():
    points = [-1.0, -math.sqrt(3.0 / 7.0), 0.0, math.sqrt(3.0 / 7.0), 1.0]
    weights = [0.1, 49.0 / 90.0, 32.0 / 45.0, 49.0 / 90.0, 0.1]
    scales = []
    for row in range(5):
        prod_val = 1.0
        for other in range(5):
            if other != row:
                prod_val = prod_val * (points[row] - points[other])
        scales.append(prod_val)
    deriv = [[0.0] * 5 for row in range(5)]
    for row in range(5):
        for col in range(5):
            if row != col:
                deriv[row][col] = scales[row] / scales[col] / (points[row] - points[col])
            else:
                total = 0.0
                for other in range(5):
                    if other != row:
                        total = total + 1.0 / (points[row] - points[other])
                deriv[row][col] = total
    stiff_one = [
        [sum((deriv[i][a] * weights[i] * deriv[i][b] for i in range(5))) for b in range(5)]
        for a in range(5)
    ]
    mass_one = [[weights[a] if a == b else 0.0 for b in range(5)] for a in range(5)]
    table = [[0.0] * 125 for row in range(125)]
    for k in range(125):
        ka, kb, kc = (k // 25, k // 5 % 5, k % 5)
        for j in range(125):
            ja, jb, jc = (j // 25, j // 5 % 5, j % 5)
            table[k][j] = 0.5 * (
                stiff_one[ka][ja] * mass_one[kb][jb] * mass_one[kc][jc]
                + mass_one[ka][ja] * stiff_one[kb][jb] * mass_one[kc][jc]
                + mass_one[ka][ja] * mass_one[kb][jb] * stiff_one[kc][jc]
            )
    assembled = [dict() for row in range(512)]
    for cell_x in range(2):
        for cell_y in range(2):
            for cell_z in range(2):
                global_ids = []
                for k in range(125):
                    node_x = (4 * cell_x + k // 25) % 8
                    node_y = (4 * cell_y + k // 5 % 5) % 8
                    node_z = (4 * cell_z + k % 5) % 8
                    global_ids.append((node_x * 8 + node_y) * 8 + node_z)
                for k in range(125):
                    row_map = assembled[global_ids[k]]
                    for j in range(125):
                        target = global_ids[j]
                        row_map[target] = row_map.get(target, 0.0) + table[k][j]
    largest = 0.0
    for row_map in assembled:
        total = sum((abs(value) for value in row_map.values()))
        largest = max(largest, total)
    bound = largest + 8.0 * 2.0
    return (np.array(table), float(0.55 * bound), float(0.45 * bound))


@functools.lru_cache(maxsize=None)
def tables():
    table, centre, half = kinetic_table()
    kin = table.astype(np.float32).astype(ml_dtypes.bfloat16).astype(np.float64)
    kin = kin.reshape(5, 5, 5, 5, 5, 5)
    planes = np.zeros((3, 3, PLANE, PLANE))
    lines = np.zeros((5, 5, PLANE))
    for j in range(-1, 5):
        for l in range(-1, 5):
            for b in range(5):
                for c in range(5):
                    y, z = 4 * j + b, 4 * l + c
                    if not (0 <= y < 16 and 0 <= z < 16):
                        continue
                    at = 16 * y + z
                    for a in range(5):
                        for other in range(5):
                            if other != a:
                                lines[a, other, at] += kin[a, b, c, other, b, c]
                    for b2 in range(5):
                        for c2 in range(5):
                            y2, z2 = 4 * j + b2, 4 * l + c2
                            far_y, far_z = y2 // 16, z2 // 16
                            source = 16 * (y2 % 16) + z2 % 16
                            for kind, locals_a in enumerate(((0, 4), (1,), (2,))):
                                value = sum(kin[a, b, c, a, b2, c2] for a in locals_a)
                                if value == 0.0:
                                    continue
                                assert far_y == 0 or far_z == 0
                                part = 1 if far_y else 2 if far_z else 0
                                planes[kind, part, source, at] += value
    line_rows = np.stack(
        [lines[0, 1], lines[0, 2], lines[0, 3], 2.0 * lines[0, 4], lines[1, 2], lines[1, 3]]
    )
    bf = ml_dtypes.bfloat16
    weights = np.zeros((3 * 3 * PLANE + 16, PLANE))
    weights[: 9 * PLANE] = planes.reshape(9 * PLANE, PLANE)
    weights[9 * PLANE : 9 * PLANE + 6] = line_rows
    return weights.astype(np.float32).astype(bf), centre, half


def iota(shape, dim):
    return lax.broadcasted_iota(jnp.int32, shape, dim)


def local_node(k):
    a = (k * 41) >> 10
    rest = k - 25 * a
    b = (rest * 205) >> 10
    return a, b, rest - 5 * b


def message_kernel(v_hbm, pot_hbm, conn_hbm, out_ref, raw, conn, pot, sems):
    copies = [
        pltpu.make_async_copy(pot_hbm, raw, sems.at[0]),
        pltpu.make_async_copy(conn_hbm, conn, sems.at[1]),
        pltpu.make_async_copy(v_hbm, out_ref.at[:, :NODES_DEV], sems.at[2]),
    ]
    for copy in copies:
        copy.start()
    lane = iota((32, 128), 1)
    code = (4 * (lane >> 4) * 17 + 4 * ((lane >> 2) & 3)) * 17 + 4 * (lane & 3)
    pot[...] = jnp.zeros_like(pot)
    copies[0].wait()
    copies[1].wait()
    pot[:, :125] = raw[...]
    here = jnp.where((conn[:, 0:1] == code) & (lane < 32), lane.astype(jnp.float32), 0.0)
    cell = jnp.sum(here, axis=1, keepdims=True)
    high = pot[...].astype(jnp.bfloat16).astype(jnp.float32)
    low = pot[...] - high
    out_ref[:, NODES_DEV : NODES_DEV + 128] = jnp.where(lane == 127, cell, high).astype(jnp.bfloat16)
    out_ref[:, NODES_DEV + 128 :] = low.astype(jnp.bfloat16)
    copies[2].wait()


def pick_kind(kind):
    a, b, c = local_node(iota((1, 128), 1))
    if kind < 4:
        hit = (b == 4) == (kind >= 2), (c == 4) == (kind % 2 == 1)
    else:
        hit = (b == 4) == (kind == 5), c == 4
    return jnp.where(hit[0] & hit[1] & (iota((1, 128), 1) < 125), 1.0, 0.0)


def place_of(i, kind):
    lane = iota((1, LANES_V), 1)
    y, z = lane >> 4, lane & 15
    j = (y >> 2) - (kind // 2 if kind < 4 else kind - 4)
    l = (z >> 2) - kind % 2 if kind < 4 else jnp.where(z == 0, 3, -1)
    good = (lane < PLANE + 16) & (j >= 0) & (j < 4) & (l >= 0)
    return jnp.where(good, 16 * i + 4 * j + l, -1).astype(jnp.float32)


def fitting():
    a, b, c = local_node(iota((128, LANES_V), 0))
    lane = iota((128, LANES_V), 1)
    fits = ((b & 3) == ((lane >> 4) & 3)) & ((c & 3) == (lane & 3)) & (lane < PLANE + 16)
    return jnp.where(fits, 1.0, 0.0)


def nodal(message, kind_range, mask, exact):
    rows, ones = [], ([], [])
    parts = [message[:, NODES_DEV : NODES_DEV + 128].astype(jnp.float32)]
    cell = parts[0][:, 127:128]
    if exact:
        parts.append(message[:, NODES_DEV + 128 :].astype(jnp.float32))
    for kind in kind_range:
        pick = pick_kind(kind)
        rows += [part * pick for part in parts]
        for i in range(2):
            one = jnp.where(cell == place_of(i, kind), 1.0, 0.0)
            ones[i].extend([one] * len(parts))
    stack = jnp.concatenate(rows, axis=0).astype(jnp.bfloat16)
    placed = jnp.concatenate([jnp.concatenate(one, axis=0) for one in ones], axis=1)
    both = lax.dot_general(
        stack, placed.astype(jnp.bfloat16), (((0,), (0,)), ((), ())), preferred_element_type=jnp.float32
    )
    total = jnp.zeros((8, LANES_V), jnp.float32)
    k = iota((8, 128), 1)
    along = local_node(k)[0]
    for i in range(2):
        values = both[:, LANES_V * i : LANES_V * (i + 1)] * mask
        high = values.astype(jnp.bfloat16)
        to_x = jnp.where((((4 * i + along) & 7) == iota((8, 128), 0)) & (k < 125), 1.0, 0.0)
        to_x = to_x.astype(jnp.bfloat16)
        total += jnp.dot(to_x, high, preferred_element_type=jnp.float32)
        if exact:
            low = (values - high.astype(jnp.float32)).astype(jnp.bfloat16)
            total += jnp.dot(to_x, low, preferred_element_type=jnp.float32)
    return total


def own_kernel(c_ref, v_ref, own_ref, edge_ref, mask_ref):
    v_ref[...] = c_ref[:, :NODES_DEV]
    mask = fitting()
    mask_ref[...] = mask
    own_ref[...] = nodal(c_ref, range(4), mask, True)
    edge_ref[...] = nodal(c_ref, range(4, 6), mask, True)


def pack_kernel(l_ref, r_ref, c_ref, own_ref, edge_ref, mask_ref, out_ref, ghost):
    even = iota((32, PLANE), 0) % 2 == 0
    mask = mask_ref[...]
    for s, message in enumerate((l_ref, c_ref, r_ref)):
        out_ref[:, NODES_DEV * s : NODES_DEV * (s + 1)] = message[:, :NODES_DEV]
    own = own_ref[...] + nodal(l_ref, range(4, 6), mask, True)
    left = nodal(l_ref, range(4), mask, False)
    right = nodal(r_ref, range(4), mask, False) + edge_ref[...]
    high = own.astype(jnp.bfloat16).astype(jnp.float32)
    for part, (first, second) in enumerate(((high, own - high), (left, right))):
        for x in range(NXL):
            main = jnp.where(even, first[x : x + 1, :PLANE], second[x : x + 1, :PLANE])
            at = V_AT + NODES_DEV * part + PLANE * x
            out_ref[:, at : at + PLANE] = main.astype(jnp.bfloat16)
            edge = jnp.where(even[:, :128], first[x : x + 1, PLANE:], second[x : x + 1, PLANE:])
            ghost[:, 16 * x : 16 * (x + 1)] = edge[:, :16]
        at = G_AT + 128 * part
        out_ref[:, at : at + 128] = ghost[...].astype(jnp.bfloat16)


def diagonal(got, g_ref, centre):
    lane, row = iota((128, NXL * 128), 1), iota((128, NXL * 128), 0)
    spread = jnp.where(((row >> 4) == (lane >> 7)) & ((row & 15) == (lane & 127)), 1.0, 0.0)
    spread = spread.astype(jnp.bfloat16)
    lane, row = iota((32, 64), 1), iota((32, 64), 0)
    source = jnp.where(lane < 32, row >> 1, ((row >> 1) + 15) & 15)
    same = source == ((lane & 31) >> 1)
    pairs = [
        jnp.where(same & good, 1.0, 0.0).astype(jnp.bfloat16)
        for good in ((lane & 1) == 0, lane >= 0, (lane & 1) == 1)
    ]
    edges = []
    for part in range(2):
        at = G_AT + 128 * part
        edge = jnp.dot(got[:, at : at + 128], spread, preferred_element_type=jnp.float32)
        edges.append(edge.astype(jnp.bfloat16))
    for s in range(3):
        part = 0 if s == 1 else 1
        at = V_AT + NODES_DEV * part
        base = jnp.dot(pairs[s][:, :32], got[:, at : at + NODES_DEV], preferred_element_type=jnp.float32)
        edge = jnp.dot(pairs[s][:, 32:], edges[part], preferred_element_type=jnp.float32)
        for x in range(NXL):
            at = PLANE * x
            first = base[:, at : at + 128] + edge[:, 128 * x : 128 * (x + 1)]
            g_ref[x, s, :, :128] = first - centre
            g_ref[x, s, :, 128:] = base[:, at + 128 : at + PLANE] - centre


def filter_step(slabs, w_ref, g_ref, out_ref, here, there, half):
    place = {x: at for at, x in enumerate(X_ORDER)}
    right_lanes = (iota((32, 128), 1) & 15) < 8
    lines = w_ref[9 * PLANE :, :].astype(jnp.float32)
    halves = [slice(128 * part, 128 * (part + 1)) for part in range(2)]

    def turned(part, value):
        return pltpu.roll(value, 30 if part == 0 else 2, 0)

    def put(ref, at, s, section, part, value):
        ref[at, s, :, PLANE * section + 128 * part : PLANE * section + 128 * (part + 1)] = value.astype(
            jnp.bfloat16
        )

    def put_sides(ref, at, part, left, middle, right):
        zero = jnp.zeros_like(left)
        put(ref, at, 0, 2, part, jnp.where(right_lanes, middle, zero))
        put(ref, at, 1, 2, part, jnp.where(right_lanes, right, left))
        put(ref, at, 2, 2, part, jnp.where(right_lanes, zero, middle))

    for x in range(NXL):
        for part in range(2):
            values = []
            for s, slab in enumerate(slabs):
                value = slab[:, PLANE * x + 128 * part : PLANE * x + 128 * (part + 1)].astype(jnp.float32)
                values.append(value)
                put(here, place[x], s, 0, part, value)
                put(here, place[x], s, 1, part, turned(part, value))
            put_sides(here, place[x], part, *values)

    def apply(src, dst, which, order):
        alpha = (1.0 if order == 0 else 2.0) / half
        first, last = which[0], which[-1] + 1
        for kind in (1, 0, 2):
            low, high = CLASS_ROWS[kind]
            count = (high - low) * (last - first) * 32
            result = jnp.dot(
                src[low:high, first:last].reshape(count, 3 * PLANE),
                w_ref[3 * PLANE * kind : 3 * PLANE * (kind + 1), :],
                preferred_element_type=jnp.float32,
            ).reshape(high - low, last - first, 32, PLANE)
            for at in range(low, high):
                x = X_ORDER[at]
                for part in range(2):
                    lanes = halves[part]
                    c01, c02, c03, c04, c12, c13 = (lines[row : row + 1, lanes] for row in range(6))
                    values = {}
                    for s in which:
                        v = lambda other: src[place[other % 8], s, :, lanes].astype(jnp.float32)
                        if x in (0, 4):
                            extra = c01 * (v(x + 1) + v(x + 7)) + c02 * (v(x + 2) + v(x + 6))
                            extra = extra + c03 * (v(x + 3) + v(x + 5)) + c04 * v(x + 4)
                        elif x in (2, 6):
                            extra = c02 * (v(x - 2) + v(x + 2)) + c12 * (v(x - 1) + v(x + 1))
                        else:
                            step = 1 if x in (1, 5) else -1
                            extra = c01 * v(x - step) + c12 * v(x + step)
                            extra = extra + c13 * v(x + 2 * step) + c03 * v(x + 3 * step)
                        diag = g_ref[x, s, :, lanes]
                        if which == (1, 2) and s == 2:
                            diag = jnp.where(right_lanes, diag, g_ref[x, 0, :, lanes])
                        new = alpha * (result[at - low, s - first, :, lanes] + extra + diag * v(x))
                        if order:
                            new = new - dst[at, s, :, lanes].astype(jnp.float32)
                        if order < DEGREE - 1:
                            new = new.astype(jnp.bfloat16).astype(jnp.float32)
                            put(dst, at, s, 0, part, new)
                            values[s] = new
                        else:
                            out_ref[:, PLANE * x + 128 * part : PLANE * x + 128 * (part + 1)] = new.astype(
                                jnp.bfloat16
                            )
                    if order == 0:
                        for s in which:
                            put(dst, at, s, 1, part, turned(part, values[s]))
                        put_sides(dst, at, part, values[0], values[1], values[2])
                    elif order == 1:
                        edge = jnp.where(right_lanes, values[2], values[0])
                        old = [src[at, s, :, lanes].astype(jnp.float32) for s in (0, 2)]
                        put(dst, at, 1, 1, part, turned(part, values[1]))
                        put(dst, at, 1, 2, part, edge)
                        put(dst, at, 2, 0, part, edge)
                        put(dst, at, 2, 1, part, turned(part, edge))
                        put(dst, at, 2, 2, part, values[1])
                        edges.append((at, part, jnp.where(right_lanes, old[1], old[0])))
                    elif order == 2:
                        put(dst, at, 1, 1, part, turned(part, values[1]))
                        put(dst, at, 1, 2, part, values[2])

    edges = []
    apply(here, there, (0, 1, 2), 0)
    apply(there, here, (0, 1, 2), 1)
    for at, part, edge in edges:
        put(there, at, 2, 0, part, edge)
    apply(here, there, (1, 2), 2)
    apply(there, here, (1,), 3)


def first_kernel(centre, half, got, w_ref, out_ref, g_ref, here, there):
    diagonal(got, g_ref, centre)
    slabs = [got.at[:, NODES_DEV * s : NODES_DEV * (s + 1)] for s in range(3)]
    filter_step(slabs, w_ref, g_ref, out_ref, here, there, half)


def later_kernel(half, c_ref, l_ref, r_ref, g_ref, st_ref, w_ref, out_ref, here, there):
    out_ref[:, NODES_DEV:] = st_ref[...]
    filter_step((l_ref, c_ref, r_ref), w_ref, g_ref, out_ref, here, there, half)


def corr_kernel(factor, got, out_ref, pairs):
    four = jnp.concatenate([got[:, :NODES_DEV]] * 4, axis=0)
    parts = [
        lax.dot_general(
            got[:, NODES_DEV * (1 + part) : NODES_DEV * (2 + part)],
            four,
            (((1,), (1,)), ((), ())),
            preferred_element_type=jnp.float32,
        )
        for part in range(2)
    ]
    lane, row = iota((NWF, 128), 1), iota((NWF, 128), 0)
    both = jnp.where(((lane >> 5) & 1) == 0, parts[0], parts[1])
    both = jnp.where((lane >> 6) == (row & 1), both * factor, 0.0)
    pairs[...] = both + pltpu.roll(both, NWF - 1, 0)
    even = pairs[pl.ds(0, 16, stride=2), :]
    both = jnp.concatenate([even] * 4, axis=0)
    out_ref[...] = jnp.where((iota((64, 128), 1) & 3) == (iota((64, 128), 0) >> 4), both, 0.0)


def share_kernel(got, out_ref):
    total = jnp.sum(got[...], axis=0, keepdims=True)
    lane, row = iota((8, 128), 1), iota((8, 128), 0)
    out_ref[...] = jnp.where(((lane & 31) >> 2) == row, total, 0.0)


def total_kernel(got, out_ref):
    total = jnp.sum(got[...], axis=0, keepdims=True)
    lane = iota((1, 128), 1)
    rows = jnp.zeros((1, 128), jnp.float32)
    for row in range(4):
        mine = jnp.where((lane >> 5) == row // 2 + 2 * (row % 2), total, 0.0)
        rows = jnp.where(lane == row, jnp.sum(mine, axis=1, keepdims=True), rows)
    out_ref[...] = rows[:, :4]


def full(shape):
    return pl.BlockSpec(shape, lambda *_: (0,) * len(shape))


def call(kernel, args, outs, scratch=(), far=(), limit=VMEM):
    hbm = pl.BlockSpec(memory_space=pltpu.HBM)
    return pl.pallas_call(
        kernel,
        grid=(1,),
        in_specs=[full(a.shape) for a in args] + [hbm] * len(far),
        out_specs=[full(o.shape) for o in outs],
        out_shape=list(outs),
        scratch_shapes=list(scratch),
        compiler_params=pltpu.CompilerParams(vmem_limit_bytes=limit),
    )(*args, *far)


def passed_along(block, axis, distance):
    devices = range(lax.axis_size(axis))
    route = [((i - distance) % len(devices), i) for i in devices]
    return lax.ppermute(block, axis, route)


def shards(cur_block, stored_blocks, cell_potential, connectivity):
    weights, centre, half = tables()
    weights = jnp.asarray(weights)
    bf, f32 = jnp.bfloat16, jnp.float32
    shape = jax.ShapeDtypeStruct
    n_cells, n_bands = lax.axis_size("cells"), lax.axis_size("bands")
    stored = stored_blocks.reshape(2, 2, n_bands, NODES_DEV).transpose(2, 1, 0, 3).reshape(NWF, 2 * NODES_DEV)
    (message,) = call(
        message_kernel,
        (),
        [shape((NWF, MESSAGE), bf)],
        [
            pltpu.VMEM((32, 125), f32),
            pltpu.VMEM((32, 125), jnp.int32),
            pltpu.VMEM((32, 128), f32),
            pltpu.SemaphoreType.DMA((3,)),
        ],
        (cur_block, cell_potential.T, connectivity.T),
        62 * 1024 * 1024,
    )
    left = passed_along(message, "cells", 1)
    right = passed_along(message, "cells", -1)
    shapes = [shape((8, LANES_V), f32), shape((8, LANES_V), f32), shape((128, LANES_V), f32)]
    own = call(own_kernel, (message,), [shape((NWF, NODES_DEV), bf)] + shapes)
    (payload,) = call(
        pack_kernel,
        (left, right, *own),
        [shape((NWF, PAYLOAD), bf)],
        [pltpu.VMEM((32, 128), f32)],
    )
    got = lax.all_to_all(payload, "bands", 0, 0, tiled=True)
    scratch = [
        pltpu.VMEM((NXL, 3, NWF, 3 * PLANE), bf),
        pltpu.VMEM((NXL, 3, NWF, 3 * PLANE), bf),
    ]
    block, diag = call(
        functools.partial(first_kernel, centre, half),
        (got, weights),
        [shape((NWF, NODES_DEV), bf), shape((NXL, 3, NWF, PLANE), f32)],
        scratch,
    )
    left = passed_along(block, "cells", 1)
    right = passed_along(block, "cells", -1)
    factor = 1.0 / math.sqrt(NODES_DEV * n_cells * n_bands)
    (block,) = call(
        functools.partial(later_kernel, half),
        (block, left, right, diag, stored, weights),
        [shape((NWF, 3 * NODES_DEV), bf)],
        scratch,
    )
    got = lax.all_to_all(block, "bands", 0, 0, tiled=True)
    filtered = got[:, :NODES_DEV]
    (partial,) = call(
        functools.partial(corr_kernel, factor),
        (got,),
        [shape((64, 128), f32)],
        [pltpu.VMEM((NWF, 128), f32)],
    )
    planes = [list(range(at, at + 64)) for at in range(0, n_cells * n_bands, 64)]
    columns = [list(range(at, n_cells, 4)) for at in range(4)]
    partial = lax.all_to_all(partial, ("cells", "bands"), 0, 0, tiled=True, axis_index_groups=planes)
    (partial,) = call(share_kernel, (partial,), [shape((8, 128), f32)])
    partial = lax.all_to_all(partial, "cells", 0, 0, tiled=True, axis_index_groups=columns)
    (total,) = call(total_kernel, (partial,), [shape((1, 4), f32)])
    return (filtered, total.T)


def solution(mesh):
    in_specs = (
        P(None, ("cells", "bands")),
        P("bands", "cells"),
        P(None, ("cells", "bands")),
        P(None, ("cells", "bands")),
    )
    out_specs = (P(None, ("cells", "bands")), P("bands", "cells"))
    return jax.shard_map(shards, mesh=mesh, in_specs=in_specs, out_specs=out_specs, check_vma=False)
```

```python
import functools
import math

import jax
import jax.numpy as jnp
import ml_dtypes
import numpy as np
from jax import lax
from jax.experimental import pallas as pl
from jax.experimental.pallas import tpu as pltpu
from jax.sharding import PartitionSpec as P

NWF = 32
DEGREE = 4
STEPS = 2
NXL = 8
NODES_DEV = 2048
PLANE = 256
LANES_V = 384
MESSAGE = NODES_DEV + 256
V_AT = 3 * NODES_DEV
G_AT = 5 * NODES_DEV
PAYLOAD = G_AT + 2 * 128
X_ORDER = (0, 4, 1, 3, 5, 7, 2, 6)
CLASS_ROWS = ((0, 2), (2, 6), (6, 8))
VMEM = 48 * 1024 * 1024


def kinetic_table():
    points = [-1.0, -math.sqrt(3.0 / 7.0), 0.0, math.sqrt(3.0 / 7.0), 1.0]
    weights = [0.1, 49.0 / 90.0, 32.0 / 45.0, 49.0 / 90.0, 0.1]
    scales = []
    for row in range(5):
        prod_val = 1.0
        for other in range(5):
            if other != row:
                prod_val = prod_val * (points[row] - points[other])
        scales.append(prod_val)
    deriv = [[0.0] * 5 for row in range(5)]
    for row in range(5):
        for col in range(5):
            if row != col:
                deriv[row][col] = scales[row] / scales[col] / (points[row] - points[col])
            else:
                total = 0.0
                for other in range(5):
                    if other != row:
                        total = total + 1.0 / (points[row] - points[other])
                deriv[row][col] = total
    stiff_one = [
        [sum((deriv[i][a] * weights[i] * deriv[i][b] for i in range(5))) for b in range(5)]
        for a in range(5)
    ]
    mass_one = [[weights[a] if a == b else 0.0 for b in range(5)] for a in range(5)]
    table = [[0.0] * 125 for row in range(125)]
    for k in range(125):
        ka, kb, kc = (k // 25, k // 5 % 5, k % 5)
        for j in range(125):
            ja, jb, jc = (j // 25, j // 5 % 5, j % 5)
            table[k][j] = 0.5 * (
                stiff_one[ka][ja] * mass_one[kb][jb] * mass_one[kc][jc]
                + mass_one[ka][ja] * stiff_one[kb][jb] * mass_one[kc][jc]
                + mass_one[ka][ja] * mass_one[kb][jb] * stiff_one[kc][jc]
            )
    assembled = [dict() for row in range(512)]
    for cell_x in range(2):
        for cell_y in range(2):
            for cell_z in range(2):
                global_ids = []
                for k in range(125):
                    node_x = (4 * cell_x + k // 25) % 8
                    node_y = (4 * cell_y + k // 5 % 5) % 8
                    node_z = (4 * cell_z + k % 5) % 8
                    global_ids.append((node_x * 8 + node_y) * 8 + node_z)
                for k in range(125):
                    row_map = assembled[global_ids[k]]
                    for j in range(125):
                        target = global_ids[j]
                        row_map[target] = row_map.get(target, 0.0) + table[k][j]
    largest = 0.0
    for row_map in assembled:
        total = sum((abs(value) for value in row_map.values()))
        largest = max(largest, total)
    bound = largest + 8.0 * 2.0
    return (np.array(table), float(0.55 * bound), float(0.45 * bound))


@functools.lru_cache(maxsize=None)
def tables():
    table, centre, half = kinetic_table()
    kin = table.astype(np.float32).astype(ml_dtypes.bfloat16).astype(np.float64)
    kin = kin.reshape(5, 5, 5, 5, 5, 5)
    planes = np.zeros((3, 3, PLANE, PLANE))
    lines = np.zeros((5, 5, PLANE))
    for j in range(-1, 5):
        for l in range(-1, 5):
            for b in range(5):
                for c in range(5):
                    y, z = 4 * j + b, 4 * l + c
                    if not (0 <= y < 16 and 0 <= z < 16):
                        continue
                    at = 16 * y + z
                    for a in range(5):
                        for other in range(5):
                            if other != a:
                                lines[a, other, at] += kin[a, b, c, other, b, c]
                    for b2 in range(5):
                        for c2 in range(5):
                            y2, z2 = 4 * j + b2, 4 * l + c2
                            far_y, far_z = y2 // 16, z2 // 16
                            source = 16 * (y2 % 16) + z2 % 16
                            for kind, locals_a in enumerate(((0, 4), (1,), (2,))):
                                value = sum(kin[a, b, c, a, b2, c2] for a in locals_a)
                                if value == 0.0:
                                    continue
                                assert far_y == 0 or far_z == 0
                                part = 1 if far_y else 2 if far_z else 0
                                planes[kind, part, source, at] += value
    line_rows = np.stack(
        [lines[0, 1], lines[0, 2], lines[0, 3], 2.0 * lines[0, 4], lines[1, 2], lines[1, 3]]
    )
    bf = ml_dtypes.bfloat16
    weights = np.zeros((3 * 3 * PLANE + 16, PLANE))
    weights[: 9 * PLANE] = planes.reshape(9 * PLANE, PLANE)
    weights[9 * PLANE : 9 * PLANE + 6] = line_rows
    return weights.astype(np.float32).astype(bf), centre, half


def iota(shape, dim):
    return lax.broadcasted_iota(jnp.int32, shape, dim)


def local_node(k):
    a = (k * 41) >> 10
    rest = k - 25 * a
    b = (rest * 205) >> 10
    return a, b, rest - 5 * b


def message_kernel(v_hbm, pot_hbm, conn_hbm, out_ref, raw, conn, pot, sems):
    copies = [
        pltpu.make_async_copy(pot_hbm, raw, sems.at[0]),
        pltpu.make_async_copy(conn_hbm, conn, sems.at[1]),
        pltpu.make_async_copy(v_hbm, out_ref.at[:, :NODES_DEV], sems.at[2]),
    ]
    for copy in copies:
        copy.start()
    lane = iota((32, 128), 1)
    code = (4 * (lane >> 4) * 17 + 4 * ((lane >> 2) & 3)) * 17 + 4 * (lane & 3)
    pot[...] = jnp.zeros_like(pot)
    copies[0].wait()
    copies[1].wait()
    pot[:, :125] = raw[...]
    here = jnp.where((conn[:, 0:1] == code) & (lane < 32), lane.astype(jnp.float32), 0.0)
    cell = jnp.sum(here, axis=1, keepdims=True)
    high = pot[...].astype(jnp.bfloat16).astype(jnp.float32)
    low = pot[...] - high
    out_ref[:, NODES_DEV : NODES_DEV + 128] = jnp.where(lane == 127, cell, high).astype(jnp.bfloat16)
    out_ref[:, NODES_DEV + 128 :] = low.astype(jnp.bfloat16)
    copies[2].wait()


def pick_kind(kind):
    a, b, c = local_node(iota((1, 128), 1))
    if kind < 4:
        hit = (b == 4) == (kind >= 2), (c == 4) == (kind % 2 == 1)
    else:
        hit = (b == 4) == (kind == 5), c == 4
    return jnp.where(hit[0] & hit[1] & (iota((1, 128), 1) < 125), 1.0, 0.0)


def place_of(i, kind):
    lane = iota((1, LANES_V), 1)
    y, z = lane >> 4, lane & 15
    j = (y >> 2) - (kind // 2 if kind < 4 else kind - 4)
    l = (z >> 2) - kind % 2 if kind < 4 else jnp.where(z == 0, 3, -1)
    good = (lane < PLANE + 16) & (j >= 0) & (j < 4) & (l >= 0)
    return jnp.where(good, 16 * i + 4 * j + l, -1).astype(jnp.float32)


def fitting():
    a, b, c = local_node(iota((128, LANES_V), 0))
    lane = iota((128, LANES_V), 1)
    fits = ((b & 3) == ((lane >> 4) & 3)) & ((c & 3) == (lane & 3)) & (lane < PLANE + 16)
    return jnp.where(fits, 1.0, 0.0)


def nodal(message, kind_range, mask, exact):
    rows, ones = [], ([], [])
    parts = [message[:, NODES_DEV : NODES_DEV + 128].astype(jnp.float32)]
    cell = parts[0][:, 127:128]
    if exact:
        parts.append(message[:, NODES_DEV + 128 :].astype(jnp.float32))
    for kind in kind_range:
        pick = pick_kind(kind)
        rows += [part * pick for part in parts]
        for i in range(2):
            one = jnp.where(cell == place_of(i, kind), 1.0, 0.0)
            ones[i].extend([one] * len(parts))
    stack = jnp.concatenate(rows, axis=0).astype(jnp.bfloat16)
    placed = jnp.concatenate([jnp.concatenate(one, axis=0) for one in ones], axis=1)
    both = lax.dot_general(
        stack, placed.astype(jnp.bfloat16), (((0,), (0,)), ((), ())), preferred_element_type=jnp.float32
    )
    total = jnp.zeros((8, LANES_V), jnp.float32)
    k = iota((8, 128), 1)
    along = local_node(k)[0]
    for i in range(2):
        values = both[:, LANES_V * i : LANES_V * (i + 1)] * mask
        high = values.astype(jnp.bfloat16)
        to_x = jnp.where((((4 * i + along) & 7) == iota((8, 128), 0)) & (k < 125), 1.0, 0.0)
        to_x = to_x.astype(jnp.bfloat16)
        total += jnp.dot(to_x, high, preferred_element_type=jnp.float32)
        if exact:
            low = (values - high.astype(jnp.float32)).astype(jnp.bfloat16)
            total += jnp.dot(to_x, low, preferred_element_type=jnp.float32)
    return total


def own_kernel(c_ref, v_ref, own_ref, edge_ref, mask_ref):
    v_ref[...] = c_ref[:, :NODES_DEV]
    mask = fitting()
    mask_ref[...] = mask
    own_ref[...] = nodal(c_ref, range(4), mask, True)
    edge_ref[...] = nodal(c_ref, range(4, 6), mask, True)


def pack_kernel(l_ref, r_ref, c_ref, own_ref, edge_ref, mask_ref, out_ref, ghost):
    even = iota((32, PLANE), 0) % 2 == 0
    mask = mask_ref[...]
    for s, message in enumerate((l_ref, c_ref, r_ref)):
        out_ref[:, NODES_DEV * s : NODES_DEV * (s + 1)] = message[:, :NODES_DEV]
    own = own_ref[...] + nodal(l_ref, range(4, 6), mask, True)
    left = nodal(l_ref, range(4), mask, False)
    right = nodal(r_ref, range(4), mask, False) + edge_ref[...]
    high = own.astype(jnp.bfloat16).astype(jnp.float32)
    for part, (first, second) in enumerate(((high, own - high), (left, right))):
        for x in range(NXL):
            main = jnp.where(even, first[x : x + 1, :PLANE], second[x : x + 1, :PLANE])
            at = V_AT + NODES_DEV * part + PLANE * x
            out_ref[:, at : at + PLANE] = main.astype(jnp.bfloat16)
            edge = jnp.where(even[:, :128], first[x : x + 1, PLANE:], second[x : x + 1, PLANE:])
            ghost[:, 16 * x : 16 * (x + 1)] = edge[:, :16]
        at = G_AT + 128 * part
        out_ref[:, at : at + 128] = ghost[...].astype(jnp.bfloat16)


def diagonal(got, g_ref, centre):
    lane, row = iota((128, NXL * 128), 1), iota((128, NXL * 128), 0)
    spread = jnp.where(((row >> 4) == (lane >> 7)) & ((row & 15) == (lane & 127)), 1.0, 0.0)
    spread = spread.astype(jnp.bfloat16)
    lane, row = iota((32, 64), 1), iota((32, 64), 0)
    source = jnp.where(lane < 32, row >> 1, ((row >> 1) + 15) & 15)
    same = source == ((lane & 31) >> 1)
    pairs = [
        jnp.where(same & good, 1.0, 0.0).astype(jnp.bfloat16)
        for good in ((lane & 1) == 0, lane >= 0, (lane & 1) == 1)
    ]
    edges = []
    for part in range(2):
        at = G_AT + 128 * part
        edge = jnp.dot(got[:, at : at + 128], spread, preferred_element_type=jnp.float32)
        edges.append(edge.astype(jnp.bfloat16))
    for s in range(3):
        part = 0 if s == 1 else 1
        at = V_AT + NODES_DEV * part
        base = jnp.dot(pairs[s][:, :32], got[:, at : at + NODES_DEV], preferred_element_type=jnp.float32)
        edge = jnp.dot(pairs[s][:, 32:], edges[part], preferred_element_type=jnp.float32)
        for x in range(NXL):
            at = PLANE * x
            first = base[:, at : at + 128] + edge[:, 128 * x : 128 * (x + 1)]
            g_ref[x, s, :, :128] = first - centre
            g_ref[x, s, :, 128:] = base[:, at + 128 : at + PLANE] - centre


def filter_step(slabs, w_ref, g_ref, out_ref, here, there, half):
    place = {x: at for at, x in enumerate(X_ORDER)}
    right_lanes = (iota((32, 128), 1) & 15) < 8
    lines = w_ref[9 * PLANE :, :].astype(jnp.float32)
    halves = [slice(128 * part, 128 * (part + 1)) for part in range(2)]

    def turned(part, value):
        return pltpu.roll(value, 30 if part == 0 else 2, 0)

    def put(ref, at, s, section, part, value):
        ref[at, s, :, PLANE * section + 128 * part : PLANE * section + 128 * (part + 1)] = value.astype(
            jnp.bfloat16
        )

    def put_sides(ref, at, part, left, middle, right):
        zero = jnp.zeros_like(left)
        put(ref, at, 0, 2, part, jnp.where(right_lanes, middle, zero))
        put(ref, at, 1, 2, part, jnp.where(right_lanes, right, left))
        put(ref, at, 2, 2, part, jnp.where(right_lanes, zero, middle))

    for x in range(NXL):
        for part in range(2):
            values = []
            for s, slab in enumerate(slabs):
                value = slab[:, PLANE * x + 128 * part : PLANE * x + 128 * (part + 1)].astype(jnp.float32)
                values.append(value)
                put(here, place[x], s, 0, part, value)
                put(here, place[x], s, 1, part, turned(part, value))
            put_sides(here, place[x], part, *values)

    def apply(src, dst, which, order):
        alpha = (1.0 if order == 0 else 2.0) / half
        first, last = which[0], which[-1] + 1
        for kind in (1, 0, 2):
            low, high = CLASS_ROWS[kind]
            count = (high - low) * (last - first) * 32
            result = jnp.dot(
                src[low:high, first:last].reshape(count, 3 * PLANE),
                w_ref[3 * PLANE * kind : 3 * PLANE * (kind + 1), :],
                preferred_element_type=jnp.float32,
            ).reshape(high - low, last - first, 32, PLANE)
            for at in range(low, high):
                x = X_ORDER[at]
                for part in range(2):
                    lanes = halves[part]
                    c01, c02, c03, c04, c12, c13 = (lines[row : row + 1, lanes] for row in range(6))
                    values = {}
                    for s in which:
                        v = lambda other: src[place[other % 8], s, :, lanes].astype(jnp.float32)
                        if x in (0, 4):
                            extra = c01 * (v(x + 1) + v(x + 7)) + c02 * (v(x + 2) + v(x + 6))
                            extra = extra + c03 * (v(x + 3) + v(x + 5)) + c04 * v(x + 4)
                        elif x in (2, 6):
                            extra = c02 * (v(x - 2) + v(x + 2)) + c12 * (v(x - 1) + v(x + 1))
                        else:
                            step = 1 if x in (1, 5) else -1
                            extra = c01 * v(x - step) + c12 * v(x + step)
                            extra = extra + c13 * v(x + 2 * step) + c03 * v(x + 3 * step)
                        diag = g_ref[x, s, :, lanes]
                        if which == (1, 2) and s == 2:
                            diag = jnp.where(right_lanes, diag, g_ref[x, 0, :, lanes])
                        new = alpha * (result[at - low, s - first, :, lanes] + extra + diag * v(x))
                        if order:
                            new = new - dst[at, s, :, lanes].astype(jnp.float32)
                        if order < DEGREE - 1:
                            new = new.astype(jnp.bfloat16).astype(jnp.float32)
                            put(dst, at, s, 0, part, new)
                            values[s] = new
                        else:
                            out_ref[:, PLANE * x + 128 * part : PLANE * x + 128 * (part + 1)] = new.astype(
                                jnp.bfloat16
                            )
                    if order == 0:
                        for s in which:
                            put(dst, at, s, 1, part, turned(part, values[s]))
                        put_sides(dst, at, part, values[0], values[1], values[2])
                    elif order == 1:
                        edge = jnp.where(right_lanes, values[2], values[0])
                        old = [src[at, s, :, lanes].astype(jnp.float32) for s in (0, 2)]
                        put(dst, at, 1, 1, part, turned(part, values[1]))
                        put(dst, at, 1, 2, part, edge)
                        put(dst, at, 2, 0, part, edge)
                        put(dst, at, 2, 1, part, turned(part, edge))
                        put(dst, at, 2, 2, part, values[1])
                        edges.append((at, part, jnp.where(right_lanes, old[1], old[0])))
                    elif order == 2:
                        put(dst, at, 1, 1, part, turned(part, values[1]))
                        put(dst, at, 1, 2, part, values[2])

    edges = []
    apply(here, there, (0, 1, 2), 0)
    apply(there, here, (0, 1, 2), 1)
    for at, part, edge in edges:
        put(there, at, 2, 0, part, edge)
    apply(here, there, (1, 2), 2)
    apply(there, here, (1,), 3)


def first_kernel(centre, half, got, w_ref, out_ref, g_ref, here, there):
    diagonal(got, g_ref, centre)
    slabs = [got.at[:, NODES_DEV * s : NODES_DEV * (s + 1)] for s in range(3)]
    filter_step(slabs, w_ref, g_ref, out_ref, here, there, half)


def later_kernel(half, c_ref, l_ref, r_ref, g_ref, st_ref, w_ref, out_ref, here, there):
    out_ref[:, NODES_DEV:] = st_ref[...]
    filter_step((l_ref, c_ref, r_ref), w_ref, g_ref, out_ref, here, there, half)


def corr_kernel(factor, got, out_ref, pairs, joined):
    four = jnp.concatenate([got[:, :NODES_DEV]] * 4, axis=0)
    parts = [
        lax.dot_general(
            got[:, NODES_DEV * (1 + part) : NODES_DEV * (2 + part)],
            four,
            (((1,), (1,)), ((), ())),
            preferred_element_type=jnp.float32,
        )
        for part in range(2)
    ]
    lane, row = iota((NWF, 128), 1), iota((NWF, 128), 0)
    both = jnp.where(((lane >> 5) & 1) == 0, parts[0], parts[1])
    both = jnp.where((lane >> 6) == (row & 1), both * factor, 0.0)
    pairs[...] = both + pltpu.roll(both, NWF - 1, 0)
    for low in range(4):
        joined[4 * low : 4 * (low + 1), :] = pairs[pl.ds(2 * low, 4, stride=8), :]
    both = jnp.concatenate([joined[...]] * 4, axis=0)
    out_ref[...] = jnp.where((iota((64, 128), 1) & 3) == (iota((64, 128), 0) >> 4), both, 0.0)


def share_kernel(got, out_ref):
    total = got[0:8, :]
    for tile in range(1, 8):
        total = total + got[8 * tile : 8 * (tile + 1), :]
    total = total + pltpu.roll(total, 4, 0)
    lane, row = iota((8, 128), 1), iota((8, 128), 0)
    mine = ((lane & 31) >> 2) == row
    for x in range(4):
        out_ref[8 * x : 8 * (x + 1), :] = jnp.where(mine, total[x : x + 1, :], 0.0)


def total_kernel(got, out_ref):
    total = jnp.sum(got[...], axis=0, keepdims=True)
    lane = iota((1, 128), 1)
    rows = jnp.zeros((1, 128), jnp.float32)
    for row in range(4):
        mine = jnp.where((lane >> 5) == row // 2 + 2 * (row % 2), total, 0.0)
        rows = jnp.where(lane == row, jnp.sum(mine, axis=1, keepdims=True), rows)
    out_ref[...] = rows[:, :4]


def full(shape):
    return pl.BlockSpec(shape, lambda *_: (0,) * len(shape))


def call(kernel, args, outs, scratch=(), far=(), limit=VMEM):
    hbm = pl.BlockSpec(memory_space=pltpu.HBM)
    return pl.pallas_call(
        kernel,
        grid=(1,),
        in_specs=[full(a.shape) for a in args] + [hbm] * len(far),
        out_specs=[full(o.shape) for o in outs],
        out_shape=list(outs),
        scratch_shapes=list(scratch),
        compiler_params=pltpu.CompilerParams(vmem_limit_bytes=limit),
    )(*args, *far)


def passed_along(block, axis, distance):
    devices = range(lax.axis_size(axis))
    route = [((i - distance) % len(devices), i) for i in devices]
    return lax.ppermute(block, axis, route)


def shards(cur_block, stored_blocks, cell_potential, connectivity):
    weights, centre, half = tables()
    weights = jnp.asarray(weights)
    bf, f32 = jnp.bfloat16, jnp.float32
    shape = jax.ShapeDtypeStruct
    n_cells, n_bands = lax.axis_size("cells"), lax.axis_size("bands")
    stored = stored_blocks.reshape(2, 2, n_bands, NODES_DEV).transpose(2, 1, 0, 3).reshape(NWF, 2 * NODES_DEV)
    (message,) = call(
        message_kernel,
        (),
        [shape((NWF, MESSAGE), bf)],
        [
            pltpu.VMEM((32, 125), f32),
            pltpu.VMEM((32, 125), jnp.int32),
            pltpu.VMEM((32, 128), f32),
            pltpu.SemaphoreType.DMA((3,)),
        ],
        (cur_block, cell_potential.T, connectivity.T),
        62 * 1024 * 1024,
    )
    left = passed_along(message, "cells", 1)
    right = passed_along(message, "cells", -1)
    shapes = [shape((8, LANES_V), f32), shape((8, LANES_V), f32), shape((128, LANES_V), f32)]
    own = call(own_kernel, (message,), [shape((NWF, NODES_DEV), bf)] + shapes)
    (payload,) = call(
        pack_kernel,
        (left, right, *own),
        [shape((NWF, PAYLOAD), bf)],
        [pltpu.VMEM((32, 128), f32)],
    )
    got = lax.all_to_all(payload, "bands", 0, 0, tiled=True)
    scratch = [
        pltpu.VMEM((NXL, 3, NWF, 3 * PLANE), bf),
        pltpu.VMEM((NXL, 3, NWF, 3 * PLANE), bf),
    ]
    block, diag = call(
        functools.partial(first_kernel, centre, half),
        (got, weights),
        [shape((NWF, NODES_DEV), bf), shape((NXL, 3, NWF, PLANE), f32)],
        scratch,
    )
    left = passed_along(block, "cells", 1)
    right = passed_along(block, "cells", -1)
    factor = 1.0 / math.sqrt(NODES_DEV * n_cells * n_bands)
    (block,) = call(
        functools.partial(later_kernel, half),
        (block, left, right, diag, stored, weights),
        [shape((NWF, 3 * NODES_DEV), bf)],
        scratch,
    )
    got = lax.all_to_all(block, "bands", 0, 0, tiled=True)
    filtered = got[:, :NODES_DEV]
    (partial,) = call(
        functools.partial(corr_kernel, factor),
        (got,),
        [shape((64, 128), f32)],
        [pltpu.VMEM((NWF, 128), f32), pltpu.VMEM((16, 128), f32)],
    )
    n_y = n_cells // 4
    device = [[[[(4 * y + z) * n_bands + 4 * x + low for low in range(4)] for z in range(4)] for x in range(4)] for y in range(n_y)]
    lines = [[device[y][x][z][low] for z in range(4) for low in range(4)] for y in range(n_y) for x in range(4)]
    across = [[device[y][x][z][low] for x in range(4) for y in range(n_y)] for z in range(4) for low in range(4)]
    both = ("cells", "bands")
    partial = lax.all_to_all(partial, both, 0, 0, tiled=True, axis_index_groups=lines)
    (partial,) = call(share_kernel, (partial,), [shape((32, 128), f32)])
    partial = lax.all_to_all(partial, both, 0, 0, tiled=True, axis_index_groups=across)
    (total,) = call(total_kernel, (partial,), [shape((1, 4), f32)])
    return (filtered, total.T)


def solution(mesh):
    in_specs = (
        P(None, ("cells", "bands")),
        P("bands", "cells"),
        P(None, ("cells", "bands")),
        P(None, ("cells", "bands")),
    )
    out_specs = (P(None, ("cells", "bands")), P("bands", "cells"))
    return jax.shard_map(shards, mesh=mesh, in_specs=in_specs, out_specs=out_specs, check_vma=False)
```

```python
import functools
import math

import jax
import jax.numpy as jnp
import ml_dtypes
import numpy as np
from jax import lax
from jax.experimental import pallas as pl
from jax.experimental.pallas import tpu as pltpu
from jax.sharding import PartitionSpec as P

NWF = 32
DEGREE = 4
STEPS = 2
NXL = 8
NODES_DEV = 2048
PLANE = 256
LANES_V = 384
MESSAGE = NODES_DEV + 256
V_AT = 3 * NODES_DEV
G_AT = 5 * NODES_DEV
PAYLOAD = G_AT + 2 * 128
X_ORDER = (0, 4, 1, 3, 5, 7, 2, 6)
CLASS_ROWS = ((0, 2), (2, 6), (6, 8))
VMEM = 48 * 1024 * 1024


def kinetic_table():
    points = [-1.0, -math.sqrt(3.0 / 7.0), 0.0, math.sqrt(3.0 / 7.0), 1.0]
    weights = [0.1, 49.0 / 90.0, 32.0 / 45.0, 49.0 / 90.0, 0.1]
    scales = []
    for row in range(5):
        prod_val = 1.0
        for other in range(5):
            if other != row:
                prod_val = prod_val * (points[row] - points[other])
        scales.append(prod_val)
    deriv = [[0.0] * 5 for row in range(5)]
    for row in range(5):
        for col in range(5):
            if row != col:
                deriv[row][col] = scales[row] / scales[col] / (points[row] - points[col])
            else:
                total = 0.0
                for other in range(5):
                    if other != row:
                        total = total + 1.0 / (points[row] - points[other])
                deriv[row][col] = total
    stiff_one = [
        [sum((deriv[i][a] * weights[i] * deriv[i][b] for i in range(5))) for b in range(5)]
        for a in range(5)
    ]
    mass_one = [[weights[a] if a == b else 0.0 for b in range(5)] for a in range(5)]
    table = [[0.0] * 125 for row in range(125)]
    for k in range(125):
        ka, kb, kc = (k // 25, k // 5 % 5, k % 5)
        for j in range(125):
            ja, jb, jc = (j // 25, j // 5 % 5, j % 5)
            table[k][j] = 0.5 * (
                stiff_one[ka][ja] * mass_one[kb][jb] * mass_one[kc][jc]
                + mass_one[ka][ja] * stiff_one[kb][jb] * mass_one[kc][jc]
                + mass_one[ka][ja] * mass_one[kb][jb] * stiff_one[kc][jc]
            )
    assembled = [dict() for row in range(512)]
    for cell_x in range(2):
        for cell_y in range(2):
            for cell_z in range(2):
                global_ids = []
                for k in range(125):
                    node_x = (4 * cell_x + k // 25) % 8
                    node_y = (4 * cell_y + k // 5 % 5) % 8
                    node_z = (4 * cell_z + k % 5) % 8
                    global_ids.append((node_x * 8 + node_y) * 8 + node_z)
                for k in range(125):
                    row_map = assembled[global_ids[k]]
                    for j in range(125):
                        target = global_ids[j]
                        row_map[target] = row_map.get(target, 0.0) + table[k][j]
    largest = 0.0
    for row_map in assembled:
        total = sum((abs(value) for value in row_map.values()))
        largest = max(largest, total)
    bound = largest + 8.0 * 2.0
    return (np.array(table), float(0.55 * bound), float(0.45 * bound))


@functools.lru_cache(maxsize=None)
def tables():
    table, centre, half = kinetic_table()
    kin = table.astype(np.float32).astype(ml_dtypes.bfloat16).astype(np.float64)
    kin = kin.reshape(5, 5, 5, 5, 5, 5)
    planes = np.zeros((3, 3, PLANE, PLANE))
    lines = np.zeros((5, 5, PLANE))
    for j in range(-1, 5):
        for l in range(-1, 5):
            for b in range(5):
                for c in range(5):
                    y, z = 4 * j + b, 4 * l + c
                    if not (0 <= y < 16 and 0 <= z < 16):
                        continue
                    at = 16 * y + z
                    for a in range(5):
                        for other in range(5):
                            if other != a:
                                lines[a, other, at] += kin[a, b, c, other, b, c]
                    for b2 in range(5):
                        for c2 in range(5):
                            y2, z2 = 4 * j + b2, 4 * l + c2
                            far_y, far_z = y2 // 16, z2 // 16
                            source = 16 * (y2 % 16) + z2 % 16
                            for kind, locals_a in enumerate(((0, 4), (1,), (2,))):
                                value = sum(kin[a, b, c, a, b2, c2] for a in locals_a)
                                if value == 0.0:
                                    continue
                                assert far_y == 0 or far_z == 0
                                part = 1 if far_y else 2 if far_z else 0
                                planes[kind, part, source, at] += value
    line_rows = np.stack(
        [lines[0, 1], lines[0, 2], lines[0, 3], 2.0 * lines[0, 4], lines[1, 2], lines[1, 3]]
    )
    bf = ml_dtypes.bfloat16
    weights = np.zeros((3 * 3 * PLANE + 16, PLANE))
    weights[: 9 * PLANE] = planes.reshape(9 * PLANE, PLANE)
    weights[9 * PLANE : 9 * PLANE + 6] = line_rows
    return weights.astype(np.float32).astype(bf), centre, half


def iota(shape, dim):
    return lax.broadcasted_iota(jnp.int32, shape, dim)


def local_node(k):
    a = (k * 41) >> 10
    rest = k - 25 * a
    b = (rest * 205) >> 10
    return a, b, rest - 5 * b


def message_kernel(v_hbm, pot_hbm, conn_hbm, out_ref, raw, conn, pot, sems):
    copies = [
        pltpu.make_async_copy(pot_hbm, raw, sems.at[0]),
        pltpu.make_async_copy(conn_hbm, conn, sems.at[1]),
        pltpu.make_async_copy(v_hbm, out_ref.at[:, :NODES_DEV], sems.at[2]),
    ]
    for copy in copies:
        copy.start()
    lane = iota((32, 128), 1)
    code = (4 * (lane >> 4) * 17 + 4 * ((lane >> 2) & 3)) * 17 + 4 * (lane & 3)
    pot[...] = jnp.zeros_like(pot)
    copies[0].wait()
    copies[1].wait()
    pot[:, :125] = raw[...]
    here = jnp.where((conn[:, 0:1] == code) & (lane < 32), lane.astype(jnp.float32), 0.0)
    cell = jnp.sum(here, axis=1, keepdims=True)
    high = pot[...].astype(jnp.bfloat16).astype(jnp.float32)
    low = pot[...] - high
    out_ref[:, NODES_DEV : NODES_DEV + 128] = jnp.where(lane == 127, cell, high).astype(jnp.bfloat16)
    out_ref[:, NODES_DEV + 128 :] = low.astype(jnp.bfloat16)
    copies[2].wait()


def pick_kind(kind):
    a, b, c = local_node(iota((1, 128), 1))
    if kind < 4:
        hit = (b == 4) == (kind >= 2), (c == 4) == (kind % 2 == 1)
    else:
        hit = (b == 4) == (kind == 5), c == 4
    return jnp.where(hit[0] & hit[1] & (iota((1, 128), 1) < 125), 1.0, 0.0)


def place_of(i, kind):
    lane = iota((1, LANES_V), 1)
    y, z = lane >> 4, lane & 15
    j = (y >> 2) - (kind // 2 if kind < 4 else kind - 4)
    l = (z >> 2) - kind % 2 if kind < 4 else jnp.where(z == 0, 3, -1)
    good = (lane < PLANE + 16) & (j >= 0) & (j < 4) & (l >= 0)
    return jnp.where(good, 16 * i + 4 * j + l, -1).astype(jnp.float32)


def fitting():
    a, b, c = local_node(iota((128, LANES_V), 0))
    lane = iota((128, LANES_V), 1)
    fits = ((b & 3) == ((lane >> 4) & 3)) & ((c & 3) == (lane & 3)) & (lane < PLANE + 16)
    return jnp.where(fits, 1.0, 0.0)


def nodal(message, kind_range, mask, exact):
    rows, ones = [], ([], [])
    parts = [message[:, NODES_DEV : NODES_DEV + 128].astype(jnp.float32)]
    cell = parts[0][:, 127:128]
    if exact:
        parts.append(message[:, NODES_DEV + 128 :].astype(jnp.float32))
    for kind in kind_range:
        pick = pick_kind(kind)
        rows += [part * pick for part in parts]
        for i in range(2):
            one = jnp.where(cell == place_of(i, kind), 1.0, 0.0)
            ones[i].extend([one] * len(parts))
    stack = jnp.concatenate(rows, axis=0).astype(jnp.bfloat16)
    placed = jnp.concatenate([jnp.concatenate(one, axis=0) for one in ones], axis=1)
    both = lax.dot_general(
        stack, placed.astype(jnp.bfloat16), (((0,), (0,)), ((), ())), preferred_element_type=jnp.float32
    )
    total = jnp.zeros((8, LANES_V), jnp.float32)
    k = iota((8, 128), 1)
    along = local_node(k)[0]
    for i in range(2):
        values = both[:, LANES_V * i : LANES_V * (i + 1)] * mask
        high = values.astype(jnp.bfloat16)
        to_x = jnp.where((((4 * i + along) & 7) == iota((8, 128), 0)) & (k < 125), 1.0, 0.0)
        to_x = to_x.astype(jnp.bfloat16)
        total += jnp.dot(to_x, high, preferred_element_type=jnp.float32)
        if exact:
            low = (values - high.astype(jnp.float32)).astype(jnp.bfloat16)
            total += jnp.dot(to_x, low, preferred_element_type=jnp.float32)
    return total


def own_kernel(c_ref, v_ref, own_ref, edge_ref, mask_ref):
    v_ref[...] = c_ref[:, :NODES_DEV]
    mask = fitting()
    mask_ref[...] = mask
    own_ref[...] = nodal(c_ref, range(4), mask, True)
    edge_ref[...] = nodal(c_ref, range(4, 6), mask, True)


def pack_kernel(l_ref, r_ref, c_ref, own_ref, edge_ref, mask_ref, out_ref, ghost):
    even = iota((32, PLANE), 0) % 2 == 0
    mask = mask_ref[...]
    for s, message in enumerate((l_ref, c_ref, r_ref)):
        out_ref[:, NODES_DEV * s : NODES_DEV * (s + 1)] = message[:, :NODES_DEV]
    own = own_ref[...] + nodal(l_ref, range(4, 6), mask, True)
    left = nodal(l_ref, range(4), mask, False)
    right = nodal(r_ref, range(4), mask, False) + edge_ref[...]
    high = own.astype(jnp.bfloat16).astype(jnp.float32)
    for part, (first, second) in enumerate(((high, own - high), (left, right))):
        for x in range(NXL):
            main = jnp.where(even, first[x : x + 1, :PLANE], second[x : x + 1, :PLANE])
            at = V_AT + NODES_DEV * part + PLANE * x
            out_ref[:, at : at + PLANE] = main.astype(jnp.bfloat16)
            edge = jnp.where(even[:, :128], first[x : x + 1, PLANE:], second[x : x + 1, PLANE:])
            ghost[:, 16 * x : 16 * (x + 1)] = edge[:, :16]
        at = G_AT + 128 * part
        out_ref[:, at : at + 128] = ghost[...].astype(jnp.bfloat16)


def diagonal(got, g_ref, centre):
    lane, row = iota((128, NXL * 128), 1), iota((128, NXL * 128), 0)
    spread = jnp.where(((row >> 4) == (lane >> 7)) & ((row & 15) == (lane & 127)), 1.0, 0.0)
    spread = spread.astype(jnp.bfloat16)
    lane, row = iota((32, 64), 1), iota((32, 64), 0)
    source = jnp.where(lane < 32, row >> 1, ((row >> 1) + 15) & 15)
    same = source == ((lane & 31) >> 1)
    pairs = [
        jnp.where(same & good, 1.0, 0.0).astype(jnp.bfloat16)
        for good in ((lane & 1) == 0, lane >= 0, (lane & 1) == 1)
    ]
    edges = []
    for part in range(2):
        at = G_AT + 128 * part
        edge = jnp.dot(got[:, at : at + 128], spread, preferred_element_type=jnp.float32)
        edges.append(edge.astype(jnp.bfloat16))
    for s in range(3):
        part = 0 if s == 1 else 1
        at = V_AT + NODES_DEV * part
        base = jnp.dot(pairs[s][:, :32], got[:, at : at + NODES_DEV], preferred_element_type=jnp.float32)
        edge = jnp.dot(pairs[s][:, 32:], edges[part], preferred_element_type=jnp.float32)
        for x in range(NXL):
            at = PLANE * x
            first = base[:, at : at + 128] + edge[:, 128 * x : 128 * (x + 1)]
            g_ref[x, s, :, :128] = first - centre
            g_ref[x, s, :, 128:] = base[:, at + 128 : at + PLANE] - centre


def filter_step(slabs, w_ref, g_ref, out_ref, here, there, half):
    place = {x: at for at, x in enumerate(X_ORDER)}
    right_lanes = (iota((32, 128), 1) & 15) < 8
    lines = w_ref[9 * PLANE :, :].astype(jnp.float32)
    halves = [slice(128 * part, 128 * (part + 1)) for part in range(2)]

    def turned(part, value):
        return pltpu.roll(value, 30 if part == 0 else 2, 0)

    def put(ref, at, s, section, part, value):
        ref[at, s, :, PLANE * section + 128 * part : PLANE * section + 128 * (part + 1)] = value.astype(
            jnp.bfloat16
        )

    def put_sides(ref, at, part, left, middle, right):
        zero = jnp.zeros_like(left)
        put(ref, at, 0, 2, part, jnp.where(right_lanes, middle, zero))
        put(ref, at, 1, 2, part, jnp.where(right_lanes, right, left))
        put(ref, at, 2, 2, part, jnp.where(right_lanes, zero, middle))

    for x in range(NXL):
        for part in range(2):
            values = []
            for s, slab in enumerate(slabs):
                value = slab[:, PLANE * x + 128 * part : PLANE * x + 128 * (part + 1)].astype(jnp.float32)
                values.append(value)
                put(here, place[x], s, 0, part, value)
                put(here, place[x], s, 1, part, turned(part, value))
            put_sides(here, place[x], part, *values)

    def apply(src, dst, which, order):
        alpha = (1.0 if order == 0 else 2.0) / half
        first, last = which[0], which[-1] + 1
        for kind in (1, 0, 2):
            low, high = CLASS_ROWS[kind]
            count = (high - low) * (last - first) * 32
            result = jnp.dot(
                src[low:high, first:last].reshape(count, 3 * PLANE),
                w_ref[3 * PLANE * kind : 3 * PLANE * (kind + 1), :],
                preferred_element_type=jnp.float32,
            ).reshape(high - low, last - first, 32, PLANE)
            for at in range(low, high):
                x = X_ORDER[at]
                for part in range(2):
                    lanes = halves[part]
                    c01, c02, c03, c04, c12, c13 = (lines[row : row + 1, lanes] for row in range(6))
                    values = {}
                    for s in which:
                        v = lambda other: src[place[other % 8], s, :, lanes].astype(jnp.float32)
                        if x in (0, 4):
                            extra = c01 * (v(x + 1) + v(x + 7)) + c02 * (v(x + 2) + v(x + 6))
                            extra = extra + c03 * (v(x + 3) + v(x + 5)) + c04 * v(x + 4)
                        elif x in (2, 6):
                            extra = c02 * (v(x - 2) + v(x + 2)) + c12 * (v(x - 1) + v(x + 1))
                        else:
                            step = 1 if x in (1, 5) else -1
                            extra = c01 * v(x - step) + c12 * v(x + step)
                            extra = extra + c13 * v(x + 2 * step) + c03 * v(x + 3 * step)
                        diag = g_ref[x, s, :, lanes]
                        if which == (1, 2) and s == 2:
                            diag = jnp.where(right_lanes, diag, g_ref[x, 0, :, lanes])
                        new = alpha * (result[at - low, s - first, :, lanes] + extra + diag * v(x))
                        if order:
                            new = new - dst[at, s, :, lanes].astype(jnp.float32)
                        if order < DEGREE - 1:
                            new = new.astype(jnp.bfloat16).astype(jnp.float32)
                            put(dst, at, s, 0, part, new)
                            values[s] = new
                        else:
                            out_ref[:, PLANE * x + 128 * part : PLANE * x + 128 * (part + 1)] = new.astype(
                                jnp.bfloat16
                            )
                    if order == 0:
                        for s in which:
                            put(dst, at, s, 1, part, turned(part, values[s]))
                        put_sides(dst, at, part, values[0], values[1], values[2])
                    elif order == 1:
                        edge = jnp.where(right_lanes, values[2], values[0])
                        old = [src[at, s, :, lanes].astype(jnp.float32) for s in (0, 2)]
                        put(dst, at, 1, 1, part, turned(part, values[1]))
                        put(dst, at, 1, 2, part, edge)
                        put(dst, at, 2, 0, part, edge)
                        put(dst, at, 2, 1, part, turned(part, edge))
                        put(dst, at, 2, 2, part, values[1])
                        edges.append((at, part, jnp.where(right_lanes, old[1], old[0])))
                    elif order == 2:
                        put(dst, at, 1, 1, part, turned(part, values[1]))
                        put(dst, at, 1, 2, part, values[2])

    edges = []
    apply(here, there, (0, 1, 2), 0)
    apply(there, here, (0, 1, 2), 1)
    for at, part, edge in edges:
        put(there, at, 2, 0, part, edge)
    apply(here, there, (1, 2), 2)
    apply(there, here, (1,), 3)


def first_kernel(centre, half, got, w_ref, out_ref, g_ref, here, there):
    diagonal(got, g_ref, centre)
    slabs = [got.at[:, NODES_DEV * s : NODES_DEV * (s + 1)] for s in range(3)]
    filter_step(slabs, w_ref, g_ref, out_ref, here, there, half)


def later_kernel(half, c_ref, l_ref, r_ref, g_ref, st_ref, w_ref, out_ref, here, there):
    out_ref[:, NODES_DEV:] = st_ref[...]
    filter_step((l_ref, c_ref, r_ref), w_ref, g_ref, out_ref, here, there, half)


def corr_kernel(factor, got, out_ref, filtered_ref, pairs):
    filtered_ref[...] = got[:, :NODES_DEV]
    four = jnp.concatenate([got[:, :NODES_DEV]] * 4, axis=0)
    parts = [
        lax.dot_general(
            got[:, NODES_DEV * (1 + part) : NODES_DEV * (2 + part)],
            four,
            (((1,), (1,)), ((), ())),
            preferred_element_type=jnp.float32,
        )
        for part in range(2)
    ]
    lane, row = iota((NWF, 128), 1), iota((NWF, 128), 0)
    both = jnp.where(((lane >> 5) & 1) == 0, parts[0], parts[1])
    both = jnp.where((lane >> 6) == (row & 1), both * factor, 0.0)
    pairs[...] = both + pltpu.roll(both, NWF - 1, 0)
    even = pairs[pl.ds(0, 16, stride=2), :]
    both = jnp.concatenate([even] * 4, axis=0)
    out_ref[...] = jnp.where((iota((64, 128), 1) & 3) == (iota((64, 128), 0) >> 4), both, 0.0)


def share_kernel(got, out_ref):
    total = jnp.sum(got[...], axis=0, keepdims=True)
    lane, row = iota((8, 128), 1), iota((8, 128), 0)
    out_ref[...] = jnp.where(((lane & 31) >> 2) == row, total, 0.0)


def total_kernel(got, out_ref):
    total = jnp.sum(got[...], axis=0, keepdims=True)
    lane = iota((1, 128), 1)
    rows = jnp.zeros((1, 128), jnp.float32)
    for row in range(4):
        mine = jnp.where((lane >> 5) == row // 2 + 2 * (row % 2), total, 0.0)
        rows = jnp.where(lane == row, jnp.sum(mine, axis=1, keepdims=True), rows)
    out_ref[...] = rows[:, :4]


def full(shape):
    return pl.BlockSpec(shape, lambda *_: (0,) * len(shape))


def call(kernel, args, outs, scratch=(), far=(), limit=VMEM):
    hbm = pl.BlockSpec(memory_space=pltpu.HBM)
    return pl.pallas_call(
        kernel,
        grid=(1,),
        in_specs=[full(a.shape) for a in args] + [hbm] * len(far),
        out_specs=[full(o.shape) for o in outs],
        out_shape=list(outs),
        scratch_shapes=list(scratch),
        compiler_params=pltpu.CompilerParams(vmem_limit_bytes=limit),
    )(*args, *far)


def passed_along(block, axis, distance):
    devices = range(lax.axis_size(axis))
    route = [((i - distance) % len(devices), i) for i in devices]
    return lax.ppermute(block, axis, route)


def shards(cur_block, stored_blocks, cell_potential, connectivity):
    weights, centre, half = tables()
    weights = jnp.asarray(weights)
    bf, f32 = jnp.bfloat16, jnp.float32
    shape = jax.ShapeDtypeStruct
    n_cells, n_bands = lax.axis_size("cells"), lax.axis_size("bands")
    stored = stored_blocks.reshape(2, 2, n_bands, NODES_DEV).transpose(2, 1, 0, 3).reshape(NWF, 2 * NODES_DEV)
    (message,) = call(
        message_kernel,
        (),
        [shape((NWF, MESSAGE), bf)],
        [
            pltpu.VMEM((32, 125), f32),
            pltpu.VMEM((32, 125), jnp.int32),
            pltpu.VMEM((32, 128), f32),
            pltpu.SemaphoreType.DMA((3,)),
        ],
        (cur_block, cell_potential.T, connectivity.T),
        62 * 1024 * 1024,
    )
    left = passed_along(message, "cells", 1)
    right = passed_along(message, "cells", -1)
    shapes = [shape((8, LANES_V), f32), shape((8, LANES_V), f32), shape((128, LANES_V), f32)]
    own = call(own_kernel, (message,), [shape((NWF, NODES_DEV), bf)] + shapes)
    (payload,) = call(
        pack_kernel,
        (left, right, *own),
        [shape((NWF, PAYLOAD), bf)],
        [pltpu.VMEM((32, 128), f32)],
    )
    got = lax.all_to_all(payload, "bands", 0, 0, tiled=True)
    scratch = [
        pltpu.VMEM((NXL, 3, NWF, 3 * PLANE), bf),
        pltpu.VMEM((NXL, 3, NWF, 3 * PLANE), bf),
    ]
    block, diag = call(
        functools.partial(first_kernel, centre, half),
        (got, weights),
        [shape((NWF, NODES_DEV), bf), shape((NXL, 3, NWF, PLANE), f32)],
        scratch,
    )
    left = passed_along(block, "cells", 1)
    right = passed_along(block, "cells", -1)
    factor = 1.0 / math.sqrt(NODES_DEV * n_cells * n_bands)
    (block,) = call(
        functools.partial(later_kernel, half),
        (block, left, right, diag, stored, weights),
        [shape((NWF, 3 * NODES_DEV), bf)],
        scratch,
    )
    got = lax.all_to_all(block, "bands", 0, 0, tiled=True)
    partial, filtered = call(
        functools.partial(corr_kernel, factor),
        (got,),
        [shape((64, 128), f32), shape((NWF, NODES_DEV), bf)],
        [pltpu.VMEM((NWF, 128), f32)],
    )
    planes = [list(range(at, at + 64)) for at in range(0, n_cells * n_bands, 64)]
    columns = [list(range(at, n_cells, 4)) for at in range(4)]
    partial = lax.all_to_all(partial, ("cells", "bands"), 0, 0, tiled=True, axis_index_groups=planes)
    (partial,) = call(share_kernel, (partial,), [shape((8, 128), f32)])
    partial = lax.all_to_all(partial, "cells", 0, 0, tiled=True, axis_index_groups=columns)
    (total,) = call(total_kernel, (partial,), [shape((1, 4), f32)])
    return (filtered, total.T)


def solution(mesh):
    in_specs = (
        P(None, ("cells", "bands")),
        P("bands", "cells"),
        P(None, ("cells", "bands")),
        P(None, ("cells", "bands")),
    )
    out_specs = (P(None, ("cells", "bands")), P("bands", "cells"))
    return jax.shard_map(shards, mesh=mesh, in_specs=in_specs, out_specs=out_specs, check_vma=False)
```
